256 devices in a mesh: ctx: 16 (over z, core), grp: 4 (over y), dp: 4 (over x).
Axes of the slice: x: 4, y: 4, z: 8, core: 2. Of those that a mesh axis runs over, the one named last changes fastest.
Arguments:
- hidden_in: bfloat16 [4, 2048, 8192], P('dp', 'ctx'), may hold values from -6 to 6
- teacher_queries: bfloat16 [4, 2048, 8192], P('dp', 'ctx', 'grp'), may hold values from -5 to 5
- teacher_keys: bfloat16 [4, 2048, 1024], P('dp', 'ctx', 'grp'), may hold values from -5 to 5
- teacher_values: bfloat16 [4, 2048, 1024], P('dp', 'ctx', 'grp'), may hold values from -5 to 5
- doc_lengths: int32 [4, 4], P('dp'), may hold values from 1 to 1024, 2048 in all within a row
- dt_weight: bfloat16 [8192, 64], P(None, 'grp'), may hold values from -0.0625 to 0.0625
- dt_bias: float32 [64], P('grp'), may hold values from -2 to 1
- decay_log: float32 [64], P('grp')
- skip_gain: float32 [64], P('grp'), may hold values from 0.5 to 2
- norm_gain: float32 [8192], P('grp'), may hold values from 0.1 to 1.9
Outputs:
- student_out: bfloat16 [4, 2048, 8192], P('dp', 'ctx', 'grp')
- grad_dt_weight: float32 [8192, 64], P(None, 'grp')
- grad_dt_bias: float32 [64], P('grp')
- grad_decay_log: float32 [64], P('grp')
- grad_skip_gain: float32 [64], P('grp')
- grad_norm_gain: float32 [8192], P('grp')
The draws below stay inside these ranges and needn't reach their ends.
Inputs may be any that keep to these rules, and one draw needn't show every extreme that they name: `doc_lengths`: each row sums to 2048; its longest document has exactly 1024 positions.
All inputs are finite; a program needn't handle non-finite values.
Results may differ from the reference program's by a relative error of at most 0.0028.
Values may be sent and summed in bfloat16 or wider, within the bound.
No kernel may reach another device: no remote copies, remote signals or barrier semaphores. Data moves between devices by JAX's collectives and lax.ppermute only.
A program may use at most 128 MiB of HBM per device.

```python
import math
import jax
import jax.numpy as jnp
import numpy as np
from jax import lax

D = 8192
HEADS = 64
KV_HEADS = 8
HDIM = 128
SEQ_DEV = 128
NDOC = 4
LEN = 2048
SEQS = 4
N_CTX = 16


def draw_teacher_queries(key, part):
    key = jax.random.fold_in(key, 11)
    values = jax.random.truncated_normal(key, -4.0, 4.0, (SEQS, LEN, HEADS * HDIM), jnp.float32)
    return values.astype(jnp.bfloat16)


def draw_teacher_keys(key, part):
    key = jax.random.fold_in(key, 12)
    values = jax.random.truncated_normal(key, -4.0, 4.0, (SEQS, LEN, KV_HEADS * HDIM), jnp.float32)
    return values.astype(jnp.bfloat16)


def mixed_rates(key, slow_share):
    pick_key, slow_key, fast_key = jax.random.split(key, 3)
    slow = jax.random.uniform(pick_key, (HEADS,), jnp.float32) < slow_share
    slow_log = math.log(0.05 / LEN) + jax.random.uniform(slow_key, (HEADS,), jnp.float32) * math.log(10.0)
    fast_log = math.log(0.02) + jax.random.uniform(fast_key, (HEADS,), jnp.float32) * math.log(5.0)
    return jnp.where(slow, slow_log, fast_log)


def draw_decay_log(key, part):
    key = jax.random.fold_in(key, 21)
    values = mixed_rates(key, 0.5)
    return values.astype(jnp.float32)


def block_scale(stream_key, dims, cuts, low, high):
    factor_of = 1.0
    for position, blocks in cuts:
        draws = jax.random.uniform(jax.random.fold_in(jax.random.fold_in(stream_key, 6), position), (blocks,), jnp.float32, low / len(cuts), high / len(cuts))
        factor_of = factor_of * jnp.repeat(jnp.exp(draws), dims[position] // blocks).reshape((-1,) + (1,) * (len(dims) - 1 - position))
    return factor_of


def length_profile(number_of, total, reach, slope):
    loads = [(1 << 20) // math.isqrt(grade ** slope) + 1 for grade in range(2, number_of + 1)]
    surplus, counts = total - reach - (number_of - 1), [1] * (number_of - 1)
    while surplus > 0:
        candidates = [i for i in range(number_of - 1) if counts[i] < reach]
        mass, budget = sum([loads[i] for i in candidates]), surplus
        for i in candidates:
            addition = min(reach - counts[i], max(1, budget * loads[i] // mass), surplus)
            counts[i] = counts[i] + addition
            surplus = surplus - addition
    return np.array([reach] + counts)


def uneven_parts(rng, amount, total, bound, slope):
    if amount == 2:
        one = jax.random.randint(rng, (), max(1, total - bound), min(bound, total - 1) + 1)
        return jnp.stack([one, total - one])
    sizes = jnp.asarray(length_profile(amount, total, bound, slope), jnp.int32)
    twos = (amount - 1) // 2
    giver, sink = sizes[1:1 + 2 * twos:2], sizes[2:2 + 2 * twos:2]
    margin = jnp.minimum(giver - 1, bound - sink)
    passed = jax.random.randint(jax.random.fold_in(rng, 1), (twos,), 0, 1 << 20) % (margin + 1)
    sizes = sizes.at[1:1 + 2 * twos:2].set(giver - passed).at[2:2 + 2 * twos:2].set(sink + passed)
    return sizes[jax.random.permutation(jax.random.fold_in(rng, 2), amount)]


def scatter_about(rng, dims, scale, reach, cuts=(), held_as=jnp.bfloat16):
    drawn = scale * jax.random.normal(rng, dims, jnp.float32)
    if cuts:
        drawn = drawn * block_scale(rng, dims, cuts, -0.22, 0.18)
    return jnp.clip(drawn, -reach, reach).astype(held_as)


def setup_inputs(seed: int = 0) -> dict:
    seeds = jax.random.split(jax.random.key(seed), 11)
    hidden_in = scatter_about(seeds[0], (SEQS, LEN, D), 1.0, 6.0, ((0, 4), (1, 16)))
    teacher_queries = draw_teacher_queries(jax.random.fold_in(seeds[10], 71), 0)
    teacher_keys = draw_teacher_keys(jax.random.fold_in(seeds[10], 71), 0)
    teacher_values = scatter_about(seeds[3], (SEQS, LEN, KV_HEADS * HDIM), 1.0, 5.0, ((0, 4), (1, 16), (2, 4)))
    doc_lengths = jax.vmap(lambda own: uneven_parts(own, NDOC, LEN, LEN // 2, 2))(jax.random.split(seeds[4], SEQS)).reshape((SEQS, NDOC)).astype(jnp.int32)
    dt_weight = scatter_about(seeds[5], (D, HEADS), D ** -0.5, 0.0625, ((1, 4),))
    dt_bias = jnp.clip(-2.0 + 3.0 * jax.random.uniform(seeds[6], (HEADS,), jnp.float32) ** block_scale(seeds[6], (HEADS,), ((0, 4),), -0.2, 0.2), -2.0, 1.0)
    decay_log = draw_decay_log(jax.random.fold_in(seeds[10], 71), 0)
    skip_gain = jnp.clip(0.5 + 1.5 * jax.random.uniform(seeds[8], (HEADS,), jnp.float32) ** block_scale(seeds[8], (HEADS,), ((0, 4),), -0.2, 0.2), 0.5, 2.0)
    norm_gain = jnp.clip(1.0 + 0.18 * jax.random.normal(seeds[9], (HEADS * HDIM,), jnp.float32), 0.1, 1.9)
    return {"hidden_in": hidden_in, "teacher_queries": teacher_queries, "teacher_keys": teacher_keys, "teacher_values": teacher_values, "doc_lengths": doc_lengths, "dt_weight": dt_weight, "dt_bias": dt_bias, "decay_log": decay_log, "skip_gain": skip_gain, "norm_gain": norm_gain}


EPSILON = 1e-05

def segment_of(positions, lengths_row):
    starts = jnp.cumsum(lengths_row) - lengths_row
    return lax.optimization_barrier(jnp.sum((positions[:, None] >= starts[None, 1:]).astype(jnp.int32), axis=1)).astype(jnp.int32)

def block_output(query_block, key_block, value_block, step_size, decay_rate, skip_gain, segment_block, before, state_in):
    row_count = step_size.shape[0]
    head_count = step_size.shape[1]
    kv_count = key_block.shape[1] // HDIM
    group_size = head_count // kv_count
    query_low = query_block.reshape(row_count, kv_count, group_size, HDIM)
    key_low = key_block.reshape(row_count, kv_count, HDIM)
    value_low = value_block.reshape(row_count, kv_count, HDIM)
    cumulative = jnp.cumsum(-(decay_rate[None, :] * step_size), axis=0)
    cum_split = cumulative.T.reshape(kv_count, group_size, row_count)
    row_order = jnp.arange(row_count, dtype=jnp.int32)
    allowed = (segment_block[:, None] == segment_block[None, :]) & (row_order[None, :] <= row_order[:, None])
    log_gaps = jnp.where(allowed, cum_split[:, :, :, None] - cum_split[:, :, None, :], 0.0)
    mixing = jnp.where(allowed, jnp.exp(log_gaps), 0.0) * step_size.T.reshape(kv_count, group_size, 1, row_count)
    intersection = jnp.einsum('tgrp,ugp->grtu', query_low, key_low, preferred_element_type=jnp.float32)
    within = jnp.einsum('grtu,ugp->tgrp', intersection * mixing, value_low.astype(jnp.float32), precision=lax.Precision.HIGH)
    carried = jnp.where(segment_block == before, 1.0, 0.0).astype(step_size.dtype)
    entering = jnp.exp(cumulative).reshape(row_count, kv_count, group_size) * carried[:, None, None]
    state_split = state_in.reshape(kv_count, group_size, HDIM, HDIM)
    entering_term = jnp.einsum('tgrn,grnp->tgrp', query_low.astype(jnp.float32), state_split, precision=lax.Precision.HIGH) * entering[..., None]
    direct = skip_gain.reshape(kv_count, group_size)[None, :, :, None] * value_low.astype(jnp.float32)[:, :, None, :]
    return (within + entering_term + direct).reshape(row_count, head_count * HDIM)

def block_state(key_block, value_block, step_size, decay_rate, segment_block, before):
    row_count = step_size.shape[0]
    head_count = step_size.shape[1]
    kv_count = key_block.shape[1] // HDIM
    group_size = head_count // kv_count
    key_low = key_block.reshape(row_count, kv_count, HDIM)
    value_low = value_block.reshape(row_count, kv_count, HDIM)
    cumulative = jnp.cumsum(-(decay_rate[None, :] * step_size), axis=0)
    final_log = cumulative[row_count - 1]
    same_final = segment_block == segment_block[row_count - 1]
    tail_weight = jnp.where(same_final[:, None], jnp.exp(jnp.where(same_final[:, None], final_log[None, :] - cumulative, 0.0)), 0.0) * step_size
    tail_split = tail_weight.T.reshape(kv_count, group_size, row_count)
    weighted = tail_split[:, :, :, None] * jnp.transpose(key_low, (1, 0, 2))[:, None, :, :]
    local_state = jnp.einsum('grun,ugp->grnp', weighted, value_low.astype(jnp.float32), precision=lax.Precision.HIGH)
    carried = jnp.where(segment_block[row_count - 1] == before, 1.0, 0.0).astype(step_size.dtype)
    decay_all = jnp.exp(final_log) * carried
    return (decay_all, local_state.reshape(head_count, HDIM, HDIM))

def teacher_sequence(query_seq, key_seq, value_seq, segment):
    group_size = HEADS // KV_HEADS
    block_rows = math.gcd(512, LEN)
    positions = jnp.arange(LEN, dtype=jnp.int32)
    key_all = key_seq.reshape(LEN, KV_HEADS, HDIM).astype(jnp.float32)
    value_all = value_seq.reshape(LEN, KV_HEADS, HDIM).astype(jnp.float32)
    query_all = query_seq.reshape(LEN, KV_HEADS, group_size, HDIM)

    def one_block(block_index):
        start_row = block_index * block_rows
        query_rows = lax.dynamic_slice_in_dim(query_all, start_row, block_rows, 0).astype(jnp.float32)
        row_positions = start_row + jnp.arange(block_rows, dtype=jnp.int32)
        row_segments = lax.dynamic_slice_in_dim(segment, start_row, block_rows, 0)
        allowed = (positions[None, :] <= row_positions[:, None]) & (segment[None, :] == row_segments[:, None])

        def one_head(head_index):
            scores = jnp.einsum('trp,up->rtu', query_rows[:, head_index], key_all[:, head_index]) * (1.0 / math.sqrt(HDIM))
            masked = jnp.where(allowed[None], scores, -jnp.inf)
            maxima = lax.optimization_barrier(jnp.max(masked, axis=-1, keepdims=True))
            weights = jnp.where(allowed[None], jnp.exp(scores - maxima), 0.0)
            totals = lax.optimization_barrier(jnp.sum(weights, axis=-1))
            rounded = lax.optimization_barrier(weights.astype(jnp.bfloat16)).astype(jnp.float32)
            mixed = jnp.einsum('rtu,up->trp', rounded, value_all[:, head_index])
            return mixed / totals.T[:, :, None]
        head_outs = lax.map(one_head, jnp.arange(KV_HEADS, dtype=jnp.int32))
        return jnp.transpose(head_outs, (1, 0, 2, 3)).astype(jnp.bfloat16)
    blocks = lax.map(one_block, jnp.arange(LEN // block_rows, dtype=jnp.int32))
    return blocks.reshape(LEN, HEADS * HDIM)

def student_sequence(query_seq, key_seq, value_seq, step_seq, segment, decay_rate, skip_gain):

    def block_step(carried_state, block_index):
        first_row = block_index * SEQ_DEV

        def block_slice(array):
            return lax.dynamic_slice_in_dim(array, first_row, SEQ_DEV, 0)
        segment_block = block_slice(segment)
        before = jnp.where(block_index > 0, segment[jnp.maximum(first_row - 1, 0)], -1).astype(jnp.int32)
        output = block_output(block_slice(query_seq), block_slice(key_seq), block_slice(value_seq), block_slice(step_seq), decay_rate, skip_gain, segment_block, before, carried_state)
        decay_all, local_state = block_state(block_slice(key_seq), block_slice(value_seq), block_slice(step_seq), decay_rate, segment_block, before)
        return (decay_all[:, None, None] * carried_state + local_state, output)
    initial = jnp.zeros((HEADS, HDIM, HDIM), jnp.float32)
    _, outputs = lax.scan(jax.checkpoint(block_step), initial, jnp.arange(N_CTX, dtype=jnp.int32))
    return outputs.reshape(LEN, HEADS * HDIM)

def reference(hidden_in, teacher_queries, teacher_keys, teacher_values, doc_lengths, dt_weight, dt_bias, decay_log, skip_gain, norm_gain):
    positions = jnp.arange(LEN, dtype=jnp.int32)
    segments = jax.vmap(lambda lengths_row: segment_of(positions, lengths_row))(doc_lengths)
    teacher_out = lax.map(lambda packed: teacher_sequence(*packed), (teacher_queries, teacher_keys, teacher_values, segments))
    hidden_flat = hidden_in.reshape(SEQS * LEN, D)
    pre = jnp.dot(hidden_flat, dt_weight, preferred_element_type=jnp.float32) + dt_bias
    step_size = jax.nn.softplus(pre).reshape(SEQS, LEN, HEADS)
    decay_rate = jnp.exp(decay_log)

    def distill(step_all, rate_all, skip_all, gain_all):
        raw = lax.map(lambda packed: student_sequence(*packed, rate_all, skip_all), (teacher_queries, teacher_keys, teacher_values, step_all, segments))
        inverse = lax.rsqrt(lax.optimization_barrier(jnp.mean(raw * raw, axis=-1, keepdims=True)) + EPSILON)
        normed = raw * inverse * gain_all
        difference = normed - teacher_out.astype(jnp.float32)
        return (jnp.sum(difference * difference) / (SEQS * LEN), normed)
    distill_loss, pullback, normed = jax.vjp(distill, step_size, decay_rate, skip_gain, norm_gain, has_aux=True)
    grad_step, grad_rate, grad_skip, grad_gain = pullback(jnp.ones_like(distill_loss))
    grad_pre = grad_step.reshape(SEQS * LEN, HEADS) * jax.nn.sigmoid(pre)
    grad_weight = jnp.dot(hidden_flat.T, grad_pre.astype(jnp.bfloat16), preferred_element_type=jnp.float32)
    grad_bias = lax.optimization_barrier(jnp.sum(grad_pre, axis=0))
    return (normed.astype(jnp.bfloat16), grad_weight, grad_bias, grad_rate * decay_rate, grad_skip, grad_gain)
```

```python
import functools
import math

import jax
import jax.numpy as jnp
from jax import lax
from jax.experimental import pallas as pl
from jax.experimental.pallas import tpu as pltpu
from jax.sharding import PartitionSpec as P

HDIM = 128
EPSILON = 1e-05
BACK = 8
NEG = -1e30
LOG2E = math.log2(math.e)
F32 = jnp.float32
BF16 = jnp.bfloat16


def mm(a, b):
    return jnp.dot(a, b, preferred_element_type=F32)


def two_parts(x):
    high = x.astype(BF16)
    return high, (x - high.astype(F32)).astype(BF16)


def mm_two(a, b):
    high, low = two_parts(a)
    return mm(high, b) + mm(low, b)


def mm_right(a, b):
    high, low = two_parts(b)
    return mm(a, high) + mm(a, low)


def iota(shape, dim):
    return lax.broadcasted_iota(jnp.int32, shape, dim)


def to_row(x):
    rows = x.shape[0]
    if rows < 128:
        x = jnp.concatenate([x, jnp.zeros((128 - rows, x.shape[1]), F32)], axis=0)
    return jnp.sum(x.T, axis=0, keepdims=True)


def column_of(values, rows):
    row = iota((rows, 128), 0)
    out = jnp.zeros((rows, 128), F32)
    for h in range(rows):
        out = jnp.where(row == h, values[h], out)
    return out


def place_of(consts, rows):
    core = lax.axis_index("core")
    place = lax.axis_index("z") * lax.axis_size("core") + core
    starts = [consts[i : i + 1, :].astype(jnp.int32) for i in range(3)]
    return (place * rows, *starts, core, place)


def segment_at(pos, info):
    return (
        (pos >= info[1]).astype(jnp.int32)
        + (pos >= info[2]).astype(jnp.int32)
        + (pos >= info[3]).astype(jnp.int32)
    )


def prep_kernel(
    kv, lengths, bias, decay, skip, gain, hidden, weight, keys, values, payload, slope, consts
):
    pre = (
        lax.dot_general(
            weight[...], hidden[...], (((1,), (1,)), ((), ())), preferred_element_type=F32
        )
        + column_of(bias, weight.shape[0])
    )
    step = jnp.maximum(pre, 0.0) + jnp.log1p(jnp.exp(-jnp.abs(pre)))
    slope[...] = 1.0 / (1.0 + jnp.exp(-pre))
    for g in range(kv):
        cols = slice(g * HDIM, (g + 1) * HDIM)
        payload[g * HDIM : (g + 1) * HDIM, :] = keys[:, cols].astype(F32).T.astype(BF16)
        payload[(kv + g) * HDIM : (kv + g + 1) * HDIM, :] = values[:, cols]
    heads = step.shape[0]
    consts[0:heads, :] = jnp.exp(column_of(decay, heads))
    consts[heads : 2 * heads, :] = column_of(skip, heads)
    for h in range(heads):
        consts[2 * heads + h : 2 * heads + h + 1, :] = gain[:, h * HDIM : (h + 1) * HDIM]
    one = lengths[0, 0]
    two = one + lengths[0, 1]
    starts = (one, two, two + lengths[0, 2], 0, 0, 0, 0, 0)
    row = iota((8, 128), 0)
    marks = jnp.zeros((8, 128), jnp.int32)
    for i in range(3):
        marks = jnp.where(row == i, starts[i], marks)
    consts[3 * heads :, :] = marks.astype(F32)
    first = 2 * kv * HDIM
    for part in range(3):
        piece = step.astype(BF16)
        payload[first + part * heads : first + (part + 1) * heads, :] = piece
        step = step - piece.astype(F32)


def masks(info):
    first = info[0]
    before = jnp.where(
        first > 0, segment_at(jnp.maximum(first - 1, 0) + iota((1, 128), 1) * 0, info), -1
    )
    row_pos = first + iota((128, 128), 0)
    col_pos = first + iota((128, 128), 1)
    row_seg = segment_at(row_pos, info)
    allowed = (row_seg == segment_at(col_pos, info)) & (col_pos <= row_pos)
    carried = row_seg == before
    return first, before, allowed, carried


def match_row(info, first, before, d, rows):
    pos = first - 128 * d + iota((rows, 128), 1)
    return (segment_at(pos, info) == before) & (pos >= 0)


PARTS = ((0, 1, 2), (3, 4), (5, 6, 7, 8))


def layout(*sizes):
    starts, total = [], 0
    for size in sizes:
        starts.append(total)
        total += -(-size // 128) * 128
    return starts, total


def carry_rows(heads, kv, blocks, first):
    past = len(blocks) - (1 if first else 0)
    small = heads * (2 + len(blocks) + past)
    turned = 0 if first else kv * len(blocks) * 128
    wide = heads * 128
    return layout(wide, wide, wide, wide, small, 3 * heads + 8 if first else 0, turned, turned)


def keep_rows(heads, kv, blocks):
    turned = kv * len(blocks) * 128
    return layout(heads * 128, heads * 128, kv * 128, turned, turned)


def real_rows(heads, kv):
    count = BACK + 1
    wide = heads * 128
    return layout(wide, wide, wide, 3 * heads + 8, count * heads, BACK * heads, kv * count * 128)


def half_rows(heads, kv):
    return layout(heads * 128, kv * (BACK + 1) * 128)


def slab(start, h):
    return pl.ds(pl.multiple_of(start + h * 128, 128), 128)


def forward_kernel(kv, heads, blocks, first, last, *refs):
    refs = list(refs)

    def take(count):
        out = refs[:count]
        del refs[:count]
        return out

    queries = take(1)[0]
    sources = [take(1 if d % 2 == 0 else 2) for d in blocks]
    if first:
        consts, carry, keep, kt, vv, bias, key32 = refs
    elif not last:
        origin, carry, kt, vv, bias, key32 = refs
        before_carry, before_at = origin, carry_rows(heads, kv, PARTS[0], True)[0]
    else:
        origin, before_carry, keep, real, half, stats, kt, vv, bias, key32, acc = refs
        before_at = carry_rows(heads, kv, PARTS[1], False)[0]
        acc[...] = jnp.zeros_like(acc)
    origin_at = carry_rows(heads, kv, PARTS[0], True)[0]
    keep_at = keep_rows(heads, kv, PARTS[0])[0]
    real_at = real_rows(heads, kv)[0]
    half_at = half_rows(heads, kv)[0]
    carry_at = carry_rows(heads, kv, blocks, first)[0]
    if first:
        constant, base = consts, 0
        carry[carry_at[5] : carry_at[5] + consts.shape[0], :] = consts[...]
        cum_ref = carry
    else:
        constant, base = origin, origin_at[5]
        cum_ref = origin
    cum_at = origin_at[4] + heads
    group = heads // kv
    size = 3 * heads + 8
    info = place_of(constant[base + size - 8 : base + size, :], queries.shape[0])
    even_core = info[4] == 0
    start, before, allowed, carried = masks(info)

    reach = (iota((128, 128), 0) <= iota((128, 128), 1)).astype(BF16)
    if first:
        after = jnp.zeros((heads, 128), F32)
    else:
        after = before_carry[before_at[4] : before_at[4] + heads, :]
    rate = constant[base : base + heads, :]
    own = 1 if first else 0
    past = len(blocks) - own
    steps, fades = [], []
    for i, d in enumerate(blocks):
        at = slice(128 * i, 128 * i + 128)
        near = sources[i]

        def piece(low, high):
            if d % 2 == 0:
                return near[0][low:high, :]
            return jnp.where(even_core, near[0][low:high, :], near[1][low:high, :])

        for g in range(kv):
            block = piece(g * HDIM, (g + 1) * HDIM)
            value = piece((kv + g) * HDIM, (kv + g + 1) * HDIM)
            kt[g, :, at] = block
            vv[g, at, :] = value
            block, value = block.astype(F32), value.astype(F32)
            if last:
                row = (g * (BACK + 1) + d) * 128
                half[half_at[1] + row : half_at[1] + row + 128, :] = kt[g, :, at]
                real[real_at[6] + row : real_at[6] + row + 128, :] = value.T
            else:
                row = (g * len(blocks) + i) * 128
                out, where = (keep, keep_at[3:5]) if first else (carry, carry_at[6:8])
                out[where[0] + row : where[0] + row + 128, :] = block
                out[where[1] + row : where[1] + row + 128, :] = value.T
            if d == 0:
                keep[keep_at[2] + 128 * g : keep_at[2] + 128 * g + 128, :] = value
            else:
                key32[g, :, 128 * (i - own) : 128 * (i - own) + 128] = block
        first_step = 2 * kv * HDIM
        parts = [piece(first_step + k * heads, first_step + (k + 1) * heads) for k in range(3)]
        step = parts[0].astype(F32) + parts[1].astype(F32) + parts[2].astype(F32)
        sums = mm(parts[0], reach) + mm(parts[1], reach) + mm(parts[2], reach)
        steps.append(step)
        if d == 0:
            carry[cum_at : cum_at + heads, :] = sums
            bias[:, at] = jnp.where(allowed, 0.0, NEG)
        else:
            total = jnp.broadcast_to(sums[:, 127:128], (heads, 128))
            left = jnp.maximum(total - sums, 0.0) + after
            found = match_row(info, start, before, d, heads)
            fades.append(jnp.where(found, jnp.exp(-rate * left), 0.0))
            after = after + total
            both = carried & match_row(info, start, before, d, 128)
            bias[:, at] = jnp.where(both, 0.0, NEG)
    if last:
        small, step_at, fade_at = real, real_at[4] + heads * blocks[0], real_at[5]
        fade_at = fade_at + heads * (blocks[0] - 1)
        real[real_at[3] : real_at[3] + size, :] = origin[base : base + size, :]
        for p, source in ((0, origin), (1, before_carry)):
            where = carry_rows(heads, kv, PARTS[p], p == 0)[0]
            count = len(PARTS[p])
            low = where[4] + heads * 2
            rows = heads * count
            to = real_at[4] + heads * PARTS[p][0]
            real[to : to + rows, :] = source[low : low + rows, :]
            low, back = low + rows, count - (1 if p == 0 else 0)
            rows = heads * back
            to = real_at[5] + heads * (max(PARTS[p][0], 1) - 1)
            real[to : to + rows, :] = source[low : low + rows, :]
            turned, where = (keep, keep_at[3:5]) if p == 0 else (source, where[6:8])
            for g in range(kv):
                rows = 128 * count
                low = g * rows
                to = (g * (BACK + 1) + PARTS[p][0]) * 128
                half[half_at[1] + to : half_at[1] + to + rows, :] = turned[
                    where[0] + low : where[0] + low + rows, :
                ].astype(BF16)
                real[real_at[6] + to : real_at[6] + to + rows, :] = turned[
                    where[1] + low : where[1] + low + rows, :
                ]
    else:
        small, step_at = carry, carry_at[4] + heads * 2
        fade_at = step_at + heads * len(blocks)
        carry[carry_at[4] : carry_at[4] + heads, :] = after
    for i, step in enumerate(steps):
        small[step_at + heads * i : step_at + heads * (i + 1), :] = step
    for i, fade in enumerate(fades):
        small[fade_at + heads * i : fade_at + heads * (i + 1), :] = fade

    def one_head(h, unused):
        g = h // group
        query = queries[:, slab(0, h)]
        scores = mm(query, kt[g])
        scaled = scores * (LOG2E / math.sqrt(HDIM)) + bias[...]
        top = jnp.broadcast_to(jnp.max(scaled, axis=1, keepdims=True), (128, 128))
        if not first:
            old = before_carry[slab(before_at[0], h), :]
            top = jnp.maximum(old, top)
        weights = [
            jnp.exp2(scaled[:, 128 * i : 128 * i + 128] - top) for i in range(len(blocks))
        ]
        total = weights[0]
        for other in weights[1:]:
            total = total + other
        total = jnp.broadcast_to(jnp.sum(total, axis=1, keepdims=True), (128, 128))
        mixed = mm(jnp.concatenate([w.astype(BF16) for w in weights], axis=1), vv[g])
        weight_row = jnp.concatenate(
            [
                small[pl.ds(fade_at + heads * i + h, 1), :]
                * small[pl.ds(step_at + heads * (own + i) + h, 1), :]
                for i in range(past)
            ],
            axis=1,
        )
        state = mm_two(key32[g] * weight_row, vv[g, 128 * own :, :])
        if not first:
            scale = jnp.exp2(old - top)
            total = total + before_carry[slab(before_at[1], h), :] * scale
            mixed = mixed + before_carry[slab(before_at[2], h), :] * scale
            state = state + before_carry[slab(before_at[3], h), :]
        if not last:
            carry[slab(carry_at[0], h), :] = top
            carry[slab(carry_at[1], h), :] = total
            carry[slab(carry_at[2], h), :] = mixed
            carry[slab(carry_at[3], h), :] = state
        rate_h = constant[pl.ds(base + h, 1), :]
        if first:
            cum_row = jnp.broadcast_to(cum_ref[pl.ds(cum_at + h, 1), :], (128, 128))
            cum_col = cum_row.T
            decay = jnp.where(
                allowed, jnp.exp(-rate_h * jnp.maximum(cum_col - cum_row, 0.0)), 0.0
            )
            decayed = scores[:, :128] * decay
            keep[slab(keep_at[1], h), :] = decayed
            skipped = (
                constant[pl.ds(base + heads + h, 1), :] * keep[slab(keep_at[2], g), :]
            )
            mixing = decayed * small[pl.ds(step_at + h, 1), :]
            keep[slab(keep_at[0], h), :] = mm_two(mixing, vv[g, :128, :]) + skipped
        if last:
            teach = (mixed / total).astype(BF16)
            half[slab(half_at[0], h), :] = teach
            cum_col = jnp.broadcast_to(cum_ref[pl.ds(cum_at + h, 1), :], (128, 128)).T
            entering = jnp.where(carried, jnp.exp(-rate_h * cum_col), 0.0)
            off = mm_right(query, state) * entering
            raw = keep[slab(keep_at[0], h), :] + off
            real[slab(real_at[0], h), :] = raw
            real[slab(real_at[1], h), :] = off
            real[slab(real_at[2], h), :] = entering
            gained = raw * constant[pl.ds(base + 2 * heads + h, 1), :]
            acc[0] += raw * raw
            acc[1] += gained * gained
            acc[2] += gained * teach.astype(F32)
        return unused

    lax.fori_loop(0, heads, one_head, 0, unroll=4)
    if last:
        stats[...] = jnp.concatenate(
            [to_row(acc[0]), to_row(acc[1]), to_row(acc[2]), jnp.zeros((5, 128), F32)], axis=0
        )


def forward(kv, heads, rows, part, operands):
    blocks = PARTS[part]
    first, last = part == 0, part == len(PARTS) - 1
    wide = 128 * len(blocks)
    past = len(blocks) - (1 if first else 0)
    if last:
        outs = [
            shape((real_rows(heads, kv)[1], 128)),
            shape((half_rows(heads, kv)[1], 128), BF16),
            shape((8, 128)),
        ]
    else:
        outs = [shape((carry_rows(heads, kv, blocks, first)[1], 128))]
    if first:
        outs.append(shape((keep_rows(heads, kv, blocks)[1], 128)))
    scratch = [
        pltpu.VMEM((kv, HDIM, wide), BF16),
        pltpu.VMEM((kv, wide, HDIM), BF16),
        pltpu.VMEM((rows, wide), F32),
        pltpu.VMEM((kv, HDIM, 128 * past), F32),
    ]
    if last:
        scratch.append(pltpu.VMEM((3, rows, HDIM), F32))
    return pl.pallas_call(
        functools.partial(forward_kernel, kv, heads, blocks, first, last),
        out_shape=outs,
        in_specs=vmem(len(operands)),
        out_specs=vmem(len(outs)),
        scratch_shapes=scratch,
        compiler_params=SMALL,
        cost_estimate=pl.CostEstimate(
            flops=len(blocks) * heads * rows * 128 * 128 * 12,
            bytes_accessed=len(blocks) * 3 * 1024 * 1024,
            transcendentals=2 * heads * rows * wide,
        ),
        name="forward_" + "abc"[part],
    )(*operands)


def backward_kernel(kv, heads, features, row_total, *refs):
    queries, keep, real, half, stats, student_out, grads, gain_out, small_out, *refs = refs
    inv_col, coef_col, late, skip_rows, direct_rows, minus_rows, row_sums = refs
    keep_at = keep_rows(heads, kv, PARTS[0])[0]
    real_at = real_rows(heads, kv)[0]
    half_at = half_rows(heads, kv)[0]
    group = heads // kv
    size = 3 * heads + 8
    base = real_at[3]
    info = place_of(real[base + size - 8 : base + size, :], queries.shape[0])
    place, count = info[5], grads.shape[0]
    grads[...] = jnp.zeros_like(grads)
    row_sums[...] = jnp.zeros_like(row_sums)
    share = 2.0 / row_total
    squares, gained_squares, crossed = stats[0:1, :], stats[1:2, :], stats[2:3, :]
    inverse = lax.rsqrt(squares / features + EPSILON)
    inner = share * (inverse * gained_squares - crossed)
    coef = inverse * inverse * inverse * inner / features
    inv_col[...] = jnp.broadcast_to(inverse, (128, 128)).T
    coef_col[...] = jnp.broadcast_to(coef, (128, 128)).T
    row_i, col_i = iota((128, 128), 0), iota((128, 128), 1)
    later = (row_i >= col_i).astype(BF16)
    strict = (row_i < col_i).astype(BF16)

    def one_head(h, unused):
        g = h // group
        cols = slab(0, h)
        query = queries[:, cols]
        raw, off = real[slab(real_at[0], h), :], real[slab(real_at[1], h), :]
        scale = real[pl.ds(base + 2 * heads + h, 1), :]
        inv = inv_col[...]
        normed = raw * inv * scale
        student_out[:, cols] = normed.astype(BF16)
        grad_normed = (normed - half[slab(half_at[0], h), :].astype(F32)) * share
        gain_out[:, cols] = jnp.sum(grad_normed * raw * inv, axis=0, keepdims=True)
        grad = inv * grad_normed * scale - raw * coef_col[...]
        value = keep[slab(keep_at[2], g), :]
        skip_rows[pl.ds(h, 1), :] = jnp.sum(grad * value, axis=0, keepdims=True)
        entering = real[slab(real_at[2], h), :]
        grad_state = mm_two((grad * entering).T, query)
        turned = [slab(g * ((BACK + 1) * 128), d) for d in range(BACK + 1)]
        keys = jnp.concatenate(
            [half[pl.ds(half_at[1] + turned[d].start, 128), :] for d in range(1, BACK + 1)],
            axis=1,
        )
        reached = mm_two(grad_state, keys)
        for d in range(1, BACK + 1):
            values = real[pl.ds(real_at[6] + turned[d].start, 128), :]
            late[d - 1, pl.ds(h, 1), :] = jnp.sum(
                reached[:, 128 * d - 128 : 128 * d] * values, axis=0, keepdims=True
            )
        own_values = real[pl.ds(real_at[6] + turned[0].start, 128), :].astype(BF16)
        pulled = mm_two(grad, own_values)
        pairs = keep[slab(keep_at[1], h), :] * pulled
        direct_rows[pl.ds(h, 1), :] = jnp.sum(pairs, axis=0, keepdims=True)
        pairs = jnp.where(
            row_i > col_i, pairs * real[pl.ds(real_at[4] + h, 1), :], 0.0
        )
        minus_rows[pl.ds(h, 1), :] = jnp.sum(pairs, axis=0, keepdims=True)
        sums = jnp.sum(pairs + grad * off, axis=1, keepdims=True)
        row_sums[...] += jnp.where(col_i == h, jnp.broadcast_to(sums, (128, 128)), 0.0)
        return unused

    lax.fori_loop(0, heads, one_head, 0, unroll=4)

    def summed(x, triangle):
        high, low = two_parts(x)
        rest = (x - high.astype(F32) - low.astype(F32)).astype(BF16)
        return mm(high, triangle) + mm(low, triangle) + mm(rest, triangle)

    rate = real[base : base + heads, :]
    spanned = summed(row_sums[...].T[:heads, :] - minus_rows[...], later)
    grads[place] = direct_rows[...] - rate * spanned
    rate_rows = spanned * real[real_at[4] : real_at[4] + heads, :]
    earlier = jnp.zeros((heads, 128), F32)
    for d in range(BACK, 0, -1):
        step = real[real_at[4] + heads * d : real_at[4] + heads * (d + 1), :]
        fade = real[real_at[5] + heads * (d - 1) : real_at[5] + heads * d, :]
        direct = late[d - 1] * fade
        whole = direct * step
        spanned = summed(whole, strict) + earlier
        grads[lax.rem(place - d + count, count)] = direct - rate * spanned
        rate_rows = rate_rows + spanned * step
        earlier = earlier + jnp.sum(whole, axis=1, keepdims=True)
    small_out[...] = jnp.concatenate(
        [to_row(skip_rows[...]), -to_row(rate_rows * rate), jnp.zeros((6, 128), F32)], axis=0
    )


def weight_kernel(slope, hidden, gain, small, grads, keep, send):
    total = jnp.sum(grads[...], axis=0)
    grad_pre = total * slope[...]
    low = grad_pre.astype(BF16)
    heads = low.shape[0]
    count = keep.shape[0] // (heads + 1)
    tiles = gain.shape[1] // 128
    core = lax.axis_index("core")

    def fill(out, half):
        for j in range(count):
            i = half * count + j
            start = j * (heads + 1)
            out[start : start + heads, :] = mm(low, hidden[:, 128 * i : 128 * i + 128])
            at = slice(start + heads, start + heads + 1)
            if i < tiles:
                out[at, :] = gain[:, 128 * i : 128 * i + 128]
            elif i == tiles:
                out[at, :] = to_row(grad_pre)
            elif i == tiles + 1:
                out[at, :] = small[1:2, :]
            elif i == tiles + 2:
                out[at, :] = small[0:1, :]
            else:
                out[at, :] = jnp.zeros((1, 128), F32)

    for mine in range(2):

        @pl.when(core == mine)
        def _():
            fill(keep, mine)
            fill(send, 1 - mine)


def finish_kernel(mine, other, weight, bias, decay, skip, gain):
    heads = weight.shape[0]
    count = mine.shape[0] // (heads + 1)
    tiles = gain.shape[1] // 128
    core = lax.axis_index("core")

    def place(source, half):
        for j in range(count):
            i = half * count + j
            start = j * (heads + 1)
            weight[:, 128 * i : 128 * i + 128] = source[start : start + heads, :]
            row = source[start + heads : start + heads + 1, :]
            if i < tiles:
                gain[:, 128 * i : 128 * i + 128] = row
            if i == tiles:
                bias[...] = row[:, :heads]
            if i == tiles + 1:
                decay[...] = row[:, :heads]
            if i == tiles + 2:
                skip[...] = row[:, :heads]

    for half in range(2):

        @pl.when(core == half)
        def _():
            place(mine, half)
            place(other, 1 - half)


def vmem(count):
    return [pl.BlockSpec(memory_space=pltpu.VMEM)] * count


def smem(count):
    return [pl.BlockSpec(memory_space=pltpu.SMEM)] * count


def shape(dims, kind=F32):
    return jax.ShapeDtypeStruct(dims, kind)


LARGE = pltpu.CompilerParams(vmem_limit_bytes=56 * 1024 * 1024)
SMALL = pltpu.CompilerParams(vmem_limit_bytes=16 * 1024 * 1024)


def body(
    hidden_in,
    teacher_queries,
    teacher_keys,
    teacher_values,
    doc_lengths,
    dt_weight,
    dt_bias,
    decay_log,
    skip_gain,
    norm_gain,
):
    rows = teacher_queries.shape[1]
    heads = dt_weight.shape[1]
    kv = teacher_keys.shape[2] // HDIM
    width = heads * HDIM
    features = width * lax.axis_size("grp")
    depth = hidden_in.shape[2]
    chips = lax.axis_size("z")
    blocks = 2 * chips
    row_total = lax.axis_size("dp") * rows * blocks
    hidden = hidden_in[0]
    gain = norm_gain[None, :]
    cargo = 2 * kv * HDIM + 3 * heads

    payload, slope, consts = pl.pallas_call(
        functools.partial(prep_kernel, kv),
        out_shape=[
            shape((cargo, 128), BF16),
            shape((heads, 128)),
            shape((3 * heads + 8, 128)),
        ],
        in_specs=smem(4) + vmem(5),
        out_specs=vmem(3),
        compiler_params=LARGE,
        name="prep",
    )(
        doc_lengths, dt_bias, decay_log, skip_gain, gain, hidden, dt_weight.T,
        teacher_keys[0], teacher_values[0],
    )

    swap = [(0, 1), (1, 0)]
    hop = [(i, (i + 1) % chips) for i in range(chips)]
    jump = [(i, (i + 4) % chips) for i in range(chips)]
    queries = teacher_queries[0]
    run = functools.partial(forward, kv, heads, rows)

    def across(part):
        return lax.ppermute(part, "core", swap)

    hop1 = lax.ppermute(payload, "z", hop)
    hop4 = lax.ppermute(payload, "z", jump)
    sib0 = across(payload)
    hop2 = lax.ppermute(hop1, "z", hop)
    sib1 = across(hop1)
    origin, keep = run(0, [queries, payload, sib1, sib0, hop1, consts])
    hop2, hop4, origin = lax.optimization_barrier((hop2, hop4, origin))
    hop3 = lax.ppermute(hop2, "z", hop)
    sib2, sib4 = across(hop2), across(hop4)
    (carry,) = run(1, [queries, sib2, sib1, hop2, origin])
    hop3, carry = lax.optimization_barrier((hop3, carry))
    sib3 = across(hop3)
    real, half, stats = run(
        2, [queries, sib3, sib2, hop3, sib4, sib3, hop4, origin, carry, keep]
    )

    stats = lax.psum(stats, "grp")

    student, grads, grad_gain, small = pl.pallas_call(
        functools.partial(backward_kernel, kv, heads, features, row_total),
        out_shape=[
            shape((rows, width), BF16),
            shape((blocks, heads, 128)),
            shape((1, width)),
            shape((8, 128)),
        ],
        in_specs=vmem(5),
        out_specs=vmem(4),
        scratch_shapes=[
            pltpu.VMEM((rows, 128), F32),
            pltpu.VMEM((rows, 128), F32),
            pltpu.VMEM((BACK, heads, 128), F32),
            pltpu.VMEM((heads, 128), F32),
            pltpu.VMEM((heads, 128), F32),
            pltpu.VMEM((heads, 128), F32),
            pltpu.VMEM((128, 128), F32),
        ],
        compiler_params=SMALL,
        name="backward",
    )(queries, keep, real, half, stats)

    grads = lax.all_to_all(grads, ("z", "core"), 0, 0, tiled=True)

    axes = ("z", "dp")
    count = chips * lax.axis_size("dp")
    part = shape((count * (heads + 1), 128))
    keep, send = pl.pallas_call(
        weight_kernel,
        out_shape=[part, part],
        in_specs=vmem(5),
        out_specs=vmem(2),
        compiler_params=SMALL,
        name="weights",
    )(slope, hidden, grad_gain, small, grads)

    half = keep + lax.ppermute(send, "core", swap)
    half = half.reshape(count, heads + 1, 1, 128)
    got = lax.all_to_all(half, axes, 0, 0, tiled=True)
    summed = jnp.sum(got, axis=0)
    spread = jnp.broadcast_to(summed[None], got.shape)
    mine = lax.all_to_all(spread, axes, 0, 0, tiled=True)
    mine = mine.reshape(count * (heads + 1), 128)
    other = lax.ppermute(mine, "core", swap)
    grad_weight, bias, decay, skip, gained = pl.pallas_call(
        finish_kernel,
        out_shape=[shape((heads, depth))] + [shape((1, heads))] * 3 + [shape((1, width))],
        in_specs=vmem(2),
        out_specs=vmem(5),
        compiler_params=SMALL,
        name="finish",
    )(mine, other)
    return (student[None], grad_weight.T, bias[0], decay[0], skip[0], gained[0])


def solution(mesh):
    sizes = dict(mesh.shape)
    split = jax.sharding.Mesh(
        mesh.devices.reshape(sizes["ctx"] // 2, 2, sizes["grp"], sizes["dp"]),
        ("z", "core", "grp", "dp"),
    )
    ctx = ("z", "core")
    placed = (
        P("dp", ctx, None),
        P("dp", ctx, "grp"),
        P("dp", ctx, "grp"),
        P("dp", ctx, "grp"),
        P("dp", None),
        P(None, "grp"),
        P("grp"),
        P("grp"),
        P("grp"),
        P("grp"),
    )
    return jax.shard_map(
        body,
        mesh=split,
        in_specs=placed,
        out_specs=(P("dp", ctx, "grp"), P(None, "grp"), P("grp"), P("grp"), P("grp"), P("grp")),
        check_vma=False,
    )
```

```python
import functools
import math

import jax
import jax.numpy as jnp
from jax import lax
from jax.experimental import pallas as pl
from jax.experimental.pallas import tpu as pltpu
from jax.sharding import PartitionSpec as P

HDIM = 128
EPSILON = 1e-05
BACK = 8
NEG = -1e30
LOG2E = math.log2(math.e)
F32 = jnp.float32
BF16 = jnp.bfloat16


def mm(a, b):
    return jnp.dot(a, b, preferred_element_type=F32)


def two_parts(x):
    high = x.astype(BF16)
    return high, (x - high.astype(F32)).astype(BF16)


def mm_two(a, b):
    high, low = two_parts(a)
    return mm(high, b) + mm(low, b)


def mm_right(a, b):
    high, low = two_parts(b)
    return mm(a, high) + mm(a, low)


def iota(shape, dim):
    return lax.broadcasted_iota(jnp.int32, shape, dim)


def to_row(x):
    rows = x.shape[0]
    if rows < 128:
        x = jnp.concatenate([x, jnp.zeros((128 - rows, x.shape[1]), F32)], axis=0)
    return jnp.sum(x.T, axis=0, keepdims=True)


def column_of(values, rows):
    row = iota((rows, 128), 0)
    out = jnp.zeros((rows, 128), F32)
    for h in range(rows):
        out = jnp.where(row == h, values[h], out)
    return out


def place_of(consts, rows):
    core = lax.axis_index("core")
    place = lax.axis_index("z") * lax.axis_size("core") + core
    starts = [consts[i : i + 1, :].astype(jnp.int32) for i in range(3)]
    return (place * rows, *starts, core, place)


def segment_at(pos, info):
    return (
        (pos >= info[1]).astype(jnp.int32)
        + (pos >= info[2]).astype(jnp.int32)
        + (pos >= info[3]).astype(jnp.int32)
    )


def prep_kernel(
    kv, lengths, bias, decay, skip, gain, hidden, weight, keys, values, payload, slope, consts
):
    pre = (
        lax.dot_general(
            weight[...], hidden[...], (((1,), (1,)), ((), ())), preferred_element_type=F32
        )
        + column_of(bias, weight.shape[0])
    )
    step = jnp.maximum(pre, 0.0) + jnp.log1p(jnp.exp(-jnp.abs(pre)))
    slope[...] = 1.0 / (1.0 + jnp.exp(-pre))
    for g in range(kv):
        cols = slice(g * HDIM, (g + 1) * HDIM)
        payload[g * HDIM : (g + 1) * HDIM, :] = keys[:, cols].astype(F32).T.astype(BF16)
        payload[(kv + g) * HDIM : (kv + g + 1) * HDIM, :] = values[:, cols]
    heads = step.shape[0]
    consts[0:heads, :] = jnp.exp(column_of(decay, heads))
    consts[heads : 2 * heads, :] = column_of(skip, heads)
    for h in range(heads):
        consts[2 * heads + h : 2 * heads + h + 1, :] = gain[:, h * HDIM : (h + 1) * HDIM]
    one = lengths[0, 0]
    two = one + lengths[0, 1]
    starts = (one, two, two + lengths[0, 2], 0, 0, 0, 0, 0)
    row = iota((8, 128), 0)
    marks = jnp.zeros((8, 128), jnp.int32)
    for i in range(3):
        marks = jnp.where(row == i, starts[i], marks)
    consts[3 * heads :, :] = marks.astype(F32)
    first = 2 * kv * HDIM
    for part in range(3):
        piece = step.astype(BF16)
        payload[first + part * heads : first + (part + 1) * heads, :] = piece
        step = step - piece.astype(F32)


def masks(info):
    first = info[0]
    before = jnp.where(
        first > 0, segment_at(jnp.maximum(first - 1, 0) + iota((1, 128), 1) * 0, info), -1
    )
    row_pos = first + iota((128, 128), 0)
    col_pos = first + iota((128, 128), 1)
    row_seg = segment_at(row_pos, info)
    allowed = (row_seg == segment_at(col_pos, info)) & (col_pos <= row_pos)
    carried = row_seg == before
    return first, before, allowed, carried


def match_row(info, first, before, d, rows):
    pos = first - 128 * d + iota((rows, 128), 1)
    return (segment_at(pos, info) == before) & (pos >= 0)


PARTS = ((0,), (1, 2), (3, 4), (5, 6, 7, 8))


def layout(*sizes):
    starts, total = [], 0
    for size in sizes:
        starts.append(total)
        total += -(-size // 128) * 128
    return starts, total


def carry_rows(heads, kv, part):
    count = len(PARTS[part])
    wide = heads * 128
    if part == 0:
        return layout(wide, wide, wide, 0, heads * 3, 3 * heads + 8, 0, 0)
    turned = kv * count * 128
    return layout(wide, wide, wide, wide, heads * (2 + 2 * count), 0, turned, turned)


def keep_rows(heads, kv):
    return layout(heads * 128, heads * 128, kv * 128, kv * 128, kv * 128)


def real_rows(heads, kv):
    count = BACK + 1
    wide = heads * 128
    return layout(wide, wide, wide, 3 * heads + 8, count * heads, BACK * heads, kv * count * 128)


def half_rows(heads, kv):
    return layout(heads * 128, kv * (BACK + 1) * 128)


def slab(start, h):
    return pl.ds(pl.multiple_of(start + h * 128, 128), 128)


def forward_kernel(kv, heads, part, *refs):
    refs = list(refs)

    def take(count):
        out = refs[:count]
        del refs[:count]
        return out

    first, last = part == 0, part == len(PARTS) - 1
    blocks = PARTS[part]
    queries = take(1)[0]
    sources = [take(1 if d % 2 == 0 else 2) for d in blocks]
    if first:
        consts, carry, keep = take(3)
        cum_ref, value_ref = refs[-2:]
    else:
        origin = take(1)[0]
        carries = [origin] + take(part - 1)
        before_carry = carries[-1]
        before_at = carry_rows(heads, kv, part - 1)[0]
    if last:
        keep, real, half, stats = take(4)
        acc = refs[-1]
        acc[...] = jnp.zeros_like(acc)
    elif not first:
        carry = take(1)[0]
    kt, vv, bias, step_ref = take(4)
    if not first:
        key32, fade_ref = take(2)
    origin_at = carry_rows(heads, kv, 0)[0]
    keep_at = keep_rows(heads, kv)[0]
    real_at = real_rows(heads, kv)[0]
    half_at = half_rows(heads, kv)[0]
    carry_at = carry_rows(heads, kv, part)[0]
    if first:
        constant, base = consts, 0
        carry[carry_at[5] : carry_at[5] + consts.shape[0], :] = consts[...]
    else:
        constant, base = origin, origin_at[5]
    cum_at = origin_at[4] + heads
    group = heads // kv
    size = 3 * heads + 8
    info = place_of(constant[base + size - 8 : base + size, :], queries.shape[0])
    even_core = info[4] == 0
    start, before, allowed, carried = masks(info)

    reach = (iota((128, 128), 0) <= iota((128, 128), 1)).astype(BF16)
    if first:
        after = jnp.zeros((heads, 128), F32)
    else:
        after = before_carry[before_at[4] : before_at[4] + heads, :]
    rate = constant[base : base + heads, :]
    for i, d in enumerate(blocks):
        at = slice(128 * i, 128 * i + 128)
        near = sources[i]

        def piece(low, high):
            if d % 2 == 0:
                return near[0][low:high, :]
            return jnp.where(even_core, near[0][low:high, :], near[1][low:high, :])

        for g in range(kv):
            block = piece(g * HDIM, (g + 1) * HDIM)
            value = piece((kv + g) * HDIM, (kv + g + 1) * HDIM)
            kt[g, :, at] = block
            vv[g, at, :] = value
            block, value = block.astype(F32), value.astype(F32)
            if last:
                row = (g * (BACK + 1) + d) * 128
                half[half_at[1] + row : half_at[1] + row + 128, :] = kt[g, :, at]
                real[real_at[6] + row : real_at[6] + row + 128, :] = value.T
            else:
                row = (g * len(blocks) + i) * 128
                out, where = (keep, keep_at[3:5]) if first else (carry, carry_at[6:8])
                out[where[0] + row : where[0] + row + 128, :] = block
                out[where[1] + row : where[1] + row + 128, :] = value.T
            if first:
                keep[keep_at[2] + 128 * g : keep_at[2] + 128 * g + 128, :] = value
                value_ref[g] = value
            else:
                key32[g, :, at] = block
        first_step = 2 * kv * HDIM
        parts = [piece(first_step + k * heads, first_step + (k + 1) * heads) for k in range(3)]
        step = parts[0].astype(F32) + parts[1].astype(F32) + parts[2].astype(F32)
        sums = mm(parts[0], reach) + mm(parts[1], reach) + mm(parts[2], reach)
        step_ref[i] = step
        if first:
            carry[cum_at : cum_at + heads, :] = sums
            cum_ref[...] = sums
            bias[:, at] = jnp.where(allowed, 0.0, NEG)
        else:
            total = jnp.broadcast_to(sums[:, 127:128], (heads, 128))
            left = jnp.maximum(total - sums, 0.0) + after
            found = match_row(info, start, before, d, heads)
            fade_ref[i] = jnp.where(found, jnp.exp(-rate * left), 0.0)
            after = after + total
            both = carried & match_row(info, start, before, d, 128)
            bias[:, at] = jnp.where(both, 0.0, NEG)
    if last:
        real[real_at[3] : real_at[3] + size, :] = origin[base : base + size, :]
        for p, source in enumerate(carries):
            where = carry_rows(heads, kv, p)[0]
            count = len(PARTS[p])
            low = where[4] + heads * 2
            rows = heads * count
            to = real_at[4] + heads * PARTS[p][0]
            real[to : to + rows, :] = source[low : low + rows, :]
            if p > 0:
                low = low + rows
                to = real_at[5] + heads * (PARTS[p][0] - 1)
                real[to : to + rows, :] = source[low : low + rows, :]
            turned, where = (keep, keep_at[3:5]) if p == 0 else (source, where[6:8])
            for g in range(kv):
                rows = 128 * count
                low = g * rows
                to = (g * (BACK + 1) + PARTS[p][0]) * 128
                half[half_at[1] + to : half_at[1] + to + rows, :] = turned[
                    where[0] + low : where[0] + low + rows, :
                ].astype(BF16)
                real[real_at[6] + to : real_at[6] + to + rows, :] = turned[
                    where[1] + low : where[1] + low + rows, :
                ]
        small, step_at = real, real_at[4] + heads * blocks[0]
        fade_at = real_at[5] + heads * (blocks[0] - 1)
    else:
        small, step_at = carry, carry_at[4] + heads * 2
        fade_at = step_at + heads * len(blocks)
        carry[carry_at[4] : carry_at[4] + heads, :] = after
    for i in range(len(blocks)):
        small[step_at + heads * i : step_at + heads * (i + 1), :] = step_ref[i]
        if not first:
            small[fade_at + heads * i : fade_at + heads * (i + 1), :] = fade_ref[i]

    def one_head(h, unused):
        g = h // group
        query = queries[:, slab(0, h)]
        scores = mm(query, kt[g])
        scaled = scores * (LOG2E / math.sqrt(HDIM)) + bias[...]
        top = jnp.broadcast_to(jnp.max(scaled, axis=1, keepdims=True), (128, 128))
        if not first:
            old = before_carry[slab(before_at[0], h), :]
            top = jnp.maximum(old, top)
        weights = [
            jnp.exp2(scaled[:, 128 * i : 128 * i + 128] - top) for i in range(len(blocks))
        ]
        total = weights[0]
        for other in weights[1:]:
            total = total + other
        total = jnp.broadcast_to(jnp.sum(total, axis=1, keepdims=True), (128, 128))
        mixed = mm(jnp.concatenate([w.astype(BF16) for w in weights], axis=1), vv[g])
        if not first:
            weight_row = jnp.concatenate(
                [
                    fade_ref[i, pl.ds(h, 1), :] * step_ref[i, pl.ds(h, 1), :]
                    for i in range(len(blocks))
                ],
                axis=1,
            )
            state = mm_two(key32[g] * weight_row, vv[g])
            scale = jnp.exp2(old - top)
            total = total + before_carry[slab(before_at[1], h), :] * scale
            mixed = mixed + before_carry[slab(before_at[2], h), :] * scale
            if part > 1:
                state = state + before_carry[slab(before_at[3], h), :]
        if not last:
            carry[slab(carry_at[0], h), :] = top
            carry[slab(carry_at[1], h), :] = total
            carry[slab(carry_at[2], h), :] = mixed
            if not first:
                carry[slab(carry_at[3], h), :] = state
        rate_h = constant[pl.ds(base + h, 1), :]
        if first:
            cum_row = jnp.broadcast_to(cum_ref[pl.ds(h, 1), :], (128, 128))
            cum_col = cum_row.T
            decay = jnp.where(
                allowed, jnp.exp(-rate_h * jnp.maximum(cum_col - cum_row, 0.0)), 0.0
            )
            decayed = scores[:, :128] * decay
            keep[slab(keep_at[1], h), :] = decayed
            skipped = constant[pl.ds(base + heads + h, 1), :] * value_ref[g]
            mixing = decayed * step_ref[0, pl.ds(h, 1), :]
            keep[slab(keep_at[0], h), :] = mm_two(mixing, vv[g, :128, :]) + skipped
        if last:
            teach = (mixed / total).astype(BF16)
            half[slab(half_at[0], h), :] = teach
            cum_col = jnp.broadcast_to(origin[pl.ds(cum_at + h, 1), :], (128, 128)).T
            entering = jnp.where(carried, jnp.exp(-rate_h * cum_col), 0.0)
            off = mm_right(query, state) * entering
            raw = keep[slab(keep_at[0], h), :] + off
            real[slab(real_at[0], h), :] = raw
            real[slab(real_at[1], h), :] = off
            real[slab(real_at[2], h), :] = entering
            gained = raw * constant[pl.ds(base + 2 * heads + h, 1), :]
            acc[0] += raw * raw
            acc[1] += gained * gained
            acc[2] += gained * teach.astype(F32)
        return unused

    lax.fori_loop(0, heads, one_head, 0, unroll=4)
    if last:
        stats[...] = jnp.concatenate(
            [to_row(acc[0]), to_row(acc[1]), to_row(acc[2]), jnp.zeros((5, 128), F32)], axis=0
        )


def forward(kv, heads, rows, part, operands):
    blocks = PARTS[part]
    first, last = part == 0, part == len(PARTS) - 1
    wide = 128 * len(blocks)
    if last:
        outs = [
            shape((real_rows(heads, kv)[1], 128)),
            shape((half_rows(heads, kv)[1], 128), BF16),
            shape((8, 128)),
        ]
    else:
        outs = [shape((carry_rows(heads, kv, part)[1], 128))]
    if first:
        outs.append(shape((keep_rows(heads, kv)[1], 128)))
    scratch = [
        pltpu.VMEM((kv, HDIM, wide), BF16),
        pltpu.VMEM((kv, wide, HDIM), BF16),
        pltpu.VMEM((rows, wide), F32),
        pltpu.VMEM((len(blocks), heads, 128), F32),
    ]
    if first:
        scratch += [pltpu.VMEM((heads, 128), F32), pltpu.VMEM((kv, rows, HDIM), F32)]
    else:
        scratch += [
            pltpu.VMEM((kv, HDIM, wide), F32),
            pltpu.VMEM((len(blocks), heads, 128), F32),
        ]
    if last:
        scratch.append(pltpu.VMEM((3, rows, HDIM), F32))
    return pl.pallas_call(
        functools.partial(forward_kernel, kv, heads, part),
        out_shape=outs,
        in_specs=vmem(len(operands)),
        out_specs=vmem(len(outs)),
        scratch_shapes=scratch,
        compiler_params=SMALL,
        cost_estimate=pl.CostEstimate(
            flops=len(blocks) * heads * rows * 128 * 128 * 12,
            bytes_accessed=len(blocks) * 3 * 1024 * 1024,
            transcendentals=2 * heads * rows * wide,
        ),
        name="forward_" + "abcd"[part],
    )(*operands)


def backward_kernel(kv, heads, groups, features, row_total, *refs):
    queries, keep, real, half, *refs = refs
    stats = refs[0][...]
    for other in refs[1:groups]:
        stats = stats + other[...]
    student_out, grads, gain_out, small_out, *refs = refs[groups:]
    inv_col, coef_col, late, skip_rows, direct_rows, minus_rows, row_sums = refs
    keep_at = keep_rows(heads, kv)[0]
    real_at = real_rows(heads, kv)[0]
    half_at = half_rows(heads, kv)[0]
    group = heads // kv
    size = 3 * heads + 8
    base = real_at[3]
    info = place_of(real[base + size - 8 : base + size, :], queries.shape[0])
    place, count = info[5], grads.shape[0]
    grads[...] = jnp.zeros_like(grads)
    row_sums[...] = jnp.zeros_like(row_sums)
    share = 2.0 / row_total
    squares, gained_squares, crossed = stats[0:1, :], stats[1:2, :], stats[2:3, :]
    inverse = lax.rsqrt(squares / features + EPSILON)
    inner = share * (inverse * gained_squares - crossed)
    coef = inverse * inverse * inverse * inner / features
    inv_col[...] = jnp.broadcast_to(inverse, (128, 128)).T
    coef_col[...] = jnp.broadcast_to(coef, (128, 128)).T
    row_i, col_i = iota((128, 128), 0), iota((128, 128), 1)
    later = (row_i >= col_i).astype(BF16)
    strict = (row_i < col_i).astype(BF16)

    def one_head(h, unused):
        g = h // group
        cols = slab(0, h)
        query = queries[:, cols]
        raw, off = real[slab(real_at[0], h), :], real[slab(real_at[1], h), :]
        scale = real[pl.ds(base + 2 * heads + h, 1), :]
        inv = inv_col[...]
        normed = raw * inv * scale
        student_out[:, cols] = normed.astype(BF16)
        grad_normed = (normed - half[slab(half_at[0], h), :].astype(F32)) * share
        gain_out[:, cols] = jnp.sum(grad_normed * raw * inv, axis=0, keepdims=True)
        grad = inv * grad_normed * scale - raw * coef_col[...]
        value = keep[slab(keep_at[2], g), :]
        skip_rows[pl.ds(h, 1), :] = jnp.sum(grad * value, axis=0, keepdims=True)
        entering = real[slab(real_at[2], h), :]
        grad_state = mm_two((grad * entering).T, query)
        turned = [slab(g * ((BACK + 1) * 128), d) for d in range(BACK + 1)]
        keys = jnp.concatenate(
            [half[pl.ds(half_at[1] + turned[d].start, 128), :] for d in range(1, BACK + 1)],
            axis=1,
        )
        reached = mm_two(grad_state, keys)
        for d in range(1, BACK + 1):
            values = real[pl.ds(real_at[6] + turned[d].start, 128), :]
            late[d - 1, pl.ds(h, 1), :] = jnp.sum(
                reached[:, 128 * d - 128 : 128 * d] * values, axis=0, keepdims=True
            )
        own_values = real[pl.ds(real_at[6] + turned[0].start, 128), :].astype(BF16)
        pulled = mm_two(grad, own_values)
        pairs = keep[slab(keep_at[1], h), :] * pulled
        direct_rows[pl.ds(h, 1), :] = jnp.sum(pairs, axis=0, keepdims=True)
        pairs = jnp.where(
            row_i > col_i, pairs * real[pl.ds(real_at[4] + h, 1), :], 0.0
        )
        minus_rows[pl.ds(h, 1), :] = jnp.sum(pairs, axis=0, keepdims=True)
        sums = jnp.sum(pairs + grad * off, axis=1, keepdims=True)
        row_sums[...] += jnp.where(col_i == h, jnp.broadcast_to(sums, (128, 128)), 0.0)
        return unused

    lax.fori_loop(0, heads, one_head, 0, unroll=4)

    def summed(x, triangle):
        high, low = two_parts(x)
        rest = (x - high.astype(F32) - low.astype(F32)).astype(BF16)
        return mm(high, triangle) + mm(low, triangle) + mm(rest, triangle)

    rate = real[base : base + heads, :]
    spanned = summed(row_sums[...].T[:heads, :] - minus_rows[...], later)
    grads[place] = direct_rows[...] - rate * spanned
    rate_rows = spanned * real[real_at[4] : real_at[4] + heads, :]
    earlier = jnp.zeros((heads, 128), F32)
    for d in range(BACK, 0, -1):
        step = real[real_at[4] + heads * d : real_at[4] + heads * (d + 1), :]
        fade = real[real_at[5] + heads * (d - 1) : real_at[5] + heads * d, :]
        direct = late[d - 1] * fade
        whole = direct * step
        spanned = summed(whole, strict) + earlier
        grads[lax.rem(place - d + count, count)] = direct - rate * spanned
        rate_rows = rate_rows + spanned * step
        earlier = earlier + jnp.sum(whole, axis=1, keepdims=True)
    small_out[...] = jnp.concatenate(
        [to_row(skip_rows[...]), -to_row(rate_rows * rate), jnp.zeros((6, 128), F32)], axis=0
    )


def weight_kernel(slope, hidden, gain, small, grads, keep, send):
    total = jnp.sum(grads[...], axis=0)
    grad_pre = total * slope[...]
    low = grad_pre.astype(BF16)
    heads = low.shape[0]
    count = keep.shape[0] // (heads + 1)
    tiles = gain.shape[1] // 128
    core = lax.axis_index("core")

    def fill(out, half):
        for j in range(count):
            i = half * count + j
            start = j * (heads + 1)
            out[start : start + heads, :] = mm(low, hidden[:, 128 * i : 128 * i + 128])
            at = slice(start + heads, start + heads + 1)
            if i < tiles:
                out[at, :] = gain[:, 128 * i : 128 * i + 128]
            elif i == tiles:
                out[at, :] = to_row(grad_pre)
            elif i == tiles + 1:
                out[at, :] = small[1:2, :]
            elif i == tiles + 2:
                out[at, :] = small[0:1, :]
            else:
                out[at, :] = jnp.zeros((1, 128), F32)

    for mine in range(2):

        @pl.when(core == mine)
        def _():
            fill(keep, mine)
            fill(send, 1 - mine)


def finish_kernel(mine, other, weight, bias, decay, skip, gain):
    heads = weight.shape[0]
    count = mine.shape[0] // (heads + 1)
    tiles = gain.shape[1] // 128
    core = lax.axis_index("core")

    def place(source, half):
        for j in range(count):
            i = half * count + j
            start = j * (heads + 1)
            weight[:, 128 * i : 128 * i + 128] = source[start : start + heads, :]
            row = source[start + heads : start + heads + 1, :]
            if i < tiles:
                gain[:, 128 * i : 128 * i + 128] = row
            if i == tiles:
                bias[...] = row[:, :heads]
            if i == tiles + 1:
                decay[...] = row[:, :heads]
            if i == tiles + 2:
                skip[...] = row[:, :heads]

    for half in range(2):

        @pl.when(core == half)
        def _():
            place(mine, half)
            place(other, 1 - half)


def vmem(count):
    return [pl.BlockSpec(memory_space=pltpu.VMEM)] * count


def smem(count):
    return [pl.BlockSpec(memory_space=pltpu.SMEM)] * count


def shape(dims, kind=F32):
    return jax.ShapeDtypeStruct(dims, kind)


LARGE = pltpu.CompilerParams(vmem_limit_bytes=56 * 1024 * 1024)
SMALL = pltpu.CompilerParams(vmem_limit_bytes=16 * 1024 * 1024)


def body(
    hidden_in,
    teacher_queries,
    teacher_keys,
    teacher_values,
    doc_lengths,
    dt_weight,
    dt_bias,
    decay_log,
    skip_gain,
    norm_gain,
):
    rows = teacher_queries.shape[1]
    heads = dt_weight.shape[1]
    kv = teacher_keys.shape[2] // HDIM
    width = heads * HDIM
    features = width * lax.axis_size("grp")
    depth = hidden_in.shape[2]
    chips = lax.axis_size("z")
    blocks = 2 * chips
    row_total = lax.axis_size("dp") * rows * blocks
    hidden = hidden_in[0]
    gain = norm_gain[None, :]
    cargo = 2 * kv * HDIM + 3 * heads

    payload, slope, consts = pl.pallas_call(
        functools.partial(prep_kernel, kv),
        out_shape=[
            shape((cargo, 128), BF16),
            shape((heads, 128)),
            shape((3 * heads + 8, 128)),
        ],
        in_specs=smem(4) + vmem(5),
        out_specs=vmem(3),
        compiler_params=LARGE,
        name="prep",
    )(
        doc_lengths, dt_bias, decay_log, skip_gain, gain, hidden, dt_weight.T,
        teacher_keys[0], teacher_values[0],
    )

    swap = [(0, 1), (1, 0)]
    hop = [(i, (i + 1) % chips) for i in range(chips)]
    jump = [(i, (i + 4) % chips) for i in range(chips)]
    queries = teacher_queries[0]
    run = functools.partial(forward, kv, heads, rows)

    def across(part):
        return lax.ppermute(part, "core", swap)

    hop1 = lax.ppermute(payload, "z", hop)
    hop4 = lax.ppermute(payload, "z", jump)
    sib0 = across(payload)
    origin, keep = run(0, [queries, payload, consts])
    hop1, origin = lax.optimization_barrier((hop1, origin))
    hop2 = lax.ppermute(hop1, "z", hop)
    sib1 = across(hop1)
    (carry1,) = run(1, [queries, sib1, sib0, hop1, origin])
    hop2, hop4, carry1 = lax.optimization_barrier((hop2, hop4, carry1))
    hop3 = lax.ppermute(hop2, "z", hop)
    sib2, sib4 = across(hop2), across(hop4)
    (carry2,) = run(2, [queries, sib2, sib1, hop2, origin, carry1])
    hop3, carry2 = lax.optimization_barrier((hop3, carry2))
    sib3 = across(hop3)
    real, half, stats = run(
        3, [queries, sib3, sib2, hop3, sib4, sib3, hop4, origin, carry1, carry2, keep]
    )
    groups = lax.axis_size("grp")
    all_stats = [stats] + [
        lax.ppermute(stats, "grp", [(i, (i + k) % groups) for i in range(groups)])
        for k in range(1, groups)
    ]

    student, grads, grad_gain, small = pl.pallas_call(
        functools.partial(backward_kernel, kv, heads, groups, features, row_total),
        out_shape=[
            shape((rows, width), BF16),
            shape((blocks, heads, 128)),
            shape((1, width)),
            shape((8, 128)),
        ],
        in_specs=vmem(4 + groups),
        out_specs=vmem(4),
        scratch_shapes=[
            pltpu.VMEM((rows, 128), F32),
            pltpu.VMEM((rows, 128), F32),
            pltpu.VMEM((BACK, heads, 128), F32),
            pltpu.VMEM((heads, 128), F32),
            pltpu.VMEM((heads, 128), F32),
            pltpu.VMEM((heads, 128), F32),
            pltpu.VMEM((128, 128), F32),
        ],
        compiler_params=SMALL,
        name="backward",
    )(queries, keep, real, half, *all_stats)

    grads = lax.all_to_all(grads, ("z", "core"), 0, 0, tiled=True)

    axes = ("z", "dp")
    count = chips * lax.axis_size("dp")
    part = shape((count * (heads + 1), 128))
    keep, send = pl.pallas_call(
        weight_kernel,
        out_shape=[part, part],
        in_specs=vmem(5),
        out_specs=vmem(2),
        compiler_params=SMALL,
        name="weights",
    )(slope, hidden, grad_gain, small, grads)

    half = keep + lax.ppermute(send, "core", swap)
    half = half.reshape(count, heads + 1, 1, 128)
    got = lax.all_to_all(half, axes, 0, 0, tiled=True)
    summed = jnp.sum(got, axis=0)
    spread = jnp.broadcast_to(summed[None], got.shape)
    mine = lax.all_to_all(spread, axes, 0, 0, tiled=True)
    mine = mine.reshape(count * (heads + 1), 128)
    other = lax.ppermute(mine, "core", swap)
    grad_weight, bias, decay, skip, gained = pl.pallas_call(
        finish_kernel,
        out_shape=[shape((heads, depth))] + [shape((1, heads))] * 3 + [shape((1, width))],
        in_specs=vmem(2),
        out_specs=vmem(5),
        compiler_params=SMALL,
        name="finish",
    )(mine, other)
    return (student[None], grad_weight.T, bias[0], decay[0], skip[0], gained[0])


def solution(mesh):
    sizes = dict(mesh.shape)
    split = jax.sharding.Mesh(
        mesh.devices.reshape(sizes["ctx"] // 2, 2, sizes["grp"], sizes["dp"]),
        ("z", "core", "grp", "dp"),
    )
    ctx = ("z", "core")
    placed = (
        P("dp", ctx, None),
        P("dp", ctx, "grp"),
        P("dp", ctx, "grp"),
        P("dp", ctx, "grp"),
        P("dp", None),
        P(None, "grp"),
        P("grp"),
        P("grp"),
        P("grp"),
        P("grp"),
    )
    return jax.shard_map(
        body,
        mesh=split,
        in_specs=placed,
        out_specs=(P("dp", ctx, "grp"), P(None, "grp"), P("grp"), P("grp"), P("grp"), P("grp")),
        check_vma=False,
    )
```

```python
import functools
import math

import jax
import jax.numpy as jnp
from jax import lax
from jax.experimental import pallas as pl
from jax.experimental.pallas import tpu as pltpu
from jax.sharding import PartitionSpec as P

HDIM = 128
EPSILON = 1e-05
BACK = 8
NEG = -1e30
LOG2E = math.log2(math.e)
F32 = jnp.float32
BF16 = jnp.bfloat16


def mm(a, b):
    return jnp.dot(a, b, preferred_element_type=F32)


def two_parts(x):
    high = x.astype(BF16)
    return high, (x - high.astype(F32)).astype(BF16)


def mm_two(a, b):
    high, low = two_parts(a)
    return mm(high, b) + mm(low, b)


def mm_right(a, b):
    high, low = two_parts(b)
    return mm(a, high) + mm(a, low)


def iota(shape, dim):
    return lax.broadcasted_iota(jnp.int32, shape, dim)


def to_row(x):
    rows = x.shape[0]
    if rows < 128:
        x = jnp.concatenate([x, jnp.zeros((128 - rows, x.shape[1]), F32)], axis=0)
    return jnp.sum(x.T, axis=0, keepdims=True)


def column_of(values, rows):
    row = iota((rows, 128), 0)
    out = jnp.zeros((rows, 128), F32)
    for h in range(rows):
        out = jnp.where(row == h, values[h], out)
    return out


def place_of(consts, rows):
    core = lax.axis_index("core")
    place = lax.axis_index("z") * lax.axis_size("core") + core
    starts = [consts[i : i + 1, :].astype(jnp.int32) for i in range(3)]
    return (place * rows, *starts, core, place)


def segment_at(pos, info):
    return (
        (pos >= info[1]).astype(jnp.int32)
        + (pos >= info[2]).astype(jnp.int32)
        + (pos >= info[3]).astype(jnp.int32)
    )


def prep_kernel(
    kv,
    lengths,
    bias,
    decay,
    skip,
    gain,
    hidden,
    weight,
    keys,
    values,
    queries,
    payload,
    slope,
    local,
    consts,
):
    heads = weight.shape[0]
    pre = (
        lax.dot_general(
            hidden[...], weight[...], (((1,), (1,)), ((), ())), preferred_element_type=F32
        ).T
        + column_of(bias, heads)
    )
    step = jnp.maximum(pre, 0.0) + jnp.log1p(jnp.exp(-jnp.abs(pre)))
    slope[...] = 1.0 / (1.0 + jnp.exp(-pre))
    for g in range(kv):
        cols = slice(g * HDIM, (g + 1) * HDIM)
        payload[g * HDIM : (g + 1) * HDIM, :] = keys[:, cols].astype(F32).T.astype(BF16)
        payload[(kv + g) * HDIM : (kv + g + 1) * HDIM, :] = values[:, cols]
    consts[0:heads, :] = jnp.exp(column_of(decay, heads))
    consts[heads : 2 * heads, :] = column_of(skip, heads)
    for h in range(heads):
        consts[2 * heads + h : 2 * heads + h + 1, :] = gain[:, h * HDIM : (h + 1) * HDIM]
    one = lengths[0, 0]
    two = one + lengths[0, 1]
    starts = (one, two, two + lengths[0, 2], 0, 0, 0, 0, 0)
    row = iota((8, 128), 0)
    marks = jnp.zeros((8, 128), jnp.int32)
    for i in range(3):
        marks = jnp.where(row == i, starts[i], marks)
    consts[3 * heads : 3 * heads + 8, :] = marks.astype(F32)
    consts[3 * heads + 8 :, :] = jnp.zeros((consts.shape[0] - 3 * heads - 8, 128), F32)
    first = 2 * kv * HDIM
    for part in range(3):
        piece = step.astype(BF16)
        payload[first + part * heads : first + (part + 1) * heads, :] = piece
        step = step - piece.astype(F32)
    at = local_rows(heads, kv)[0]
    for h in range(heads):
        local[at[0] + 128 * h : at[0] + 128 * h + 128, :] = queries[:, 128 * h : 128 * h + 128]
    local[at[1] : at[1] + payload.shape[0], :] = payload[...]
    rest = consts[...]
    for part in range(3):
        piece = rest.astype(BF16)
        local[at[2 + part] : at[2 + part] + rest.shape[0], :] = piece
        rest = rest - piece.astype(F32)


def masks(info):
    first = info[0]
    before = jnp.where(
        first > 0, segment_at(jnp.maximum(first - 1, 0) + iota((1, 128), 1) * 0, info), -1
    )
    row_pos = first + iota((128, 128), 0)
    col_pos = first + iota((128, 128), 1)
    row_seg = segment_at(row_pos, info)
    allowed = (row_seg == segment_at(col_pos, info)) & (col_pos <= row_pos)
    carried = row_seg == before
    return first, before, allowed, carried


def match_row(info, first, before, d, rows):
    pos = first - 128 * d + iota((rows, 128), 1)
    return (segment_at(pos, info) == before) & (pos >= 0)


PARTS = ((0,), (1, 2), (3, 4), (5, 6), (7, 8))


def layout(*sizes):
    starts, total = [], 0
    for size in sizes:
        starts.append(total)
        total += -(-size // 128) * 128
    return starts, total


def carry_rows(heads, kv, part):
    count = len(PARTS[part])
    wide = heads * 128
    if part == 0:
        return layout(wide, wide, wide, 0, heads * 3, const_rows(heads), 0, 0)
    turned = kv * count * 128
    return layout(wide, wide, wide, wide, heads * (2 + 2 * count), 0, turned, turned)


def const_rows(heads):
    return -(-(3 * heads + 8) // 16) * 16


def local_rows(heads, kv):
    size = const_rows(heads)
    cargo = 2 * kv * HDIM + 3 * heads
    starts, total = [], 0
    for rows in (heads * 128, cargo, size, size, size):
        starts.append(total)
        total += rows
    return starts, total


def keep_rows(heads, kv):
    return layout(heads * 128, heads * 128, kv * 128, kv * 128, kv * 128)


def real_rows(heads, kv):
    count = BACK + 1
    wide = heads * 128
    return layout(
        wide, wide, wide, const_rows(heads), count * heads, BACK * heads, kv * count * 128
    )


def half_rows(heads, kv):
    return layout(heads * 128, kv * (BACK + 1) * 128)


def slab(start, h):
    return pl.ds(pl.multiple_of(start + h * 128, 128), 128)


def forward_kernel(kv, heads, part, *refs):
    refs = list(refs)

    def take(count):
        out = refs[:count]
        del refs[:count]
        return out

    first, last = part == 0, part == len(PARTS) - 1
    blocks = PARTS[part]
    local = take(1)[0]
    local_at = local_rows(heads, kv)[0]
    if first:
        sources = [[local]]
        carry, keep = take(2)
        cum_ref, value_ref, consts = refs[-3:]
        total = jnp.zeros(consts.shape, F32)
        for i in range(3):
            total += local[local_at[2 + i] : local_at[2 + i] + consts.shape[0], :].astype(F32)
        consts[...] = total
    else:
        sources = [take(1 if d % 2 == 0 else 2) for d in blocks]
        origin = take(1)[0]
        carries = [origin] + take(part - 1)
        before_carry = carries[-1]
        before_at = carry_rows(heads, kv, part - 1)[0]
    if last:
        keep, real, half, stats = take(4)
        acc = refs[-1]
        acc[...] = jnp.zeros_like(acc)
    elif not first:
        carry = take(1)[0]
    kt, vv, bias, step_ref = take(4)
    if not first:
        key32, fade_ref = take(2)
    origin_at = carry_rows(heads, kv, 0)[0]
    keep_at = keep_rows(heads, kv)[0]
    real_at = real_rows(heads, kv)[0]
    half_at = half_rows(heads, kv)[0]
    carry_at = carry_rows(heads, kv, part)[0]
    if first:
        constant, base = consts, 0
        carry[carry_at[5] : carry_at[5] + consts.shape[0], :] = consts[...]
    else:
        constant, base = origin, origin_at[5]
    cum_at = origin_at[4] + heads
    group = heads // kv
    size = 3 * heads + 8
    info = place_of(constant[base + size - 8 : base + size, :], 128)
    even_core = info[4] == 0
    start, before, allowed, carried = masks(info)

    reach = (iota((128, 128), 0) <= iota((128, 128), 1)).astype(BF16)
    if first:
        after = jnp.zeros((heads, 128), F32)
    else:
        after = before_carry[before_at[4] : before_at[4] + heads, :]
    rate = constant[base : base + heads, :]
    for i, d in enumerate(blocks):
        at = slice(128 * i, 128 * i + 128)
        near = sources[i]

        def piece(low, high):
            if first:
                return near[0][local_at[1] + low : local_at[1] + high, :]
            if d % 2 == 0:
                return near[0][low:high, :]
            return jnp.where(even_core, near[0][low:high, :], near[1][low:high, :])

        for g in range(kv):
            block = piece(g * HDIM, (g + 1) * HDIM)
            value = piece((kv + g) * HDIM, (kv + g + 1) * HDIM)
            kt[g, :, at] = block
            vv[g, at, :] = value
            block, value = block.astype(F32), value.astype(F32)
            if last:
                row = (g * (BACK + 1) + d) * 128
                half[half_at[1] + row : half_at[1] + row + 128, :] = kt[g, :, at]
                real[real_at[6] + row : real_at[6] + row + 128, :] = value.T
            else:
                row = (g * len(blocks) + i) * 128
                out, where = (keep, keep_at[3:5]) if first else (carry, carry_at[6:8])
                out[where[0] + row : where[0] + row + 128, :] = block
                out[where[1] + row : where[1] + row + 128, :] = value.T
            if first:
                keep[keep_at[2] + 128 * g : keep_at[2] + 128 * g + 128, :] = value
                value_ref[g] = value
            else:
                key32[g, :, at] = block
        first_step = 2 * kv * HDIM
        parts = [piece(first_step + k * heads, first_step + (k + 1) * heads) for k in range(3)]
        step = parts[0].astype(F32) + parts[1].astype(F32) + parts[2].astype(F32)
        sums = mm(parts[0], reach) + mm(parts[1], reach) + mm(parts[2], reach)
        step_ref[i] = step
        if first:
            carry[cum_at : cum_at + heads, :] = sums
            cum_ref[...] = sums
            bias[:, at] = jnp.where(allowed, 0.0, NEG)
        else:
            total = jnp.broadcast_to(sums[:, 127:128], (heads, 128))
            left = jnp.maximum(total - sums, 0.0) + after
            found = match_row(info, start, before, d, heads)
            fade_ref[i] = jnp.where(found, jnp.exp(-rate * left), 0.0)
            after = after + total
            both = carried & match_row(info, start, before, d, 128)
            bias[:, at] = jnp.where(both, 0.0, NEG)
    if last:
        real[real_at[3] : real_at[3] + size, :] = origin[base : base + size, :]
        for p, source in enumerate(carries):
            where = carry_rows(heads, kv, p)[0]
            count = len(PARTS[p])
            low = where[4] + heads * 2
            rows = heads * count
            to = real_at[4] + heads * PARTS[p][0]
            real[to : to + rows, :] = source[low : low + rows, :]
            if p > 0:
                low = low + rows
                to = real_at[5] + heads * (PARTS[p][0] - 1)
                real[to : to + rows, :] = source[low : low + rows, :]
            turned, where = (keep, keep_at[3:5]) if p == 0 else (source, where[6:8])
            for g in range(kv):
                rows = 128 * count
                low = g * rows
                to = (g * (BACK + 1) + PARTS[p][0]) * 128
                half[half_at[1] + to : half_at[1] + to + rows, :] = turned[
                    where[0] + low : where[0] + low + rows, :
                ].astype(BF16)
                real[real_at[6] + to : real_at[6] + to + rows, :] = turned[
                    where[1] + low : where[1] + low + rows, :
                ]
        small, step_at = real, real_at[4] + heads * blocks[0]
        fade_at = real_at[5] + heads * (blocks[0] - 1)
    else:
        small, step_at = carry, carry_at[4] + heads * 2
        fade_at = step_at + heads * len(blocks)
        carry[carry_at[4] : carry_at[4] + heads, :] = after
    for i in range(len(blocks)):
        small[step_at + heads * i : step_at + heads * (i + 1), :] = step_ref[i]
        if not first:
            small[fade_at + heads * i : fade_at + heads * (i + 1), :] = fade_ref[i]

    def one_head(h, unused):
        g = h // group
        query = local[slab(local_at[0], h), :]
        scores = mm(query, kt[g])
        scaled = scores * (LOG2E / math.sqrt(HDIM)) + bias[...]
        top = jnp.broadcast_to(jnp.max(scaled, axis=1, keepdims=True), (128, 128))
        if not first:
            old = before_carry[slab(before_at[0], h), :]
            top = jnp.maximum(old, top)
        weights = [
            jnp.exp2(scaled[:, 128 * i : 128 * i + 128] - top) for i in range(len(blocks))
        ]
        total = weights[0]
        for other in weights[1:]:
            total = total + other
        total = jnp.broadcast_to(jnp.sum(total, axis=1, keepdims=True), (128, 128))
        mixed = mm(jnp.concatenate([w.astype(BF16) for w in weights], axis=1), vv[g])
        if not first:
            weight_row = jnp.concatenate(
                [
                    fade_ref[i, pl.ds(h, 1), :] * step_ref[i, pl.ds(h, 1), :]
                    for i in range(len(blocks))
                ],
                axis=1,
            )
            state = mm_two(key32[g] * weight_row, vv[g])
            scale = jnp.exp2(old - top)
            total = total + before_carry[slab(before_at[1], h), :] * scale
            mixed = mixed + before_carry[slab(before_at[2], h), :] * scale
            if part > 1:
                state = state + before_carry[slab(before_at[3], h), :]
        if not last:
            carry[slab(carry_at[0], h), :] = top
            carry[slab(carry_at[1], h), :] = total
            carry[slab(carry_at[2], h), :] = mixed
            if not first:
                carry[slab(carry_at[3], h), :] = state
        rate_h = constant[pl.ds(base + h, 1), :]
        if first:
            cum_row = jnp.broadcast_to(cum_ref[pl.ds(h, 1), :], (128, 128))
            cum_col = cum_row.T
            decay = jnp.where(
                allowed, jnp.exp(-rate_h * jnp.maximum(cum_col - cum_row, 0.0)), 0.0
            )
            decayed = scores[:, :128] * decay
            keep[slab(keep_at[1], h), :] = decayed
            skipped = constant[pl.ds(base + heads + h, 1), :] * value_ref[g]
            mixing = decayed * step_ref[0, pl.ds(h, 1), :]
            keep[slab(keep_at[0], h), :] = mm_two(mixing, vv[g, :128, :]) + skipped
        if last:
            teach = (mixed / total).astype(BF16)
            half[slab(half_at[0], h), :] = teach
            cum_col = jnp.broadcast_to(origin[pl.ds(cum_at + h, 1), :], (128, 128)).T
            entering = jnp.where(carried, jnp.exp(-rate_h * cum_col), 0.0)
            off = mm_right(query, state) * entering
            raw = keep[slab(keep_at[0], h), :] + off
            real[slab(real_at[0], h), :] = raw
            real[slab(real_at[1], h), :] = off
            real[slab(real_at[2], h), :] = entering
            gained = raw * constant[pl.ds(base + 2 * heads + h, 1), :]
            acc[0] += raw * raw
            acc[1] += gained * gained
            acc[2] += gained * teach.astype(F32)
        return unused

    lax.fori_loop(0, heads, one_head, 0, unroll=4)
    if last:
        stats[...] = jnp.concatenate(
            [to_row(acc[0]), to_row(acc[1]), to_row(acc[2]), jnp.zeros((5, 128), F32)], axis=0
        )


def forward(kv, heads, rows, part, operands):
    blocks = PARTS[part]
    first, last = part == 0, part == len(PARTS) - 1
    wide = 128 * len(blocks)
    if last:
        outs = [
            shape((real_rows(heads, kv)[1], 128)),
            shape((half_rows(heads, kv)[1], 128), BF16),
            shape((8, 128)),
        ]
    else:
        outs = [shape((carry_rows(heads, kv, part)[1], 128))]
    if first:
        outs.append(shape((keep_rows(heads, kv)[1], 128)))
    scratch = [
        pltpu.VMEM((kv, HDIM, wide), BF16),
        pltpu.VMEM((kv, wide, HDIM), BF16),
        pltpu.VMEM((rows, wide), F32),
        pltpu.VMEM((len(blocks), heads, 128), F32),
    ]
    if first:
        scratch += [
            pltpu.VMEM((heads, 128), F32),
            pltpu.VMEM((kv, rows, HDIM), F32),
            pltpu.VMEM((const_rows(heads), 128), F32),
        ]
    else:
        scratch += [
            pltpu.VMEM((kv, HDIM, wide), F32),
            pltpu.VMEM((len(blocks), heads, 128), F32),
        ]
    if last:
        scratch.append(pltpu.VMEM((3, rows, HDIM), F32))
    return pl.pallas_call(
        functools.partial(forward_kernel, kv, heads, part),
        out_shape=outs,
        in_specs=vmem(len(operands)),
        out_specs=vmem(len(outs)),
        scratch_shapes=scratch,
        compiler_params=SMALL,
        cost_estimate=pl.CostEstimate(
            flops=len(blocks) * heads * rows * 128 * 128 * 12,
            bytes_accessed=len(blocks) * 3 * 1024 * 1024,
            transcendentals=2 * heads * rows * wide,
        ),
        name="forward_" + "abcde"[part],
    )(*operands)


def backward_kernel(kv, heads, groups, features, row_total, *refs):
    local, keep, real, half, *refs = refs
    stats = refs[0][...]
    for other in refs[1:groups]:
        stats = stats + other[...]
    student_out, grads, gain_out, small_out, *refs = refs[groups:]
    inv_col, coef_col, late, skip_rows, direct_rows, minus_rows, row_sums = refs
    keep_at = keep_rows(heads, kv)[0]
    real_at = real_rows(heads, kv)[0]
    half_at = half_rows(heads, kv)[0]
    group = heads // kv
    size = 3 * heads + 8
    base = real_at[3]
    info = place_of(real[base + size - 8 : base + size, :], 128)
    place, count = info[5], grads.shape[0]
    grads[...] = jnp.zeros_like(grads)
    row_sums[...] = jnp.zeros_like(row_sums)
    share = 2.0 / row_total
    squares, gained_squares, crossed = stats[0:1, :], stats[1:2, :], stats[2:3, :]
    inverse = lax.rsqrt(squares / features + EPSILON)
    inner = share * (inverse * gained_squares - crossed)
    coef = inverse * inverse * inverse * inner / features
    inv_col[...] = jnp.broadcast_to(inverse, (128, 128)).T
    coef_col[...] = jnp.broadcast_to(coef, (128, 128)).T
    row_i, col_i = iota((128, 128), 0), iota((128, 128), 1)
    later = (row_i >= col_i).astype(BF16)
    strict = (row_i < col_i).astype(BF16)

    def one_head(h, unused):
        g = h // group
        cols = slab(0, h)
        query = local[slab(0, h), :]
        raw, off = real[slab(real_at[0], h), :], real[slab(real_at[1], h), :]
        scale = real[pl.ds(base + 2 * heads + h, 1), :]
        inv = inv_col[...]
        normed = raw * inv * scale
        student_out[:, cols] = normed.astype(BF16)
        grad_normed = (normed - half[slab(half_at[0], h), :].astype(F32)) * share
        gain_out[:, cols] = jnp.sum(grad_normed * raw * inv, axis=0, keepdims=True)
        grad = inv * grad_normed * scale - raw * coef_col[...]
        value = keep[slab(keep_at[2], g), :]
        skip_rows[pl.ds(h, 1), :] = jnp.sum(grad * value, axis=0, keepdims=True)
        entering = real[slab(real_at[2], h), :]
        grad_state = mm_two((grad * entering).T, query)
        turned = [slab(g * ((BACK + 1) * 128), d) for d in range(BACK + 1)]
        keys = jnp.concatenate(
            [half[pl.ds(half_at[1] + turned[d].start, 128), :] for d in range(1, BACK + 1)],
            axis=1,
        )
        reached = mm_two(grad_state, keys)
        for d in range(1, BACK + 1):
            values = real[pl.ds(real_at[6] + turned[d].start, 128), :]
            late[d - 1, pl.ds(h, 1), :] = jnp.sum(
                reached[:, 128 * d - 128 : 128 * d] * values, axis=0, keepdims=True
            )
        own_values = real[pl.ds(real_at[6] + turned[0].start, 128), :].astype(BF16)
        pulled = mm_two(grad, own_values)
        pairs = keep[slab(keep_at[1], h), :] * pulled
        direct_rows[pl.ds(h, 1), :] = jnp.sum(pairs, axis=0, keepdims=True)
        pairs = jnp.where(
            row_i > col_i, pairs * real[pl.ds(real_at[4] + h, 1), :], 0.0
        )
        minus_rows[pl.ds(h, 1), :] = jnp.sum(pairs, axis=0, keepdims=True)
        sums = jnp.sum(pairs + grad * off, axis=1, keepdims=True)
        row_sums[...] += jnp.where(col_i == h, jnp.broadcast_to(sums, (128, 128)), 0.0)
        return unused

    lax.fori_loop(0, heads, one_head, 0, unroll=4)

    def summed(x, triangle):
        high, low = two_parts(x)
        rest = (x - high.astype(F32) - low.astype(F32)).astype(BF16)
        return mm(high, triangle) + mm(low, triangle) + mm(rest, triangle)

    rate = real[base : base + heads, :]
    spanned = summed(row_sums[...].T[:heads, :] - minus_rows[...], later)
    grads[place] = direct_rows[...] - rate * spanned
    rate_rows = spanned * real[real_at[4] : real_at[4] + heads, :]
    earlier = jnp.zeros((heads, 128), F32)
    for d in range(BACK, 0, -1):
        step = real[real_at[4] + heads * d : real_at[4] + heads * (d + 1), :]
        fade = real[real_at[5] + heads * (d - 1) : real_at[5] + heads * d, :]
        direct = late[d - 1] * fade
        whole = direct * step
        spanned = summed(whole, strict) + earlier
        grads[lax.rem(place - d + count, count)] = direct - rate * spanned
        rate_rows = rate_rows + spanned * step
        earlier = earlier + jnp.sum(whole, axis=1, keepdims=True)
    small_out[...] = jnp.concatenate(
        [to_row(skip_rows[...]), -to_row(rate_rows * rate), jnp.zeros((6, 128), F32)], axis=0
    )


def weight_kernel(slope, hidden, gain, small, grads, keep, send):
    total = jnp.sum(grads[...], axis=0)
    grad_pre = total * slope[...]
    low = grad_pre.astype(BF16)
    heads = low.shape[0]
    count = keep.shape[0] // (heads + 1)
    tiles = gain.shape[1] // 128
    core = lax.axis_index("core")

    def fill(out, half):
        for j in range(count):
            i = half * count + j
            start = j * (heads + 1)
            out[start : start + heads, :] = mm(low, hidden[:, 128 * i : 128 * i + 128])
            at = slice(start + heads, start + heads + 1)
            if i < tiles:
                out[at, :] = gain[:, 128 * i : 128 * i + 128]
            elif i == tiles:
                out[at, :] = to_row(grad_pre)
            elif i == tiles + 1:
                out[at, :] = small[1:2, :]
            elif i == tiles + 2:
                out[at, :] = small[0:1, :]
            else:
                out[at, :] = jnp.zeros((1, 128), F32)

    for mine in range(2):

        @pl.when(core == mine)
        def _():
            fill(keep, mine)
            fill(send, 1 - mine)


def finish_kernel(mine, other, weight, bias, decay, skip, gain):
    heads = weight.shape[0]
    count = mine.shape[0] // (heads + 1)
    tiles = gain.shape[1] // 128
    core = lax.axis_index("core")

    def place(source, half):
        for j in range(count):
            i = half * count + j
            start = j * (heads + 1)
            weight[:, 128 * i : 128 * i + 128] = source[start : start + heads, :]
            row = source[start + heads : start + heads + 1, :]
            if i < tiles:
                gain[:, 128 * i : 128 * i + 128] = row
            if i == tiles:
                bias[...] = row[:, :heads]
            if i == tiles + 1:
                decay[...] = row[:, :heads]
            if i == tiles + 2:
                skip[...] = row[:, :heads]

    for half in range(2):

        @pl.when(core == half)
        def _():
            place(mine, half)
            place(other, 1 - half)


def vmem(count):
    return [pl.BlockSpec(memory_space=pltpu.VMEM)] * count


def smem(count):
    return [pl.BlockSpec(memory_space=pltpu.SMEM)] * count


def shape(dims, kind=F32):
    return jax.ShapeDtypeStruct(dims, kind)


LARGE = pltpu.CompilerParams(vmem_limit_bytes=56 * 1024 * 1024)
SMALL = pltpu.CompilerParams(vmem_limit_bytes=16 * 1024 * 1024)


def body(
    hidden_in,
    teacher_queries,
    teacher_keys,
    teacher_values,
    doc_lengths,
    dt_weight,
    dt_bias,
    decay_log,
    skip_gain,
    norm_gain,
):
    rows = teacher_queries.shape[1]
    heads = dt_weight.shape[1]
    kv = teacher_keys.shape[2] // HDIM
    width = heads * HDIM
    features = width * lax.axis_size("grp")
    depth = hidden_in.shape[2]
    chips = lax.axis_size("z")
    blocks = 2 * chips
    row_total = lax.axis_size("dp") * rows * blocks
    hidden = hidden_in[0]
    gain = norm_gain[None, :]
    cargo = 2 * kv * HDIM + 3 * heads

    payload, slope, local = pl.pallas_call(
        functools.partial(prep_kernel, kv),
        out_shape=[
            shape((cargo, 128), BF16),
            shape((heads, 128)),
            shape((local_rows(heads, kv)[1], 128), BF16),
        ],
        in_specs=smem(4) + vmem(6),
        out_specs=vmem(3),
        scratch_shapes=[pltpu.VMEM((const_rows(heads), 128), F32)],
        compiler_params=LARGE,
        name="prep",
    )(
        doc_lengths, dt_bias, decay_log, skip_gain, gain, hidden, dt_weight.T,
        teacher_keys[0], teacher_values[0], teacher_queries[0],
    )

    swap = [(0, 1), (1, 0)]
    hop = [(i, (i + 1) % chips) for i in range(chips)]
    run = functools.partial(forward, kv, heads, rows)

    def across(part):
        return lax.ppermute(part, "core", swap)

    hop1 = lax.ppermute(payload, "z", hop)
    sib0 = across(payload)
    hop2 = lax.ppermute(hop1, "z", hop)
    sib1 = across(hop1)
    origin, keep = run(0, [local])
    hop2, origin = lax.optimization_barrier((hop2, origin))
    hop3 = lax.ppermute(hop2, "z", hop)
    sib2 = across(hop2)
    (carry1,) = run(1, [local, sib1, sib0, hop1, origin])
    hop3, carry1 = lax.optimization_barrier((hop3, carry1))
    hop4 = lax.ppermute(hop3, "z", hop)
    sib3 = across(hop3)
    (carry2,) = run(2, [local, sib2, sib1, hop2, origin, carry1])
    hop4, carry2 = lax.optimization_barrier((hop4, carry2))
    sib4 = across(hop4)
    (carry3,) = run(3, [local, sib3, sib2, hop3, origin, carry1, carry2])
    real, half, stats = run(
        4, [local, sib4, sib3, hop4, origin, carry1, carry2, carry3, keep]
    )
    groups = lax.axis_size("grp")
    all_stats = [stats] + [
        lax.ppermute(stats, "grp", [(i, (i + k) % groups) for i in range(groups)])
        for k in range(1, groups)
    ]

    student, grads, grad_gain, small = pl.pallas_call(
        functools.partial(backward_kernel, kv, heads, groups, features, row_total),
        out_shape=[
            shape((rows, width), BF16),
            shape((blocks, heads, 128)),
            shape((1, width)),
            shape((8, 128)),
        ],
        in_specs=vmem(4 + groups),
        out_specs=vmem(4),
        scratch_shapes=[
            pltpu.VMEM((rows, 128), F32),
            pltpu.VMEM((rows, 128), F32),
            pltpu.VMEM((BACK, heads, 128), F32),
            pltpu.VMEM((heads, 128), F32),
            pltpu.VMEM((heads, 128), F32),
            pltpu.VMEM((heads, 128), F32),
            pltpu.VMEM((128, 128), F32),
        ],
        compiler_params=SMALL,
        name="backward",
    )(local, keep, real, half, *all_stats)

    grads = lax.all_to_all(grads, ("z", "core"), 0, 0, tiled=True)

    axes = ("z", "dp")
    count = chips * lax.axis_size("dp")
    part = shape((count * (heads + 1), 128))
    keep, send = pl.pallas_call(
        weight_kernel,
        out_shape=[part, part],
        in_specs=vmem(5),
        out_specs=vmem(2),
        compiler_params=SMALL,
        name="weights",
    )(slope, hidden, grad_gain, small, grads)

    half = keep + lax.ppermute(send, "core", swap)
    half = half.reshape(count, heads + 1, 1, 128)
    got = lax.all_to_all(half, axes, 0, 0, tiled=True)
    summed = jnp.sum(got, axis=0)
    spread = jnp.broadcast_to(summed[None], got.shape)
    mine = lax.all_to_all(spread, axes, 0, 0, tiled=True)
    mine = mine.reshape(count * (heads + 1), 128)
    other = lax.ppermute(mine, "core", swap)
    grad_weight, bias, decay, skip, gained = pl.pallas_call(
        finish_kernel,
        out_shape=[shape((heads, depth))] + [shape((1, heads))] * 3 + [shape((1, width))],
        in_specs=vmem(2),
        out_specs=vmem(5),
        compiler_params=SMALL,
        name="finish",
    )(mine, other)
    return (student[None], grad_weight.T, bias[0], decay[0], skip[0], gained[0])


def solution(mesh):
    sizes = dict(mesh.shape)
    split = jax.sharding.Mesh(
        mesh.devices.reshape(sizes["ctx"] // 2, 2, sizes["grp"], sizes["dp"]),
        ("z", "core", "grp", "dp"),
    )
    ctx = ("z", "core")
    placed = (
        P("dp", ctx, None),
        P("dp", ctx, "grp"),
        P("dp", ctx, "grp"),
        P("dp", ctx, "grp"),
        P("dp", None),
        P(None, "grp"),
        P("grp"),
        P("grp"),
        P("grp"),
        P("grp"),
    )
    return jax.shard_map(
        body,
        mesh=split,
        in_specs=placed,
        out_specs=(P("dp", ctx, "grp"), P(None, "grp"), P("grp"), P("grp"), P("grp"), P("grp")),
        check_vma=False,
    )
```

```python
import functools
import math

import jax
import jax.numpy as jnp
from jax import lax
from jax.experimental import pallas as pl
from jax.experimental.pallas import tpu as pltpu
from jax.sharding import PartitionSpec as P

HDIM = 128
EPSILON = 1e-05
BACK = 8
NEG = -1e30
LOG2E = math.log2(math.e)
F32 = jnp.float32
BF16 = jnp.bfloat16


def mm(a, b):
    return jnp.dot(a, b, preferred_element_type=F32)


def two_parts(x):
    high = x.astype(BF16)
    return high, (x - high.astype(F32)).astype(BF16)


def mm_two(a, b):
    rows = a.shape[0]
    both = mm(jnp.concatenate(two_parts(a), axis=0), b)
    return both[:rows] + both[rows:]


def mm_apart(a, b):
    high, low = two_parts(a)
    return mm(high, b) + mm(low, b)


def mm_right(a, b):
    high, low = two_parts(b)
    return mm(a, high) + mm(a, low)


def iota(shape, dim):
    return lax.broadcasted_iota(jnp.int32, shape, dim)


def to_row(x):
    rows = x.shape[0]
    if rows < 128:
        x = jnp.concatenate([x, jnp.zeros((128 - rows, x.shape[1]), F32)], axis=0)
    return jnp.sum(x.T, axis=0, keepdims=True)


def column_of(values, rows):
    row = iota((rows, 128), 0)
    out = jnp.zeros((rows, 128), F32)
    for h in range(rows):
        out = jnp.where(row == h, values[h], out)
    return out


def place_of(consts, rows):
    core = lax.axis_index("core")
    place = lax.axis_index("z") * lax.axis_size("core") + core
    starts = [consts[i : i + 1, :].astype(jnp.int32) for i in range(3)]
    return (place * rows, *starts, core, place)


def segment_at(pos, info):
    return (
        (pos >= info[1]).astype(jnp.int32)
        + (pos >= info[2]).astype(jnp.int32)
        + (pos >= info[3]).astype(jnp.int32)
    )


def prep_kernel(
    kv,
    lengths,
    bias,
    decay,
    skip,
    gain,
    hidden_far,
    queries,
    weight,
    keys,
    values,
    payload,
    slope,
    local,
    sent,
    consts,
    hidden,
    asked,
    stage,
    fetched,
    moved,
):
    heads = weight.shape[0]
    side = sent.shape[1]
    at = local_rows(heads, kv)[0]
    chunks = fetched.shape[0]
    width = hidden.shape[1] // chunks
    fetches = []
    for i in range(chunks):
        part = slice(width * i, width * (i + 1))
        fetch = pltpu.make_async_copy(hidden_far.at[:, part], hidden.at[:, part], fetched.at[i])
        fetch.start()
        fetches.append(fetch)
    ask = pltpu.make_async_copy(queries, asked, moved.at[0])
    ask.start()
    pre = jnp.zeros((hidden.shape[0], heads), F32)
    for i in range(chunks):
        part = slice(width * i, width * (i + 1))
        fetches[i].wait()
        pre = pre + lax.dot_general(
            hidden[:, part], weight[:, part], (((1,), (1,)), ((), ())), preferred_element_type=F32
        )
    other = pl.multiple_of((1 - lax.axis_index("core")) * side, side)
    give = pltpu.make_async_copy(hidden.at[:, pl.ds(other, side)], sent, moved.at[1])
    give.start()
    pre = pre.T + column_of(bias, heads)
    step = jnp.maximum(pre, 0.0) + jnp.log1p(jnp.exp(-jnp.abs(pre)))
    slope[...] = 1.0 / (1.0 + jnp.exp(-pre))
    for g in range(kv):
        cols = slice(g * HDIM, (g + 1) * HDIM)
        payload[g * HDIM : (g + 1) * HDIM, :] = keys[:, cols].astype(F32).T.astype(BF16)
        payload[(kv + g) * HDIM : (kv + g + 1) * HDIM, :] = values[:, cols]
    consts[0:heads, :] = jnp.exp(column_of(decay, heads))
    consts[heads : 2 * heads, :] = column_of(skip, heads)
    for h in range(heads):
        consts[2 * heads + h : 2 * heads + h + 1, :] = gain[:, h * HDIM : (h + 1) * HDIM]
    one = lengths[0, 0]
    two = one + lengths[0, 1]
    starts = (one, two, two + lengths[0, 2], 0, 0, 0, 0, 0)
    row = iota((8, 128), 0)
    marks = jnp.zeros((8, 128), jnp.int32)
    for i in range(3):
        marks = jnp.where(row == i, starts[i], marks)
    consts[3 * heads : 3 * heads + 8, :] = marks.astype(F32)
    consts[3 * heads + 8 :, :] = jnp.zeros((consts.shape[0] - 3 * heads - 8, 128), F32)
    first = 2 * kv * HDIM
    for part in range(3):
        piece = step.astype(BF16)
        payload[first + part * heads : first + (part + 1) * heads, :] = piece
        step = step - piece.astype(F32)
    stage[at[1] : at[1] + payload.shape[0], :] = payload[...]
    rest = consts[...]
    for part in range(3):
        piece = rest.astype(BF16)
        stage[at[2 + part] : at[2 + part] + rest.shape[0], :] = piece
        rest = rest - piece.astype(F32)
    ask.wait()
    for h in range(heads):
        stage[at[0] + 128 * h : at[0] + 128 * h + 128, :] = asked[:, 128 * h : 128 * h + 128]
    put = pltpu.make_async_copy(stage, local, moved.at[2])
    put.start()
    give.wait()
    put.wait()


def masks(info):
    first = info[0]
    before = jnp.where(
        first > 0, segment_at(jnp.maximum(first - 1, 0) + iota((1, 128), 1) * 0, info), -1
    )
    row_pos = first + iota((128, 128), 0)
    col_pos = first + iota((128, 128), 1)
    row_seg = segment_at(row_pos, info)
    allowed = (row_seg == segment_at(col_pos, info)) & (col_pos <= row_pos)
    carried = row_seg == before
    return first, before, allowed, carried


def match_row(info, first, before, d, rows):
    pos = first - 128 * d + iota((rows, 128), 1)
    return (segment_at(pos, info) == before) & (pos >= 0)


PARTS = ((0,), (1, 2), (3, 4), (5, 6), (7, 8))


def layout(*sizes):
    starts, total = [], 0
    for size in sizes:
        starts.append(total)
        total += -(-size // 128) * 128
    return starts, total


def carry_rows(heads, kv, part):
    count = len(PARTS[part])
    wide = heads * 128
    if part == 0:
        return layout(wide, wide, wide, 0, heads * 3, const_rows(heads), 0, 0)
    turned = kv * count * 128
    return layout(
        wide, wide, wide, wide, heads * (2 + 2 * count), 0, turned, turned, wide if part == 2 else 0
    )


def const_rows(heads):
    return -(-(3 * heads + 8) // 16) * 16


def local_rows(heads, kv):
    size = const_rows(heads)
    cargo = 2 * kv * HDIM + 3 * heads
    starts, total = [], 0
    for rows in (heads * 128, cargo, size, size, size):
        starts.append(total)
        total += rows
    return starts, total


def keep_rows(heads, kv):
    return layout(heads * 128, heads * 128, kv * 128, kv * 128, kv * 128)


def real_rows(heads, kv):
    count = BACK + 1
    wide = heads * 128
    return layout(
        wide, wide, 0, const_rows(heads), count * heads, BACK * heads, kv * count * 128
    )


def half_rows(heads, kv):
    return layout(heads * 128, kv * (BACK + 1) * 128)


def slab(start, h):
    return pl.ds(pl.multiple_of(start + h * 128, 128), 128)


def forward_kernel(kv, heads, part, *refs):
    refs = list(refs)

    def take(count):
        out = refs[:count]
        del refs[:count]
        return out

    first, last = part == 0, part == len(PARTS) - 1
    blocks = PARTS[part]
    local = take(1)[0]
    local_at = local_rows(heads, kv)[0]
    if first:
        sources = [[local]]
        carry, keep = take(2)
        cum_ref, value_ref, consts = refs[-3:]
        total = jnp.zeros(consts.shape, F32)
        for i in range(3):
            total += local[local_at[2 + i] : local_at[2 + i] + consts.shape[0], :].astype(F32)
        consts[...] = total
    else:
        sources = [take(1 if d % 2 == 0 else 2) for d in blocks]
        origin = take(1)[0]
        carries = [origin] + take(part - 1)
        before_carry = carries[-1]
        before_at = carry_rows(heads, kv, part - 1)[0]
    if last:
        keep, real, half, stats = take(4)
        acc = refs[-1]
        acc[...] = jnp.zeros_like(acc)
    elif not first:
        carry = take(1)[0]
    kt, vv, bias, step_ref = take(4)
    if not first:
        key32, fade_ref = take(2)
    origin_at = carry_rows(heads, kv, 0)[0]
    keep_at = keep_rows(heads, kv)[0]
    real_at = real_rows(heads, kv)[0]
    half_at = half_rows(heads, kv)[0]
    carry_at = carry_rows(heads, kv, part)[0]
    if first:
        constant, base = consts, 0
        carry[carry_at[5] : carry_at[5] + consts.shape[0], :] = consts[...]
    else:
        constant, base = origin, origin_at[5]
    cum_at = origin_at[4] + heads
    enter_at = carry_rows(heads, kv, 2)[0][8]
    group = heads // kv
    size = 3 * heads + 8
    info = place_of(constant[base + size - 8 : base + size, :], 128)
    even_core = info[4] == 0
    start, before, allowed, carried = masks(info)

    reach = (iota((128, 128), 0) <= iota((128, 128), 1)).astype(BF16)
    if first:
        after = jnp.zeros((heads, 128), F32)
    else:
        after = before_carry[before_at[4] : before_at[4] + heads, :]
    rate = constant[base : base + heads, :]
    for i, d in enumerate(blocks):
        at = slice(128 * i, 128 * i + 128)
        near = sources[i]

        def piece(low, high):
            if first:
                return near[0][local_at[1] + low : local_at[1] + high, :]
            if d % 2 == 0:
                return near[0][low:high, :]
            return jnp.where(even_core, near[0][low:high, :], near[1][low:high, :])

        for g in range(kv):
            block = piece(g * HDIM, (g + 1) * HDIM)
            value = piece((kv + g) * HDIM, (kv + g + 1) * HDIM)
            kt[g, :, at] = block
            vv[g, at, :] = value
            block, value = block.astype(F32), value.astype(F32)
            if last:
                row = (g * (BACK + 1) + d) * 128
                half[half_at[1] + row : half_at[1] + row + 128, :] = kt[g, :, at]
                real[real_at[6] + row : real_at[6] + row + 128, :] = value.T
            else:
                row = (g * len(blocks) + i) * 128
                out, where = (keep, keep_at[3:5]) if first else (carry, carry_at[6:8])
                out[where[0] + row : where[0] + row + 128, :] = block
                out[where[1] + row : where[1] + row + 128, :] = value.T
            if first:
                keep[keep_at[2] + 128 * g : keep_at[2] + 128 * g + 128, :] = value
                value_ref[g] = value
            else:
                key32[g, :, at] = block
        first_step = 2 * kv * HDIM
        parts = [piece(first_step + k * heads, first_step + (k + 1) * heads) for k in range(3)]
        step = parts[0].astype(F32) + parts[1].astype(F32) + parts[2].astype(F32)
        sums = mm(parts[0], reach) + mm(parts[1], reach) + mm(parts[2], reach)
        step_ref[i] = step
        if first:
            carry[cum_at : cum_at + heads, :] = sums
            cum_ref[...] = sums
            bias[:, at] = jnp.where(allowed, 0.0, NEG)
        else:
            total = jnp.broadcast_to(sums[:, 127:128], (heads, 128))
            left = jnp.maximum(total - sums, 0.0) + after
            found = match_row(info, start, before, d, heads)
            fade_ref[i] = jnp.where(found, jnp.exp(-rate * left), 0.0)
            after = after + total
            both = carried & match_row(info, start, before, d, 128)
            bias[:, at] = jnp.where(both, 0.0, NEG)
    if last:
        real[real_at[3] : real_at[3] + size, :] = origin[base : base + size, :]
        for p, source in enumerate(carries):
            where = carry_rows(heads, kv, p)[0]
            count = len(PARTS[p])
            low = where[4] + heads * 2
            rows = heads * count
            to = real_at[4] + heads * PARTS[p][0]
            real[to : to + rows, :] = source[low : low + rows, :]
            if p > 0:
                low = low + rows
                to = real_at[5] + heads * (PARTS[p][0] - 1)
                real[to : to + rows, :] = source[low : low + rows, :]
            turned, where = (keep, keep_at[3:5]) if p == 0 else (source, where[6:8])
            for g in range(kv):
                rows = 128 * count
                low = g * rows
                to = (g * (BACK + 1) + PARTS[p][0]) * 128
                half[half_at[1] + to : half_at[1] + to + rows, :] = turned[
                    where[0] + low : where[0] + low + rows, :
                ].astype(BF16)
                real[real_at[6] + to : real_at[6] + to + rows, :] = turned[
                    where[1] + low : where[1] + low + rows, :
                ]
        small, step_at = real, real_at[4] + heads * blocks[0]
        fade_at = real_at[5] + heads * (blocks[0] - 1)
    else:
        small, step_at = carry, carry_at[4] + heads * 2
        fade_at = step_at + heads * len(blocks)
        carry[carry_at[4] : carry_at[4] + heads, :] = after
    for i in range(len(blocks)):
        small[step_at + heads * i : step_at + heads * (i + 1), :] = step_ref[i]
        if not first:
            small[fade_at + heads * i : fade_at + heads * (i + 1), :] = fade_ref[i]

    def rate_of(h):
        return constant[pl.ds(base + h, 1), :]

    def one_head(h, unused):
        g = h // group
        query = local[slab(local_at[0], h), :]
        scores = mm(query, kt[g])
        scaled = scores * (LOG2E / math.sqrt(HDIM)) + bias[...]
        top = jnp.broadcast_to(jnp.max(scaled, axis=1, keepdims=True), (128, 128))
        if not first:
            old = before_carry[slab(before_at[0], h), :]
            top = jnp.maximum(old, top)
        weights = [
            jnp.exp2(scaled[:, 128 * i : 128 * i + 128] - top) for i in range(len(blocks))
        ]
        total = weights[0]
        for other in weights[1:]:
            total = total + other
        total = jnp.broadcast_to(jnp.sum(total, axis=1, keepdims=True), (128, 128))
        weights = jnp.concatenate([w.astype(BF16) for w in weights], axis=1)
        if not first:
            weight_row = jnp.concatenate(
                [
                    fade_ref[i, pl.ds(h, 1), :] * step_ref[i, pl.ds(h, 1), :]
                    for i in range(len(blocks))
                ],
                axis=1,
            )
            mixed = mm(weights, vv[g])
            state = mm_apart(key32[g] * weight_row, vv[g])
            scale = jnp.exp2(old - top)
            total = total + before_carry[slab(before_at[1], h), :] * scale
            mixed = mixed + before_carry[slab(before_at[2], h), :] * scale
            if part > 1:
                state = state + before_carry[slab(before_at[3], h), :]
        else:
            decay_row = rate_of(h)
            cum_row = jnp.broadcast_to(cum_ref[pl.ds(h, 1), :], (128, 128))
            cum_col = cum_row.T
            decay = jnp.where(
                allowed, jnp.exp(-decay_row * jnp.maximum(cum_col - cum_row, 0.0)), 0.0
            )
            decayed = scores[:, :128] * decay
            keep[slab(keep_at[1], h), :] = decayed
            skipped = constant[pl.ds(base + heads + h, 1), :] * value_ref[g]
            high, low = two_parts(decayed * step_ref[0, pl.ds(h, 1), :])
            joined = mm(jnp.concatenate([weights, high, low], axis=0), vv[g])
            mixed = joined[:128]
            keep[slab(keep_at[0], h), :] = joined[128:256] + joined[256:] + skipped
        if not last:
            carry[slab(carry_at[0], h), :] = top
            carry[slab(carry_at[1], h), :] = total
            carry[slab(carry_at[2], h), :] = mixed
            if not first:
                carry[slab(carry_at[3], h), :] = state
        if part == 2:
            cum_col = jnp.broadcast_to(origin[pl.ds(cum_at + h, 1), :], (128, 128)).T
            carry[slab(enter_at, h), :] = jnp.where(
                carried, jnp.exp(-rate_of(h) * cum_col), 0.0
            )
        if last:
            teach = (mixed / total).astype(BF16)
            half[slab(half_at[0], h), :] = teach
            off = mm_right(query, state) * carries[2][slab(enter_at, h), :]
            raw = keep[slab(keep_at[0], h), :] + off
            real[slab(real_at[0], h), :] = raw
            real[slab(real_at[1], h), :] = off
            gained = raw * constant[pl.ds(base + 2 * heads + h, 1), :]
            acc[0] += raw * raw
            acc[1] += gained * gained
            acc[2] += gained * teach.astype(F32)
        return unused

    lax.fori_loop(0, heads, one_head, 0, unroll=(8, 4, 4, 8, 16)[part])
    if last:
        stats[...] = jnp.concatenate(
            [to_row(acc[0]), to_row(acc[1]), to_row(acc[2]), jnp.zeros((5, 128), F32)], axis=0
        )


def forward(kv, heads, rows, part, operands):
    blocks = PARTS[part]
    first, last = part == 0, part == len(PARTS) - 1
    wide = 128 * len(blocks)
    if last:
        outs = [
            shape((real_rows(heads, kv)[1], 128)),
            shape((half_rows(heads, kv)[1], 128), BF16),
            shape((8, 128)),
        ]
    else:
        outs = [shape((carry_rows(heads, kv, part)[1], 128))]
    if first:
        outs.append(shape((keep_rows(heads, kv)[1], 128)))
    scratch = [
        pltpu.VMEM((kv, HDIM, wide), BF16),
        pltpu.VMEM((kv, wide, HDIM), BF16),
        pltpu.VMEM((rows, wide), F32),
        pltpu.VMEM((len(blocks), heads, 128), F32),
    ]
    if first:
        scratch += [
            pltpu.VMEM((heads, 128), F32),
            pltpu.VMEM((kv, rows, HDIM), F32),
            pltpu.VMEM((const_rows(heads), 128), F32),
        ]
    else:
        scratch += [
            pltpu.VMEM((kv, HDIM, wide), F32),
            pltpu.VMEM((len(blocks), heads, 128), F32),
        ]
    if last:
        scratch.append(pltpu.VMEM((3, rows, HDIM), F32))
    return pl.pallas_call(
        functools.partial(forward_kernel, kv, heads, part),
        out_shape=outs,
        in_specs=vmem(len(operands)),
        out_specs=vmem(len(outs)),
        scratch_shapes=scratch,
        compiler_params=SMALL,
        cost_estimate=pl.CostEstimate(
            flops=len(blocks) * heads * rows * 128 * 128 * 12,
            bytes_accessed=len(blocks) * 3 * 1024 * 1024,
            transcendentals=2 * heads * rows * wide,
        ),
        name="forward_" + "abcde"[part],
    )(*operands)


def backward_kernel(kv, heads, groups, features, row_total, *refs):
    local, keep, enter, real, half, *refs = refs
    stats = refs[0][...]
    for other in refs[1:groups]:
        stats = stats + other[...]
    student_out, grads, gain_out, small_out, *refs = refs[groups:]
    inv_col, coef_col, late, skip_rows, direct_rows, minus_rows, row_sums = refs
    keep_at = keep_rows(heads, kv)[0]
    real_at = real_rows(heads, kv)[0]
    half_at = half_rows(heads, kv)[0]
    group = heads // kv
    enter_at = carry_rows(heads, kv, 2)[0][8]
    size = 3 * heads + 8
    base = real_at[3]
    info = place_of(real[base + size - 8 : base + size, :], 128)
    place, count = info[5], grads.shape[0]
    grads[...] = jnp.zeros_like(grads)
    row_sums[...] = jnp.zeros_like(row_sums)
    share = 2.0 / row_total
    squares, gained_squares, crossed = stats[0:1, :], stats[1:2, :], stats[2:3, :]
    inverse = lax.rsqrt(squares / features + EPSILON)
    inner = share * (inverse * gained_squares - crossed)
    coef = inverse * inverse * inverse * inner / features
    inv_col[...] = jnp.broadcast_to(inverse, (128, 128)).T
    coef_col[...] = jnp.broadcast_to(coef, (128, 128)).T
    row_i, col_i = iota((128, 128), 0), iota((128, 128), 1)
    later = (row_i >= col_i).astype(BF16)
    strict = (row_i < col_i).astype(BF16)

    def one_head(h, unused):
        g = h // group
        cols = slab(0, h)
        query = local[slab(0, h), :]
        raw, off = real[slab(real_at[0], h), :], real[slab(real_at[1], h), :]
        scale = real[pl.ds(base + 2 * heads + h, 1), :]
        inv = inv_col[...]
        normed = raw * inv * scale
        student_out[:, cols] = normed.astype(BF16)
        grad_normed = (normed - half[slab(half_at[0], h), :].astype(F32)) * share
        gain_out[:, cols] = jnp.sum(grad_normed * raw * inv, axis=0, keepdims=True)
        grad = inv * grad_normed * scale - raw * coef_col[...]
        value = keep[slab(keep_at[2], g), :]
        skip_rows[pl.ds(h, 1), :] = jnp.sum(grad * value, axis=0, keepdims=True)
        entering = enter[slab(enter_at, h), :]
        grad_state = mm_two((grad * entering).T, query)
        turned = [slab(g * ((BACK + 1) * 128), d) for d in range(BACK + 1)]
        keys = jnp.concatenate(
            [half[pl.ds(half_at[1] + turned[d].start, 128), :] for d in range(1, BACK + 1)],
            axis=1,
        )
        reached = mm_two(grad_state, keys)
        for d in range(1, BACK + 1):
            values = real[pl.ds(real_at[6] + turned[d].start, 128), :]
            late[d - 1, pl.ds(h, 1), :] = jnp.sum(
                reached[:, 128 * d - 128 : 128 * d] * values, axis=0, keepdims=True
            )
        own_values = real[pl.ds(real_at[6] + turned[0].start, 128), :].astype(BF16)
        pulled = mm_two(grad, own_values)
        pairs = keep[slab(keep_at[1], h), :] * pulled
        direct_rows[pl.ds(h, 1), :] = jnp.sum(pairs, axis=0, keepdims=True)
        pairs = jnp.where(
            row_i > col_i, pairs * real[pl.ds(real_at[4] + h, 1), :], 0.0
        )
        minus_rows[pl.ds(h, 1), :] = jnp.sum(pairs, axis=0, keepdims=True)
        sums = jnp.sum(pairs + grad * off, axis=1, keepdims=True)
        row_sums[...] += jnp.where(col_i == h, jnp.broadcast_to(sums, (128, 128)), 0.0)
        return unused

    lax.fori_loop(0, heads, one_head, 0, unroll=16)

    def summed(x, triangle):
        high, low = two_parts(x)
        rest = (x - high.astype(F32) - low.astype(F32)).astype(BF16)
        return mm(high, triangle) + mm(low, triangle) + mm(rest, triangle)

    rate = real[base : base + heads, :]
    spanned = summed(row_sums[...].T[:heads, :] - minus_rows[...], later)
    grads[place] = direct_rows[...] - rate * spanned
    rate_rows = spanned * real[real_at[4] : real_at[4] + heads, :]
    earlier = jnp.zeros((heads, 128), F32)
    for d in range(BACK, 0, -1):
        step = real[real_at[4] + heads * d : real_at[4] + heads * (d + 1), :]
        fade = real[real_at[5] + heads * (d - 1) : real_at[5] + heads * d, :]
        direct = late[d - 1] * fade
        whole = direct * step
        spanned = summed(whole, strict) + earlier
        grads[lax.rem(place - d + count, count)] = direct - rate * spanned
        rate_rows = rate_rows + spanned * step
        earlier = earlier + jnp.sum(whole, axis=1, keepdims=True)
    small_out[...] = jnp.concatenate(
        [to_row(skip_rows[...]), -to_row(rate_rows * rate), jnp.zeros((6, 128), F32)], axis=0
    )


def fold_kernel(grads, gain, small, out):
    total = jnp.sum(grads[...], axis=0)
    rows = total.shape[0]
    tiles = gain.shape[1] // 128
    out[0:rows, :] = total
    for i in range(tiles):
        out[rows + i : rows + i + 1, :] = gain[:, 128 * i : 128 * i + 128]
    out[rows + tiles : rows + tiles + 8, :] = small[...]


def weight_kernel(own, other, slope, slope_other, hidden, far, out, wide):
    heads = slope.shape[0]
    total = own[...] + other[...]
    core = lax.axis_index("core")
    low_core = core == 0
    near_slope, far_slope = slope[...], slope_other[...]
    top, bottom = total[0:heads], total[heads : 2 * heads]
    near_pre = jnp.where(low_core, top, bottom) * near_slope
    far_pre = jnp.where(low_core, bottom, top) * far_slope
    near_low, far_low = near_pre.astype(BF16), far_pre.astype(BF16)
    side = far.shape[1]
    count = side // 128
    tiles = total.shape[0] - 2 * heads - 8
    lines = [total[2 * heads + i : 2 * heads + i + 1] for i in range(tiles)]
    lines.append(to_row(near_pre + far_pre))
    base = 2 * heads + tiles
    lines += [total[base + 1 : base + 2], total[base : base + 1]]
    for j in range(count):
        start = j * (heads + 2)
        near = hidden[:, pl.ds(pl.multiple_of(core * side + 128 * j, 128), 128)]
        wide[start : start + heads, :] = mm(near_low, near) + mm(
            far_low, far[:, 128 * j : 128 * j + 128]
        )
        line = jnp.zeros((1, 128), F32)
        if j < len(lines):
            line = jnp.where(low_core, lines[j], line)
        high = line.astype(BF16).astype(F32)
        wide[start + heads : start + heads + 1, :] = high
        wide[start + heads + 1 : start + heads + 2, :] = line - high
    out[...] = wide[...].astype(BF16)


def spread_kernel(count, got, out, wide):
    wide[...] = got[...].astype(F32)
    each = wide.shape[0] // count
    total = wide[0:each, :]
    for j in range(1, count):
        total = total + wide[each * j : each * (j + 1), :]
    small = total[each - 2 : each - 1, :] + total[each - 1 : each, :]
    for j in range(count):
        start = (each - 1) * j
        out[start : start + each - 2, :] = total[: each - 2, :]
        out[start + each - 2 : start + each - 1, :] = small


def finish_kernel(mine, other, weight, bias, decay, skip, gain):
    heads = weight.shape[0]
    count = mine.shape[0] // (heads + 1)
    tiles = gain.shape[1] // 128
    core = lax.axis_index("core")

    def place(source, half):
        for j in range(count):
            i = half * count + j
            start = j * (heads + 1)
            weight[:, 128 * i : 128 * i + 128] = source[start : start + heads, :]
            row = source[start + heads : start + heads + 1, :]
            if i < tiles:
                gain[:, 128 * i : 128 * i + 128] = row
            if i == tiles:
                bias[...] = row[:, :heads]
            if i == tiles + 1:
                decay[...] = row[:, :heads]
            if i == tiles + 2:
                skip[...] = row[:, :heads]

    for half in range(2):

        @pl.when(core == half)
        def _():
            place(mine, half)
            place(other, 1 - half)


def vmem(count):
    return [pl.BlockSpec(memory_space=pltpu.VMEM)] * count


def smem(count):
    return [pl.BlockSpec(memory_space=pltpu.SMEM)] * count


def anywhere(count):
    return [pl.BlockSpec(memory_space=pl.ANY)] * count


def shape(dims, kind=F32):
    return jax.ShapeDtypeStruct(dims, kind)


LARGE = pltpu.CompilerParams(vmem_limit_bytes=56 * 1024 * 1024)
SMALL = pltpu.CompilerParams(vmem_limit_bytes=16 * 1024 * 1024)


def body(
    hidden_in,
    teacher_queries,
    teacher_keys,
    teacher_values,
    doc_lengths,
    dt_weight,
    dt_bias,
    decay_log,
    skip_gain,
    norm_gain,
):
    rows = teacher_queries.shape[1]
    heads = dt_weight.shape[1]
    kv = teacher_keys.shape[2] // HDIM
    width = heads * HDIM
    features = width * lax.axis_size("grp")
    depth = hidden_in.shape[2]
    chips = lax.axis_size("z")
    blocks = 2 * chips
    row_total = lax.axis_size("dp") * rows * blocks
    hidden = hidden_in[0]
    gain = norm_gain[None, :]
    cargo = 2 * kv * HDIM + 3 * heads

    payload, slope, local, sent = pl.pallas_call(
        functools.partial(prep_kernel, kv),
        out_shape=[
            shape((cargo, 128), BF16),
            shape((heads, 128)),
            shape((local_rows(heads, kv)[1], 128), BF16),
            shape((rows, depth // 2), BF16),
        ],
        in_specs=smem(4) + vmem(1) + anywhere(2) + vmem(3),
        out_specs=vmem(2) + anywhere(2),
        scratch_shapes=[
            pltpu.VMEM((const_rows(heads), 128), F32),
            pltpu.VMEM((rows, depth), BF16),
            pltpu.VMEM((rows, width), BF16),
            pltpu.VMEM((local_rows(heads, kv)[1], 128), BF16),
            pltpu.SemaphoreType.DMA((4,)),
            pltpu.SemaphoreType.DMA((3,)),
        ],
        compiler_params=LARGE,
        name="prep",
    )(
        doc_lengths, dt_bias, decay_log, skip_gain, gain, hidden, teacher_queries[0],
        dt_weight.T, teacher_keys[0], teacher_values[0],
    )

    swap = [(0, 1), (1, 0)]
    hop = [(i, (i + 1) % chips) for i in range(chips)]
    run = functools.partial(forward, kv, heads, rows)

    def across(part):
        return lax.ppermute(part, "core", swap)

    hop1 = lax.ppermute(payload, "z", hop)
    sib0 = across(payload)
    hop2 = lax.ppermute(hop1, "z", hop)
    sib1 = across(hop1)
    far = across(sent)
    slope_other = across(slope)
    origin, keep = run(0, [local])
    hop2, origin = lax.optimization_barrier((hop2, origin))
    hop3 = lax.ppermute(hop2, "z", hop)
    sib2 = across(hop2)
    (carry1,) = run(1, [local, sib1, sib0, hop1, origin])
    hop3, carry1, far, slope_other = lax.optimization_barrier((hop3, carry1, far, slope_other))
    hop4 = lax.ppermute(hop3, "z", hop)
    sib3 = across(hop3)
    (carry2,) = run(2, [local, sib2, sib1, hop2, origin, carry1])
    hop4, carry2 = lax.optimization_barrier((hop4, carry2))
    sib4 = across(hop4)
    (carry3,) = run(3, [local, sib3, sib2, hop3, origin, carry1, carry2])
    real, half, stats = run(
        4, [local, sib4, sib3, hop4, origin, carry1, carry2, carry3, keep]
    )
    groups = lax.axis_size("grp")
    all_stats = [stats] + [
        lax.ppermute(stats, "grp", [(i, (i + k) % groups) for i in range(groups)])
        for k in range(1, groups)
    ]

    student, grads, grad_gain, small = pl.pallas_call(
        functools.partial(backward_kernel, kv, heads, len(all_stats), features, row_total),
        out_shape=[
            shape((rows, width), BF16),
            shape((blocks, heads, 128)),
            shape((1, width)),
            shape((8, 128)),
        ],
        in_specs=vmem(5 + len(all_stats)),
        out_specs=vmem(4),
        scratch_shapes=[
            pltpu.VMEM((rows, 128), F32),
            pltpu.VMEM((rows, 128), F32),
            pltpu.VMEM((BACK, heads, 128), F32),
            pltpu.VMEM((heads, 128), F32),
            pltpu.VMEM((heads, 128), F32),
            pltpu.VMEM((heads, 128), F32),
            pltpu.VMEM((128, 128), F32),
        ],
        compiler_params=SMALL,
        name="backward",
    )(local, keep, carry2, real, half, *all_stats)

    grads = lax.all_to_all(grads.reshape(chips, 2 * heads, 128), "z", 0, 0, tiled=True)
    folded = pl.pallas_call(
        fold_kernel,
        out_shape=shape((3 * heads + 8, 128)),
        in_specs=vmem(3),
        out_specs=pl.BlockSpec(memory_space=pltpu.VMEM),
        compiler_params=SMALL,
        name="fold",
    )(grads, grad_gain, small)

    axes = ("z", "dp")
    count = chips * lax.axis_size("dp")
    half = pl.pallas_call(
        weight_kernel,
        out_shape=shape((count * (heads + 2), 128), BF16),
        in_specs=vmem(6),
        out_specs=pl.BlockSpec(memory_space=pltpu.VMEM),
        scratch_shapes=[pltpu.VMEM((count * (heads + 2), 128), F32)],
        compiler_params=SMALL,
        name="weights",
    )(folded, across(folded), slope, slope_other, hidden, far)
    half = half.reshape(count, (heads + 2) // 2, 2, 128)
    got = lax.all_to_all(half, axes, 0, 0, tiled=True)
    spread = pl.pallas_call(
        functools.partial(spread_kernel, count),
        out_shape=shape((count * (heads + 1), 128)),
        in_specs=vmem(1),
        out_specs=pl.BlockSpec(memory_space=pltpu.VMEM),
        scratch_shapes=[pltpu.VMEM((count * (heads + 2), 128), F32)],
        compiler_params=SMALL,
        name="spread",
    )(got.reshape(count * (heads + 2), 128))
    spread = spread.reshape(count, heads + 1, 1, 128)
    mine = lax.all_to_all(spread, axes, 0, 0, tiled=True)
    mine = mine.reshape(count * (heads + 1), 128)
    other = lax.ppermute(mine, "core", swap)
    grad_weight, bias, decay, skip, gained = pl.pallas_call(
        finish_kernel,
        out_shape=[shape((heads, depth))] + [shape((1, heads))] * 3 + [shape((1, width))],
        in_specs=vmem(2),
        out_specs=vmem(5),
        compiler_params=SMALL,
        name="finish",
    )(mine, other)
    return (student[None], grad_weight.T, bias[0], decay[0], skip[0], gained[0])


def solution(mesh):
    sizes = dict(mesh.shape)
    split = jax.sharding.Mesh(
        mesh.devices.reshape(sizes["ctx"] // 2, 2, sizes["grp"], sizes["dp"]),
        ("z", "core", "grp", "dp"),
    )
    ctx = ("z", "core")
    placed = (
        P("dp", ctx, None),
        P("dp", ctx, "grp"),
        P("dp", ctx, "grp"),
        P("dp", ctx, "grp"),
        P("dp", None),
        P(None, "grp"),
        P("grp"),
        P("grp"),
        P("grp"),
        P("grp"),
    )
    return jax.shard_map(
        body,
        mesh=split,
        in_specs=placed,
        out_specs=(P("dp", ctx, "grp"), P(None, "grp"), P("grp"), P("grp"), P("grp"), P("grp")),
        check_vma=False,
    )
```

```python
import functools
import math

import jax
import jax.numpy as jnp
from jax import lax
from jax.experimental import pallas as pl
from jax.experimental.pallas import tpu as pltpu
from jax.sharding import PartitionSpec as P

HDIM = 128
EPSILON = 1e-05
BACK = 8
NEG = -1e30
LOG2E = math.log2(math.e)
F32 = jnp.float32
BF16 = jnp.bfloat16


def mm(a, b):
    return jnp.dot(a, b, preferred_element_type=F32)


def two_parts(x):
    high = x.astype(BF16)
    return high, (x - high.astype(F32)).astype(BF16)


def mm_two(a, b):
    rows = a.shape[0]
    both = mm(jnp.concatenate(two_parts(a), axis=0), b)
    return both[:rows] + both[rows:]


def mm_apart(a, b):
    high, low = two_parts(a)
    return mm(high, b) + mm(low, b)


def mm_right(a, b):
    high, low = two_parts(b)
    return mm(a, high) + mm(a, low)


def iota(shape, dim):
    return lax.broadcasted_iota(jnp.int32, shape, dim)


def to_row(x):
    rows = x.shape[0]
    if rows < 128:
        x = jnp.concatenate([x, jnp.zeros((128 - rows, x.shape[1]), F32)], axis=0)
    return jnp.sum(x.T, axis=0, keepdims=True)


def column_of(values, rows):
    row = iota((rows, 128), 0)
    out = jnp.zeros((rows, 128), F32)
    for h in range(rows):
        out = jnp.where(row == h, values[h], out)
    return out


def place_of(consts, rows):
    core = lax.axis_index("core")
    place = lax.axis_index("z") * lax.axis_size("core") + core
    starts = [consts[i : i + 1, :].astype(jnp.int32) for i in range(3)]
    return (place * rows, *starts, core, place)


def segment_at(pos, info):
    return (
        (pos >= info[1]).astype(jnp.int32)
        + (pos >= info[2]).astype(jnp.int32)
        + (pos >= info[3]).astype(jnp.int32)
    )


def prep_kernel(
    kv,
    lengths,
    bias,
    decay,
    skip,
    gain,
    hidden,
    weight,
    keys,
    values,
    queries,
    payload,
    slope,
    local,
    consts,
):
    heads = weight.shape[0]
    pre = (
        lax.dot_general(
            hidden[...], weight[...], (((1,), (1,)), ((), ())), preferred_element_type=F32
        ).T
        + column_of(bias, heads)
    )
    step = jnp.maximum(pre, 0.0) + jnp.log1p(jnp.exp(-jnp.abs(pre)))
    slope[...] = 1.0 / (1.0 + jnp.exp(-pre))
    for g in range(kv):
        cols = slice(g * HDIM, (g + 1) * HDIM)
        payload[g * HDIM : (g + 1) * HDIM, :] = keys[:, cols].astype(F32).T.astype(BF16)
        payload[(kv + g) * HDIM : (kv + g + 1) * HDIM, :] = values[:, cols]
    consts[0:heads, :] = jnp.exp(column_of(decay, heads))
    consts[heads : 2 * heads, :] = column_of(skip, heads)
    for h in range(heads):
        consts[2 * heads + h : 2 * heads + h + 1, :] = gain[:, h * HDIM : (h + 1) * HDIM]
    one = lengths[0, 0]
    two = one + lengths[0, 1]
    starts = (one, two, two + lengths[0, 2], 0, 0, 0, 0, 0)
    row = iota((8, 128), 0)
    marks = jnp.zeros((8, 128), jnp.int32)
    for i in range(3):
        marks = jnp.where(row == i, starts[i], marks)
    consts[3 * heads : 3 * heads + 8, :] = marks.astype(F32)
    consts[3 * heads + 8 :, :] = jnp.zeros((consts.shape[0] - 3 * heads - 8, 128), F32)
    first = 2 * kv * HDIM
    for part in range(3):
        piece = step.astype(BF16)
        payload[first + part * heads : first + (part + 1) * heads, :] = piece
        step = step - piece.astype(F32)
    at = local_rows(heads, kv)[0]
    for h in range(heads):
        local[at[0] + 128 * h : at[0] + 128 * h + 128, :] = queries[:, 128 * h : 128 * h + 128]
    local[at[1] : at[1] + payload.shape[0], :] = payload[...]
    rest = consts[...]
    for part in range(3):
        piece = rest.astype(BF16)
        local[at[2 + part] : at[2 + part] + rest.shape[0], :] = piece
        rest = rest - piece.astype(F32)


def masks(info):
    first = info[0]
    before = jnp.where(
        first > 0, segment_at(jnp.maximum(first - 1, 0) + iota((1, 128), 1) * 0, info), -1
    )
    row_pos = first + iota((128, 128), 0)
    col_pos = first + iota((128, 128), 1)
    row_seg = segment_at(row_pos, info)
    allowed = (row_seg == segment_at(col_pos, info)) & (col_pos <= row_pos)
    carried = row_seg == before
    return first, before, allowed, carried


def match_row(info, first, before, d, rows):
    pos = first - 128 * d + iota((rows, 128), 1)
    return (segment_at(pos, info) == before) & (pos >= 0)


PARTS = ((0,), (1, 2), (3, 4), (5, 6), (7, 8))


def layout(*sizes):
    starts, total = [], 0
    for size in sizes:
        starts.append(total)
        total += -(-size // 128) * 128
    return starts, total


def carry_rows(heads, kv, part):
    count = len(PARTS[part])
    wide = heads * 128
    if part == 0:
        return layout(wide, wide, wide, 0, heads * 3, const_rows(heads), 0, 0)
    turned = kv * count * 128
    return layout(
        wide, wide, wide, wide, heads * (2 + 2 * count), 0, turned, turned, wide if part == 2 else 0
    )


def const_rows(heads):
    return -(-(3 * heads + 8) // 16) * 16


def local_rows(heads, kv):
    size = const_rows(heads)
    cargo = 2 * kv * HDIM + 3 * heads
    starts, total = [], 0
    for rows in (heads * 128, cargo, size, size, size):
        starts.append(total)
        total += rows
    return starts, total


def keep_rows(heads, kv):
    return layout(heads * 128, heads * 128, kv * 128, kv * 128, kv * 128)


def real_rows(heads, kv):
    count = BACK + 1
    wide = heads * 128
    return layout(
        wide, wide, 0, const_rows(heads), count * heads, BACK * heads, kv * count * 128
    )


def half_rows(heads, kv):
    return layout(heads * 128, kv * (BACK + 1) * 128)


def slab(start, h):
    return pl.ds(pl.multiple_of(start + h * 128, 128), 128)


def forward_kernel(kv, heads, part, *refs):
    refs = list(refs)

    def take(count):
        out = refs[:count]
        del refs[:count]
        return out

    first, last = part == 0, part == len(PARTS) - 1
    blocks = PARTS[part]
    local = take(1)[0]
    local_at = local_rows(heads, kv)[0]
    if first:
        sources = [[local]]
        carry, keep = take(2)
        cum_ref, value_ref, consts = refs[-3:]
        total = jnp.zeros(consts.shape, F32)
        for i in range(3):
            total += local[local_at[2 + i] : local_at[2 + i] + consts.shape[0], :].astype(F32)
        consts[...] = total
    else:
        sources = [take(1 if d % 2 == 0 else 2) for d in blocks]
        origin = take(1)[0]
        carries = [origin] + take(part - 1)
        before_carry = carries[-1]
        before_at = carry_rows(heads, kv, part - 1)[0]
    if last:
        keep, real, half, stats = take(4)
        acc = refs[-1]
        acc[...] = jnp.zeros_like(acc)
    elif not first:
        carry = take(1)[0]
    kt, vv, bias, step_ref = take(4)
    if not first:
        key32, fade_ref = take(2)
    origin_at = carry_rows(heads, kv, 0)[0]
    keep_at = keep_rows(heads, kv)[0]
    real_at = real_rows(heads, kv)[0]
    half_at = half_rows(heads, kv)[0]
    carry_at = carry_rows(heads, kv, part)[0]
    if first:
        constant, base = consts, 0
        carry[carry_at[5] : carry_at[5] + consts.shape[0], :] = consts[...]
    else:
        constant, base = origin, origin_at[5]
    cum_at = origin_at[4] + heads
    enter_at = carry_rows(heads, kv, 2)[0][8]
    group = heads // kv
    size = 3 * heads + 8
    info = place_of(constant[base + size - 8 : base + size, :], 128)
    even_core = info[4] == 0
    start, before, allowed, carried = masks(info)

    reach = (iota((128, 128), 0) <= iota((128, 128), 1)).astype(BF16)
    if first:
        after = jnp.zeros((heads, 128), F32)
    else:
        after = before_carry[before_at[4] : before_at[4] + heads, :]
    rate = constant[base : base + heads, :]
    for i, d in enumerate(blocks):
        at = slice(128 * i, 128 * i + 128)
        near = sources[i]

        def piece(low, high):
            if first:
                return near[0][local_at[1] + low : local_at[1] + high, :]
            if d % 2 == 0:
                return near[0][low:high, :]
            return jnp.where(even_core, near[0][low:high, :], near[1][low:high, :])

        for g in range(kv):
            block = piece(g * HDIM, (g + 1) * HDIM)
            value = piece((kv + g) * HDIM, (kv + g + 1) * HDIM)
            kt[g, :, at] = block
            vv[g, at, :] = value
            block, value = block.astype(F32), value.astype(F32)
            if last:
                row = (g * (BACK + 1) + d) * 128
                half[half_at[1] + row : half_at[1] + row + 128, :] = kt[g, :, at]
                real[real_at[6] + row : real_at[6] + row + 128, :] = value.T
            else:
                row = (g * len(blocks) + i) * 128
                out, where = (keep, keep_at[3:5]) if first else (carry, carry_at[6:8])
                out[where[0] + row : where[0] + row + 128, :] = block
                out[where[1] + row : where[1] + row + 128, :] = value.T
            if first:
                keep[keep_at[2] + 128 * g : keep_at[2] + 128 * g + 128, :] = value
                value_ref[g] = value
            else:
                key32[g, :, at] = block
        first_step = 2 * kv * HDIM
        parts = [piece(first_step + k * heads, first_step + (k + 1) * heads) for k in range(3)]
        step = parts[0].astype(F32) + parts[1].astype(F32) + parts[2].astype(F32)
        sums = mm(parts[0], reach) + mm(parts[1], reach) + mm(parts[2], reach)
        step_ref[i] = step
        if first:
            carry[cum_at : cum_at + heads, :] = sums
            cum_ref[...] = sums
            bias[:, at] = jnp.where(allowed, 0.0, NEG)
        else:
            total = jnp.broadcast_to(sums[:, 127:128], (heads, 128))
            left = jnp.maximum(total - sums, 0.0) + after
            found = match_row(info, start, before, d, heads)
            fade_ref[i] = jnp.where(found, jnp.exp(-rate * left), 0.0)
            after = after + total
            both = carried & match_row(info, start, before, d, 128)
            bias[:, at] = jnp.where(both, 0.0, NEG)
    if last:
        real[real_at[3] : real_at[3] + size, :] = origin[base : base + size, :]
        for p, source in enumerate(carries):
            where = carry_rows(heads, kv, p)[0]
            count = len(PARTS[p])
            low = where[4] + heads * 2
            rows = heads * count
            to = real_at[4] + heads * PARTS[p][0]
            real[to : to + rows, :] = source[low : low + rows, :]
            if p > 0:
                low = low + rows
                to = real_at[5] + heads * (PARTS[p][0] - 1)
                real[to : to + rows, :] = source[low : low + rows, :]
            turned, where = (keep, keep_at[3:5]) if p == 0 else (source, where[6:8])
            for g in range(kv):
                rows = 128 * count
                low = g * rows
                to = (g * (BACK + 1) + PARTS[p][0]) * 128
                half[half_at[1] + to : half_at[1] + to + rows, :] = turned[
                    where[0] + low : where[0] + low + rows, :
                ].astype(BF16)
                real[real_at[6] + to : real_at[6] + to + rows, :] = turned[
                    where[1] + low : where[1] + low + rows, :
                ]
        small, step_at = real, real_at[4] + heads * blocks[0]
        fade_at = real_at[5] + heads * (blocks[0] - 1)
    else:
        small, step_at = carry, carry_at[4] + heads * 2
        fade_at = step_at + heads * len(blocks)
        carry[carry_at[4] : carry_at[4] + heads, :] = after
    for i in range(len(blocks)):
        small[step_at + heads * i : step_at + heads * (i + 1), :] = step_ref[i]
        if not first:
            small[fade_at + heads * i : fade_at + heads * (i + 1), :] = fade_ref[i]

    def rate_of(h):
        return constant[pl.ds(base + h, 1), :]

    def one_head(h, unused):
        g = h // group
        query = local[slab(local_at[0], h), :]
        scores = mm(query, kt[g])
        scaled = scores * (LOG2E / math.sqrt(HDIM)) + bias[...]
        top = jnp.broadcast_to(jnp.max(scaled, axis=1, keepdims=True), (128, 128))
        if not first:
            old = before_carry[slab(before_at[0], h), :]
            top = jnp.maximum(old, top)
        weights = [
            jnp.exp2(scaled[:, 128 * i : 128 * i + 128] - top) for i in range(len(blocks))
        ]
        total = weights[0]
        for other in weights[1:]:
            total = total + other
        total = jnp.broadcast_to(jnp.sum(total, axis=1, keepdims=True), (128, 128))
        weights = jnp.concatenate([w.astype(BF16) for w in weights], axis=1)
        if not first:
            weight_row = jnp.concatenate(
                [
                    fade_ref[i, pl.ds(h, 1), :] * step_ref[i, pl.ds(h, 1), :]
                    for i in range(len(blocks))
                ],
                axis=1,
            )
            mixed = mm(weights, vv[g])
            state = mm_apart(key32[g] * weight_row, vv[g])
            scale = jnp.exp2(old - top)
            total = total + before_carry[slab(before_at[1], h), :] * scale
            mixed = mixed + before_carry[slab(before_at[2], h), :] * scale
            if part > 1:
                state = state + before_carry[slab(before_at[3], h), :]
        else:
            decay_row = rate_of(h)
            cum_row = jnp.broadcast_to(cum_ref[pl.ds(h, 1), :], (128, 128))
            cum_col = cum_row.T
            decay = jnp.where(
                allowed, jnp.exp(-decay_row * jnp.maximum(cum_col - cum_row, 0.0)), 0.0
            )
            decayed = scores[:, :128] * decay
            keep[slab(keep_at[1], h), :] = decayed
            skipped = constant[pl.ds(base + heads + h, 1), :] * value_ref[g]
            high, low = two_parts(decayed * step_ref[0, pl.ds(h, 1), :])
            joined = mm(jnp.concatenate([weights, high, low], axis=0), vv[g])
            mixed = joined[:128]
            keep[slab(keep_at[0], h), :] = joined[128:256] + joined[256:] + skipped
        if not last:
            carry[slab(carry_at[0], h), :] = top
            carry[slab(carry_at[1], h), :] = total
            carry[slab(carry_at[2], h), :] = mixed
            if not first:
                carry[slab(carry_at[3], h), :] = state
        if part == 2:
            cum_col = jnp.broadcast_to(origin[pl.ds(cum_at + h, 1), :], (128, 128)).T
            carry[slab(enter_at, h), :] = jnp.where(
                carried, jnp.exp(-rate_of(h) * cum_col), 0.0
            )
        if last:
            teach = (mixed / total).astype(BF16)
            half[slab(half_at[0], h), :] = teach
            off = mm_right(query, state) * carries[2][slab(enter_at, h), :]
            raw = keep[slab(keep_at[0], h), :] + off
            real[slab(real_at[0], h), :] = raw
            real[slab(real_at[1], h), :] = off
            gained = raw * constant[pl.ds(base + 2 * heads + h, 1), :]
            acc[0] += raw * raw
            acc[1] += gained * gained
            acc[2] += gained * teach.astype(F32)
        return unused

    lax.fori_loop(0, heads, one_head, 0, unroll=(16, 8, 8, 16, 16)[part])
    if last:
        stats[...] = jnp.concatenate(
            [to_row(acc[0]), to_row(acc[1]), to_row(acc[2]), jnp.zeros((5, 128), F32)], axis=0
        )


def forward(kv, heads, rows, part, operands):
    blocks = PARTS[part]
    first, last = part == 0, part == len(PARTS) - 1
    wide = 128 * len(blocks)
    if last:
        outs = [
            shape((real_rows(heads, kv)[1], 128)),
            shape((half_rows(heads, kv)[1], 128), BF16),
            shape((8, 128)),
        ]
    else:
        outs = [shape((carry_rows(heads, kv, part)[1], 128))]
    if first:
        outs.append(shape((keep_rows(heads, kv)[1], 128)))
    scratch = [
        pltpu.VMEM((kv, HDIM, wide), BF16),
        pltpu.VMEM((kv, wide, HDIM), BF16),
        pltpu.VMEM((rows, wide), F32),
        pltpu.VMEM((len(blocks), heads, 128), F32),
    ]
    if first:
        scratch += [
            pltpu.VMEM((heads, 128), F32),
            pltpu.VMEM((kv, rows, HDIM), F32),
            pltpu.VMEM((const_rows(heads), 128), F32),
        ]
    else:
        scratch += [
            pltpu.VMEM((kv, HDIM, wide), F32),
            pltpu.VMEM((len(blocks), heads, 128), F32),
        ]
    if last:
        scratch.append(pltpu.VMEM((3, rows, HDIM), F32))
    return pl.pallas_call(
        functools.partial(forward_kernel, kv, heads, part),
        out_shape=outs,
        in_specs=vmem(len(operands)),
        out_specs=vmem(len(outs)),
        scratch_shapes=scratch,
        compiler_params=SMALL,
        cost_estimate=pl.CostEstimate(
            flops=len(blocks) * heads * rows * 128 * 128 * 12,
            bytes_accessed=len(blocks) * 3 * 1024 * 1024,
            transcendentals=2 * heads * rows * wide,
        ),
        name="forward_" + "abcde"[part],
    )(*operands)


def backward_kernel(kv, heads, groups, features, row_total, *refs):
    local, keep, enter, real, half, *refs = refs
    stats = refs[0][...]
    for other in refs[1:groups]:
        stats = stats + other[...]
    student_out, grads, gain_out, small_out, *refs = refs[groups:]
    inv_col, coef_col, late, skip_rows, direct_rows, minus_rows, row_sums = refs
    keep_at = keep_rows(heads, kv)[0]
    real_at = real_rows(heads, kv)[0]
    half_at = half_rows(heads, kv)[0]
    group = heads // kv
    enter_at = carry_rows(heads, kv, 2)[0][8]
    size = 3 * heads + 8
    base = real_at[3]
    info = place_of(real[base + size - 8 : base + size, :], 128)
    place, count = info[5], grads.shape[0]
    grads[...] = jnp.zeros_like(grads)
    row_sums[...] = jnp.zeros_like(row_sums)
    share = 2.0 / row_total
    squares, gained_squares, crossed = stats[0:1, :], stats[1:2, :], stats[2:3, :]
    inverse = lax.rsqrt(squares / features + EPSILON)
    inner = share * (inverse * gained_squares - crossed)
    coef = inverse * inverse * inverse * inner / features
    inv_col[...] = jnp.broadcast_to(inverse, (128, 128)).T
    coef_col[...] = jnp.broadcast_to(coef, (128, 128)).T
    row_i, col_i = iota((128, 128), 0), iota((128, 128), 1)
    later = (row_i >= col_i).astype(BF16)
    strict = (row_i < col_i).astype(BF16)

    def one_head(h, unused):
        g = h // group
        cols = slab(0, h)
        query = local[slab(0, h), :]
        raw, off = real[slab(real_at[0], h), :], real[slab(real_at[1], h), :]
        scale = real[pl.ds(base + 2 * heads + h, 1), :]
        inv = inv_col[...]
        normed = raw * inv * scale
        student_out[:, cols] = normed.astype(BF16)
        grad_normed = (normed - half[slab(half_at[0], h), :].astype(F32)) * share
        gain_out[:, cols] = jnp.sum(grad_normed * raw * inv, axis=0, keepdims=True)
        grad = inv * grad_normed * scale - raw * coef_col[...]
        value = keep[slab(keep_at[2], g), :]
        skip_rows[pl.ds(h, 1), :] = jnp.sum(grad * value, axis=0, keepdims=True)
        entering = enter[slab(enter_at, h), :]
        grad_state = mm_two((grad * entering).T, query)
        turned = [slab(g * ((BACK + 1) * 128), d) for d in range(BACK + 1)]
        keys = jnp.concatenate(
            [half[pl.ds(half_at[1] + turned[d].start, 128), :] for d in range(1, BACK + 1)],
            axis=1,
        )
        reached = mm_two(grad_state, keys)
        for d in range(1, BACK + 1):
            values = real[pl.ds(real_at[6] + turned[d].start, 128), :]
            late[d - 1, pl.ds(h, 1), :] = jnp.sum(
                reached[:, 128 * d - 128 : 128 * d] * values, axis=0, keepdims=True
            )
        own_values = real[pl.ds(real_at[6] + turned[0].start, 128), :].astype(BF16)
        pulled = mm_two(grad, own_values)
        pairs = keep[slab(keep_at[1], h), :] * pulled
        direct_rows[pl.ds(h, 1), :] = jnp.sum(pairs, axis=0, keepdims=True)
        pairs = jnp.where(
            row_i > col_i, pairs * real[pl.ds(real_at[4] + h, 1), :], 0.0
        )
        minus_rows[pl.ds(h, 1), :] = jnp.sum(pairs, axis=0, keepdims=True)
        sums = jnp.sum(pairs + grad * off, axis=1, keepdims=True)
        row_sums[...] += jnp.where(col_i == h, jnp.broadcast_to(sums, (128, 128)), 0.0)
        return unused

    lax.fori_loop(0, heads, one_head, 0, unroll=16)

    def summed(x, triangle):
        high, low = two_parts(x)
        rest = (x - high.astype(F32) - low.astype(F32)).astype(BF16)
        return mm(high, triangle) + mm(low, triangle) + mm(rest, triangle)

    rate = real[base : base + heads, :]
    spanned = summed(row_sums[...].T[:heads, :] - minus_rows[...], later)
    grads[place] = direct_rows[...] - rate * spanned
    rate_rows = spanned * real[real_at[4] : real_at[4] + heads, :]
    earlier = jnp.zeros((heads, 128), F32)
    for d in range(BACK, 0, -1):
        step = real[real_at[4] + heads * d : real_at[4] + heads * (d + 1), :]
        fade = real[real_at[5] + heads * (d - 1) : real_at[5] + heads * d, :]
        direct = late[d - 1] * fade
        whole = direct * step
        spanned = summed(whole, strict) + earlier
        grads[lax.rem(place - d + count, count)] = direct - rate * spanned
        rate_rows = rate_rows + spanned * step
        earlier = earlier + jnp.sum(whole, axis=1, keepdims=True)
    small_out[...] = jnp.concatenate(
        [to_row(skip_rows[...]), -to_row(rate_rows * rate), jnp.zeros((6, 128), F32)], axis=0
    )


def fold_kernel(grads, gain, small, out):
    total = jnp.sum(grads[...], axis=0)
    rows = total.shape[0]
    tiles = gain.shape[1] // 128
    out[0:rows, :] = total
    for i in range(tiles):
        out[rows + i : rows + i + 1, :] = gain[:, 128 * i : 128 * i + 128]
    out[rows + tiles : rows + tiles + 8, :] = small[...]


def weight_kernel(own, other, slope, slope_other, hidden, far, out, wide):
    heads = slope.shape[0]
    total = own[...] + other[...]
    core = lax.axis_index("core")
    low_core = core == 0
    near_slope, far_slope = slope[...], slope_other[...]
    top, bottom = total[0:heads], total[heads : 2 * heads]
    near_pre = jnp.where(low_core, top, bottom) * near_slope
    far_pre = jnp.where(low_core, bottom, top) * far_slope
    near_low, far_low = near_pre.astype(BF16), far_pre.astype(BF16)
    side = far.shape[1] // 2
    count = side // 128
    tiles = total.shape[0] - 2 * heads - 8
    lines = [total[2 * heads + i : 2 * heads + i + 1] for i in range(tiles)]
    lines.append(to_row(near_pre + far_pre))
    base = 2 * heads + tiles
    lines += [total[base + 1 : base + 2], total[base : base + 1]]
    for j in range(count):
        start = j * (heads + 2)
        cols = pl.ds(pl.multiple_of(core * side + 128 * j, 128), 128)
        wide[start : start + heads, :] = mm(near_low, hidden[:, cols]) + mm(
            far_low, far[:, cols]
        )
        line = jnp.zeros((1, 128), F32)
        if j < len(lines):
            line = jnp.where(low_core, lines[j], line)
        high = line.astype(BF16).astype(F32)
        wide[start + heads : start + heads + 1, :] = high
        wide[start + heads + 1 : start + heads + 2, :] = line - high
    out[...] = wide[...].astype(BF16)


def spread_kernel(count, got, out, wide):
    wide[...] = got[...].astype(F32)
    each = wide.shape[0] // count
    total = wide[0:each, :]
    for j in range(1, count):
        total = total + wide[each * j : each * (j + 1), :]
    small = total[each - 2 : each - 1, :] + total[each - 1 : each, :]
    for j in range(count):
        start = (each - 1) * j
        out[start : start + each - 2, :] = total[: each - 2, :]
        out[start + each - 2 : start + each - 1, :] = small


def finish_kernel(mine, other, weight, bias, decay, skip, gain):
    heads = weight.shape[0]
    count = mine.shape[0] // (heads + 1)
    tiles = gain.shape[1] // 128
    core = lax.axis_index("core")

    def place(source, half):
        for j in range(count):
            i = half * count + j
            start = j * (heads + 1)
            weight[:, 128 * i : 128 * i + 128] = source[start : start + heads, :]
            row = source[start + heads : start + heads + 1, :]
            if i < tiles:
                gain[:, 128 * i : 128 * i + 128] = row
            if i == tiles:
                bias[...] = row[:, :heads]
            if i == tiles + 1:
                decay[...] = row[:, :heads]
            if i == tiles + 2:
                skip[...] = row[:, :heads]

    for half in range(2):

        @pl.when(core == half)
        def _():
            place(mine, half)
            place(other, 1 - half)


def vmem(count):
    return [pl.BlockSpec(memory_space=pltpu.VMEM)] * count


def smem(count):
    return [pl.BlockSpec(memory_space=pltpu.SMEM)] * count


def shape(dims, kind=F32):
    return jax.ShapeDtypeStruct(dims, kind)


LARGE = pltpu.CompilerParams(vmem_limit_bytes=56 * 1024 * 1024)
SMALL = pltpu.CompilerParams(vmem_limit_bytes=16 * 1024 * 1024)


def body(
    hidden_in,
    teacher_queries,
    teacher_keys,
    teacher_values,
    doc_lengths,
    dt_weight,
    dt_bias,
    decay_log,
    skip_gain,
    norm_gain,
):
    rows = teacher_queries.shape[1]
    heads = dt_weight.shape[1]
    kv = teacher_keys.shape[2] // HDIM
    width = heads * HDIM
    features = width * lax.axis_size("grp")
    depth = hidden_in.shape[2]
    chips = lax.axis_size("z")
    blocks = 2 * chips
    row_total = lax.axis_size("dp") * rows * blocks
    hidden = hidden_in[0]
    gain = norm_gain[None, :]
    cargo = 2 * kv * HDIM + 3 * heads

    payload, slope, local = pl.pallas_call(
        functools.partial(prep_kernel, kv),
        out_shape=[
            shape((cargo, 128), BF16),
            shape((heads, 128)),
            shape((local_rows(heads, kv)[1], 128), BF16),
        ],
        in_specs=smem(4) + vmem(6),
        out_specs=vmem(3),
        scratch_shapes=[pltpu.VMEM((const_rows(heads), 128), F32)],
        compiler_params=LARGE,
        name="prep",
    )(
        doc_lengths, dt_bias, decay_log, skip_gain, gain, hidden, dt_weight.T,
        teacher_keys[0], teacher_values[0], teacher_queries[0],
    )

    swap = [(0, 1), (1, 0)]
    hop = [(i, (i + 1) % chips) for i in range(chips)]
    run = functools.partial(forward, kv, heads, rows)

    def across(part):
        return lax.ppermute(part, "core", swap)

    hop1 = lax.ppermute(payload, "z", hop)
    sib0 = across(payload)
    hop2 = lax.ppermute(hop1, "z", hop)
    sib1 = across(hop1)
    far = across(hidden)
    slope_other = across(slope)
    origin, keep = run(0, [local])
    hop2, origin = lax.optimization_barrier((hop2, origin))
    hop3 = lax.ppermute(hop2, "z", hop)
    sib2 = across(hop2)
    (carry1,) = run(1, [local, sib1, sib0, hop1, origin])
    hop3, carry1, far, slope_other = lax.optimization_barrier((hop3, carry1, far, slope_other))
    hop4 = lax.ppermute(hop3, "z", hop)
    sib3 = across(hop3)
    (carry2,) = run(2, [local, sib2, sib1, hop2, origin, carry1])
    hop4, carry2 = lax.optimization_barrier((hop4, carry2))
    sib4 = across(hop4)
    (carry3,) = run(3, [local, sib3, sib2, hop3, origin, carry1, carry2])
    real, half, stats = run(
        4, [local, sib4, sib3, hop4, origin, carry1, carry2, carry3, keep]
    )
    groups = lax.axis_size("grp")
    all_stats = [stats] + [
        lax.ppermute(stats, "grp", [(i, (i + k) % groups) for i in range(groups)])
        for k in range(1, groups)
    ]

    student, grads, grad_gain, small = pl.pallas_call(
        functools.partial(backward_kernel, kv, heads, len(all_stats), features, row_total),
        out_shape=[
            shape((rows, width), BF16),
            shape((blocks, heads, 128)),
            shape((1, width)),
            shape((8, 128)),
        ],
        in_specs=vmem(5 + len(all_stats)),
        out_specs=vmem(4),
        scratch_shapes=[
            pltpu.VMEM((rows, 128), F32),
            pltpu.VMEM((rows, 128), F32),
            pltpu.VMEM((BACK, heads, 128), F32),
            pltpu.VMEM((heads, 128), F32),
            pltpu.VMEM((heads, 128), F32),
            pltpu.VMEM((heads, 128), F32),
            pltpu.VMEM((128, 128), F32),
        ],
        compiler_params=SMALL,
        name="backward",
    )(local, keep, carry2, real, half, *all_stats)

    grads = lax.all_to_all(grads.reshape(chips, 2 * heads, 128), "z", 0, 0, tiled=True)
    folded = pl.pallas_call(
        fold_kernel,
        out_shape=shape((3 * heads + 8, 128)),
        in_specs=vmem(3),
        out_specs=pl.BlockSpec(memory_space=pltpu.VMEM),
        compiler_params=SMALL,
        name="fold",
    )(grads, grad_gain, small)

    axes = ("z", "dp")
    count = chips * lax.axis_size("dp")
    half = pl.pallas_call(
        weight_kernel,
        out_shape=shape((count * (heads + 2), 128), BF16),
        in_specs=vmem(6),
        out_specs=pl.BlockSpec(memory_space=pltpu.VMEM),
        scratch_shapes=[pltpu.VMEM((count * (heads + 2), 128), F32)],
        compiler_params=SMALL,
        name="weights",
    )(folded, across(folded), slope, slope_other, hidden, far)
    half = half.reshape(count, (heads + 2) // 2, 2, 128)
    got = lax.all_to_all(half, axes, 0, 0, tiled=True)
    spread = pl.pallas_call(
        functools.partial(spread_kernel, count),
        out_shape=shape((count * (heads + 1), 128)),
        in_specs=vmem(1),
        out_specs=pl.BlockSpec(memory_space=pltpu.VMEM),
        scratch_shapes=[pltpu.VMEM((count * (heads + 2), 128), F32)],
        compiler_params=SMALL,
        name="spread",
    )(got.reshape(count * (heads + 2), 128))
    spread = spread.reshape(count, heads + 1, 1, 128)
    mine = lax.all_to_all(spread, axes, 0, 0, tiled=True)
    mine = mine.reshape(count * (heads + 1), 128)
    other = lax.ppermute(mine, "core", swap)
    grad_weight, bias, decay, skip, gained = pl.pallas_call(
        finish_kernel,
        out_shape=[shape((heads, depth))] + [shape((1, heads))] * 3 + [shape((1, width))],
        in_specs=vmem(2),
        out_specs=vmem(5),
        compiler_params=SMALL,
        name="finish",
    )(mine, other)
    return (student[None], grad_weight.T, bias[0], decay[0], skip[0], gained[0])


def solution(mesh):
    sizes = dict(mesh.shape)
    split = jax.sharding.Mesh(
        mesh.devices.reshape(sizes["ctx"] // 2, 2, sizes["grp"], sizes["dp"]),
        ("z", "core", "grp", "dp"),
    )
    ctx = ("z", "core")
    placed = (
        P("dp", ctx, None),
        P("dp", ctx, "grp"),
        P("dp", ctx, "grp"),
        P("dp", ctx, "grp"),
        P("dp", None),
        P(None, "grp"),
        P("grp"),
        P("grp"),
        P("grp"),
        P("grp"),
    )
    return jax.shard_map(
        body,
        mesh=split,
        in_specs=placed,
        out_specs=(P("dp", ctx, "grp"), P(None, "grp"), P("grp"), P("grp"), P("grp"), P("grp")),
        check_vma=False,
    )
```

```python
import functools
import math

import jax
import jax.numpy as jnp
from jax import lax
from jax.experimental import pallas as pl
from jax.experimental.pallas import tpu as pltpu
from jax.sharding import PartitionSpec as P

HDIM = 128
EPSILON = 1e-05
BACK = 8
NEG = -1e30
LOG2E = math.log2(math.e)
F32 = jnp.float32
BF16 = jnp.bfloat16


def mm(a, b):
    return jnp.dot(a, b, preferred_element_type=F32)


def two_parts(x):
    high = x.astype(BF16)
    return high, (x - high.astype(F32)).astype(BF16)


def mm_two(a, b):
    rows = a.shape[0]
    both = mm(jnp.concatenate(two_parts(a), axis=0), b)
    return both[:rows] + both[rows:]


def mm_apart(a, b):
    high, low = two_parts(a)
    return mm(high, b) + mm(low, b)


def mm_right(a, b):
    high, low = two_parts(b)
    return mm(a, high) + mm(a, low)


def iota(shape, dim):
    return lax.broadcasted_iota(jnp.int32, shape, dim)


def to_row(x):
    rows = x.shape[0]
    if rows < 128:
        x = jnp.concatenate([x, jnp.zeros((128 - rows, x.shape[1]), F32)], axis=0)
    return jnp.sum(x.T, axis=0, keepdims=True)


def column_of(values, rows):
    row = iota((rows, 128), 0)
    out = jnp.zeros((rows, 128), F32)
    for h in range(rows):
        out = jnp.where(row == h, values[h], out)
    return out


def place_of(consts, rows):
    core = lax.axis_index("core")
    place = lax.axis_index("z") * lax.axis_size("core") + core
    starts = [consts[i : i + 1, :].astype(jnp.int32) for i in range(3)]
    return (place * rows, *starts, core, place)


def segment_at(pos, info):
    return (
        (pos >= info[1]).astype(jnp.int32)
        + (pos >= info[2]).astype(jnp.int32)
        + (pos >= info[3]).astype(jnp.int32)
    )


def prep_kernel(
    kv,
    lengths,
    bias,
    decay,
    skip,
    gain,
    hidden,
    weight,
    keys,
    values,
    payload,
    slope,
    consts,
):
    heads = weight.shape[0]
    pre = (
        lax.dot_general(
            hidden[...], weight[...], (((1,), (1,)), ((), ())), preferred_element_type=F32
        ).T
        + column_of(bias, heads)
    )
    step = jnp.maximum(pre, 0.0) + jnp.log1p(jnp.exp(-jnp.abs(pre)))
    slope[...] = 1.0 / (1.0 + jnp.exp(-pre))
    for g in range(kv):
        cols = slice(g * HDIM, (g + 1) * HDIM)
        payload[g * HDIM : (g + 1) * HDIM, :] = keys[:, cols].astype(F32).T.astype(BF16)
        payload[(kv + g) * HDIM : (kv + g + 1) * HDIM, :] = values[:, cols]
    consts[0:heads, :] = jnp.exp(column_of(decay, heads))
    consts[heads : 2 * heads, :] = column_of(skip, heads)
    for h in range(heads):
        consts[2 * heads + h : 2 * heads + h + 1, :] = gain[:, h * HDIM : (h + 1) * HDIM]
    one = lengths[0, 0]
    two = one + lengths[0, 1]
    starts = (one, two, two + lengths[0, 2], 0, 0, 0, 0, 0)
    row = iota((8, 128), 0)
    marks = jnp.zeros((8, 128), jnp.int32)
    for i in range(3):
        marks = jnp.where(row == i, starts[i], marks)
    consts[3 * heads : 3 * heads + 8, :] = marks.astype(F32)
    consts[3 * heads + 8 :, :] = jnp.zeros((consts.shape[0] - 3 * heads - 8, 128), F32)
    first = 2 * kv * HDIM
    for part in range(3):
        piece = step.astype(BF16)
        payload[first + part * heads : first + (part + 1) * heads, :] = piece
        step = step - piece.astype(F32)


def pack_kernel(kv, queries, payload, consts, local):
    heads = queries.shape[1] // 128
    at = local_rows(heads, kv)[0]
    for h in range(heads):
        local[at[0] + 128 * h : at[0] + 128 * h + 128, :] = queries[:, 128 * h : 128 * h + 128]
    local[at[1] : at[1] + payload.shape[0], :] = payload[...]
    rest = consts[...]
    for part in range(3):
        piece = rest.astype(BF16)
        local[at[2 + part] : at[2 + part] + rest.shape[0], :] = piece
        rest = rest - piece.astype(F32)


def masks(info):
    first = info[0]
    before = jnp.where(
        first > 0, segment_at(jnp.maximum(first - 1, 0) + iota((1, 128), 1) * 0, info), -1
    )
    row_pos = first + iota((128, 128), 0)
    col_pos = first + iota((128, 128), 1)
    row_seg = segment_at(row_pos, info)
    allowed = (row_seg == segment_at(col_pos, info)) & (col_pos <= row_pos)
    carried = row_seg == before
    return first, before, allowed, carried


def match_row(info, first, before, d, rows):
    pos = first - 128 * d + iota((rows, 128), 1)
    return (segment_at(pos, info) == before) & (pos >= 0)


PARTS = ((0,), (1, 2), (3, 4), (5, 6), (7, 8))


def layout(*sizes):
    starts, total = [], 0
    for size in sizes:
        starts.append(total)
        total += -(-size // 128) * 128
    return starts, total


def carry_rows(heads, kv, part):
    count = len(PARTS[part])
    wide = heads * 128
    if part == 0:
        return layout(wide, wide, wide, 0, heads * 3, const_rows(heads), 0, 0)
    turned = kv * count * 128
    return layout(
        wide, wide, wide, wide, heads * (2 + 2 * count), 0, turned, turned, wide if part == 2 else 0
    )


def const_rows(heads):
    return -(-(3 * heads + 8) // 16) * 16


def local_rows(heads, kv):
    size = const_rows(heads)
    cargo = 2 * kv * HDIM + 3 * heads
    starts, total = [], 0
    for rows in (heads * 128, cargo, size, size, size):
        starts.append(total)
        total += rows
    return starts, total


def keep_rows(heads, kv):
    return layout(heads * 128, heads * 128, kv * 128, kv * 128, kv * 128)


def real_rows(heads, kv):
    count = BACK + 1
    wide = heads * 128
    return layout(
        wide, wide, 0, const_rows(heads), count * heads, BACK * heads, kv * count * 128
    )


def half_rows(heads, kv):
    return layout(heads * 128, kv * (BACK + 1) * 128)


def slab(start, h):
    return pl.ds(pl.multiple_of(start + h * 128, 128), 128)


def forward_kernel(kv, heads, part, *refs):
    refs = list(refs)

    def take(count):
        out = refs[:count]
        del refs[:count]
        return out

    first, last = part == 0, part == len(PARTS) - 1
    blocks = PARTS[part]
    local = take(1)[0]
    local_at = local_rows(heads, kv)[0]
    if first:
        sources = [[local]]
        carry, keep = take(2)
        cum_ref, value_ref, consts = refs[-3:]
        total = jnp.zeros(consts.shape, F32)
        for i in range(3):
            total += local[local_at[2 + i] : local_at[2 + i] + consts.shape[0], :].astype(F32)
        consts[...] = total
    else:
        sources = [take(1 if d % 2 == 0 else 2) for d in blocks]
        origin = take(1)[0]
        carries = [origin] + take(part - 1)
        before_carry = carries[-1]
        before_at = carry_rows(heads, kv, part - 1)[0]
    if last:
        keep, real, half, stats = take(4)
        acc = refs[-1]
        acc[...] = jnp.zeros_like(acc)
    elif not first:
        carry = take(1)[0]
    kt, vv, bias, step_ref = take(4)
    if not first:
        key32, fade_ref = take(2)
    origin_at = carry_rows(heads, kv, 0)[0]
    keep_at = keep_rows(heads, kv)[0]
    real_at = real_rows(heads, kv)[0]
    half_at = half_rows(heads, kv)[0]
    carry_at = carry_rows(heads, kv, part)[0]
    if first:
        constant, base = consts, 0
        carry[carry_at[5] : carry_at[5] + consts.shape[0], :] = consts[...]
    else:
        constant, base = origin, origin_at[5]
    cum_at = origin_at[4] + heads
    enter_at = carry_rows(heads, kv, 2)[0][8]
    group = heads // kv
    size = 3 * heads + 8
    info = place_of(constant[base + size - 8 : base + size, :], 128)
    even_core = info[4] == 0
    start, before, allowed, carried = masks(info)

    reach = (iota((128, 128), 0) <= iota((128, 128), 1)).astype(BF16)
    if first:
        after = jnp.zeros((heads, 128), F32)
    else:
        after = before_carry[before_at[4] : before_at[4] + heads, :]
    rate = constant[base : base + heads, :]
    for i, d in enumerate(blocks):
        at = slice(128 * i, 128 * i + 128)
        near = sources[i]

        def piece(low, high):
            if first:
                return near[0][local_at[1] + low : local_at[1] + high, :]
            if d % 2 == 0:
                return near[0][low:high, :]
            return jnp.where(even_core, near[0][low:high, :], near[1][low:high, :])

        for g in range(kv):
            block = piece(g * HDIM, (g + 1) * HDIM)
            value = piece((kv + g) * HDIM, (kv + g + 1) * HDIM)
            kt[g, :, at] = block
            vv[g, at, :] = value
            block, value = block.astype(F32), value.astype(F32)
            if last:
                row = (g * (BACK + 1) + d) * 128
                half[half_at[1] + row : half_at[1] + row + 128, :] = kt[g, :, at]
                real[real_at[6] + row : real_at[6] + row + 128, :] = value.T
            else:
                row = (g * len(blocks) + i) * 128
                out, where = (keep, keep_at[3:5]) if first else (carry, carry_at[6:8])
                out[where[0] + row : where[0] + row + 128, :] = block
                out[where[1] + row : where[1] + row + 128, :] = value.T
            if first:
                keep[keep_at[2] + 128 * g : keep_at[2] + 128 * g + 128, :] = value
                value_ref[g] = value
            else:
                key32[g, :, at] = block
        first_step = 2 * kv * HDIM
        parts = [piece(first_step + k * heads, first_step + (k + 1) * heads) for k in range(3)]
        step = parts[0].astype(F32) + parts[1].astype(F32) + parts[2].astype(F32)
        sums = mm(parts[0], reach) + mm(parts[1], reach) + mm(parts[2], reach)
        step_ref[i] = step
        if first:
            carry[cum_at : cum_at + heads, :] = sums
            cum_ref[...] = sums
            bias[:, at] = jnp.where(allowed, 0.0, NEG)
        else:
            total = jnp.broadcast_to(sums[:, 127:128], (heads, 128))
            left = jnp.maximum(total - sums, 0.0) + after
            found = match_row(info, start, before, d, heads)
            fade_ref[i] = jnp.where(found, jnp.exp(-rate * left), 0.0)
            after = after + total
            both = carried & match_row(info, start, before, d, 128)
            bias[:, at] = jnp.where(both, 0.0, NEG)
    if last:
        real[real_at[3] : real_at[3] + size, :] = origin[base : base + size, :]
        for p, source in enumerate(carries):
            where = carry_rows(heads, kv, p)[0]
            count = len(PARTS[p])
            low = where[4] + heads * 2
            rows = heads * count
            to = real_at[4] + heads * PARTS[p][0]
            real[to : to + rows, :] = source[low : low + rows, :]
            if p > 0:
                low = low + rows
                to = real_at[5] + heads * (PARTS[p][0] - 1)
                real[to : to + rows, :] = source[low : low + rows, :]
            turned, where = (keep, keep_at[3:5]) if p == 0 else (source, where[6:8])
            for g in range(kv):
                rows = 128 * count
                low = g * rows
                to = (g * (BACK + 1) + PARTS[p][0]) * 128
                half[half_at[1] + to : half_at[1] + to + rows, :] = turned[
                    where[0] + low : where[0] + low + rows, :
                ].astype(BF16)
                real[real_at[6] + to : real_at[6] + to + rows, :] = turned[
                    where[1] + low : where[1] + low + rows, :
                ]
        small, step_at = real, real_at[4] + heads * blocks[0]
        fade_at = real_at[5] + heads * (blocks[0] - 1)
    else:
        small, step_at = carry, carry_at[4] + heads * 2
        fade_at = step_at + heads * len(blocks)
        carry[carry_at[4] : carry_at[4] + heads, :] = after
    for i in range(len(blocks)):
        small[step_at + heads * i : step_at + heads * (i + 1), :] = step_ref[i]
        if not first:
            small[fade_at + heads * i : fade_at + heads * (i + 1), :] = fade_ref[i]

    def rate_of(h):
        return constant[pl.ds(base + h, 1), :]

    def one_head(h, unused):
        g = h // group
        query = local[slab(local_at[0], h), :]
        scores = mm(query, kt[g])
        scaled = scores * (LOG2E / math.sqrt(HDIM)) + bias[...]
        top = jnp.broadcast_to(jnp.max(scaled, axis=1, keepdims=True), (128, 128))
        if not first:
            old = before_carry[slab(before_at[0], h), :]
            top = jnp.maximum(old, top)
        weights = [
            jnp.exp2(scaled[:, 128 * i : 128 * i + 128] - top) for i in range(len(blocks))
        ]
        total = weights[0]
        for other in weights[1:]:
            total = total + other
        total = jnp.broadcast_to(jnp.sum(total, axis=1, keepdims=True), (128, 128))
        weights = jnp.concatenate([w.astype(BF16) for w in weights], axis=1)
        if not first:
            weight_row = jnp.concatenate(
                [
                    fade_ref[i, pl.ds(h, 1), :] * step_ref[i, pl.ds(h, 1), :]
                    for i in range(len(blocks))
                ],
                axis=1,
            )
            mixed = mm(weights, vv[g])
            state = mm_apart(key32[g] * weight_row, vv[g])
            scale = jnp.exp2(old - top)
            total = total + before_carry[slab(before_at[1], h), :] * scale
            mixed = mixed + before_carry[slab(before_at[2], h), :] * scale
            if part > 1:
                state = state + before_carry[slab(before_at[3], h), :]
        else:
            decay_row = rate_of(h)
            cum_row = jnp.broadcast_to(cum_ref[pl.ds(h, 1), :], (128, 128))
            cum_col = cum_row.T
            decay = jnp.where(
                allowed, jnp.exp(-decay_row * jnp.maximum(cum_col - cum_row, 0.0)), 0.0
            )
            decayed = scores[:, :128] * decay
            keep[slab(keep_at[1], h), :] = decayed
            skipped = constant[pl.ds(base + heads + h, 1), :] * value_ref[g]
            high, low = two_parts(decayed * step_ref[0, pl.ds(h, 1), :])
            joined = mm(jnp.concatenate([weights, high, low], axis=0), vv[g])
            mixed = joined[:128]
            keep[slab(keep_at[0], h), :] = joined[128:256] + joined[256:] + skipped
        if not last:
            carry[slab(carry_at[0], h), :] = top
            carry[slab(carry_at[1], h), :] = total
            carry[slab(carry_at[2], h), :] = mixed
            if not first:
                carry[slab(carry_at[3], h), :] = state
        if part == 2:
            cum_col = jnp.broadcast_to(origin[pl.ds(cum_at + h, 1), :], (128, 128)).T
            carry[slab(enter_at, h), :] = jnp.where(
                carried, jnp.exp(-rate_of(h) * cum_col), 0.0
            )
        if last:
            teach = (mixed / total).astype(BF16)
            half[slab(half_at[0], h), :] = teach
            off = mm_right(query, state) * carries[2][slab(enter_at, h), :]
            raw = keep[slab(keep_at[0], h), :] + off
            real[slab(real_at[0], h), :] = raw
            real[slab(real_at[1], h), :] = off
            gained = raw * constant[pl.ds(base + 2 * heads + h, 1), :]
            acc[0] += raw * raw
            acc[1] += gained * gained
            acc[2] += gained * teach.astype(F32)
        return unused

    lax.fori_loop(0, heads, one_head, 0, unroll=(16, 8, 8, 16, 16)[part])
    if last:
        stats[...] = jnp.concatenate(
            [to_row(acc[0]), to_row(acc[1]), to_row(acc[2]), jnp.zeros((5, 128), F32)], axis=0
        )


def forward(kv, heads, rows, part, operands):
    blocks = PARTS[part]
    first, last = part == 0, part == len(PARTS) - 1
    wide = 128 * len(blocks)
    if last:
        outs = [
            shape((real_rows(heads, kv)[1], 128)),
            shape((half_rows(heads, kv)[1], 128), BF16),
            shape((8, 128)),
        ]
    else:
        outs = [shape((carry_rows(heads, kv, part)[1], 128))]
    if first:
        outs.append(shape((keep_rows(heads, kv)[1], 128)))
    scratch = [
        pltpu.VMEM((kv, HDIM, wide), BF16),
        pltpu.VMEM((kv, wide, HDIM), BF16),
        pltpu.VMEM((rows, wide), F32),
        pltpu.VMEM((len(blocks), heads, 128), F32),
    ]
    if first:
        scratch += [
            pltpu.VMEM((heads, 128), F32),
            pltpu.VMEM((kv, rows, HDIM), F32),
            pltpu.VMEM((const_rows(heads), 128), F32),
        ]
    else:
        scratch += [
            pltpu.VMEM((kv, HDIM, wide), F32),
            pltpu.VMEM((len(blocks), heads, 128), F32),
        ]
    if last:
        scratch.append(pltpu.VMEM((3, rows, HDIM), F32))
    return pl.pallas_call(
        functools.partial(forward_kernel, kv, heads, part),
        out_shape=outs,
        in_specs=vmem(len(operands)),
        out_specs=vmem(len(outs)),
        scratch_shapes=scratch,
        compiler_params=SMALL,
        cost_estimate=pl.CostEstimate(
            flops=len(blocks) * heads * rows * 128 * 128 * 12,
            bytes_accessed=len(blocks) * 3 * 1024 * 1024,
            transcendentals=2 * heads * rows * wide,
        ),
        name="forward_" + "abcde"[part],
    )(*operands)


def backward_kernel(kv, heads, groups, features, row_total, *refs):
    local, keep, enter, real, half, *refs = refs
    stats = refs[0][...]
    for other in refs[1:groups]:
        stats = stats + other[...]
    student_out, grads, gain_out, small_out, *refs = refs[groups:]
    inv_col, coef_col, late, skip_rows, direct_rows, minus_rows, row_sums = refs
    keep_at = keep_rows(heads, kv)[0]
    real_at = real_rows(heads, kv)[0]
    half_at = half_rows(heads, kv)[0]
    group = heads // kv
    enter_at = carry_rows(heads, kv, 2)[0][8]
    size = 3 * heads + 8
    base = real_at[3]
    info = place_of(real[base + size - 8 : base + size, :], 128)
    place, count = info[5], grads.shape[0]
    grads[...] = jnp.zeros_like(grads)
    row_sums[...] = jnp.zeros_like(row_sums)
    share = 2.0 / row_total
    squares, gained_squares, crossed = stats[0:1, :], stats[1:2, :], stats[2:3, :]
    inverse = lax.rsqrt(squares / features + EPSILON)
    inner = share * (inverse * gained_squares - crossed)
    coef = inverse * inverse * inverse * inner / features
    inv_col[...] = jnp.broadcast_to(inverse, (128, 128)).T
    coef_col[...] = jnp.broadcast_to(coef, (128, 128)).T
    row_i, col_i = iota((128, 128), 0), iota((128, 128), 1)
    later = (row_i >= col_i).astype(BF16)
    strict = (row_i < col_i).astype(BF16)

    def one_head(h, unused):
        g = h // group
        cols = slab(0, h)
        query = local[slab(0, h), :]
        raw, off = real[slab(real_at[0], h), :], real[slab(real_at[1], h), :]
        scale = real[pl.ds(base + 2 * heads + h, 1), :]
        inv = inv_col[...]
        normed = raw * inv * scale
        student_out[:, cols] = normed.astype(BF16)
        grad_normed = (normed - half[slab(half_at[0], h), :].astype(F32)) * share
        gain_out[:, cols] = jnp.sum(grad_normed * raw * inv, axis=0, keepdims=True)
        grad = inv * grad_normed * scale - raw * coef_col[...]
        value = keep[slab(keep_at[2], g), :]
        skip_rows[pl.ds(h, 1), :] = jnp.sum(grad * value, axis=0, keepdims=True)
        entering = enter[slab(enter_at, h), :]
        grad_state = mm_two((grad * entering).T, query)
        turned = [slab(g * ((BACK + 1) * 128), d) for d in range(BACK + 1)]
        keys = jnp.concatenate(
            [half[pl.ds(half_at[1] + turned[d].start, 128), :] for d in range(1, BACK + 1)],
            axis=1,
        )
        reached = mm_two(grad_state, keys)
        for d in range(1, BACK + 1):
            values = real[pl.ds(real_at[6] + turned[d].start, 128), :]
            late[d - 1, pl.ds(h, 1), :] = jnp.sum(
                reached[:, 128 * d - 128 : 128 * d] * values, axis=0, keepdims=True
            )
        own_values = real[pl.ds(real_at[6] + turned[0].start, 128), :].astype(BF16)
        pulled = mm_two(grad, own_values)
        pairs = keep[slab(keep_at[1], h), :] * pulled
        direct_rows[pl.ds(h, 1), :] = jnp.sum(pairs, axis=0, keepdims=True)
        pairs = jnp.where(
            row_i > col_i, pairs * real[pl.ds(real_at[4] + h, 1), :], 0.0
        )
        minus_rows[pl.ds(h, 1), :] = jnp.sum(pairs, axis=0, keepdims=True)
        sums = jnp.sum(pairs + grad * off, axis=1, keepdims=True)
        row_sums[...] += jnp.where(col_i == h, jnp.broadcast_to(sums, (128, 128)), 0.0)
        return unused

    lax.fori_loop(0, heads, one_head, 0, unroll=16)

    def summed(x, triangle):
        high, low = two_parts(x)
        rest = (x - high.astype(F32) - low.astype(F32)).astype(BF16)
        return mm(high, triangle) + mm(low, triangle) + mm(rest, triangle)

    rate = real[base : base + heads, :]
    spanned = summed(row_sums[...].T[:heads, :] - minus_rows[...], later)
    grads[place] = direct_rows[...] - rate * spanned
    rate_rows = spanned * real[real_at[4] : real_at[4] + heads, :]
    earlier = jnp.zeros((heads, 128), F32)
    for d in range(BACK, 0, -1):
        step = real[real_at[4] + heads * d : real_at[4] + heads * (d + 1), :]
        fade = real[real_at[5] + heads * (d - 1) : real_at[5] + heads * d, :]
        direct = late[d - 1] * fade
        whole = direct * step
        spanned = summed(whole, strict) + earlier
        grads[lax.rem(place - d + count, count)] = direct - rate * spanned
        rate_rows = rate_rows + spanned * step
        earlier = earlier + jnp.sum(whole, axis=1, keepdims=True)
    small_out[...] = jnp.concatenate(
        [to_row(skip_rows[...]), -to_row(rate_rows * rate), jnp.zeros((6, 128), F32)], axis=0
    )


def fold_kernel(grads, gain, small, out):
    total = jnp.sum(grads[...], axis=0)
    rows = total.shape[0]
    tiles = gain.shape[1] // 128
    out[0:rows, :] = total
    for i in range(tiles):
        out[rows + i : rows + i + 1, :] = gain[:, 128 * i : 128 * i + 128]
    out[rows + tiles : rows + tiles + 8, :] = small[...]


def weight_kernel(own, other, slope, slope_other, hidden, far, out, wide):
    heads = slope.shape[0]
    total = own[...] + other[...]
    core = lax.axis_index("core")
    low_core = core == 0
    near_slope, far_slope = slope[...], slope_other[...]
    top, bottom = total[0:heads], total[heads : 2 * heads]
    near_pre = jnp.where(low_core, top, bottom) * near_slope
    far_pre = jnp.where(low_core, bottom, top) * far_slope
    near_low, far_low = near_pre.astype(BF16), far_pre.astype(BF16)
    side = far.shape[1] // 2
    count = side // 128
    tiles = total.shape[0] - 2 * heads - 8
    lines = [total[2 * heads + i : 2 * heads + i + 1] for i in range(tiles)]
    lines.append(to_row(near_pre + far_pre))
    base = 2 * heads + tiles
    lines += [total[base + 1 : base + 2], total[base : base + 1]]
    for j in range(count):
        start = j * (heads + 2)
        cols = pl.ds(pl.multiple_of(core * side + 128 * j, 128), 128)
        wide[start : start + heads, :] = mm(near_low, hidden[:, cols]) + mm(
            far_low, far[:, cols]
        )
        line = jnp.zeros((1, 128), F32)
        if j < len(lines):
            line = jnp.where(low_core, lines[j], line)
        high = line.astype(BF16).astype(F32)
        wide[start + heads : start + heads + 1, :] = high
        wide[start + heads + 1 : start + heads + 2, :] = line - high
    out[...] = wide[...].astype(BF16)


def spread_kernel(count, got, out, wide):
    wide[...] = got[...].astype(F32)
    each = wide.shape[0] // count
    total = wide[0:each, :]
    for j in range(1, count):
        total = total + wide[each * j : each * (j + 1), :]
    small = total[each - 2 : each - 1, :] + total[each - 1 : each, :]
    for j in range(count):
        start = (each - 1) * j
        out[start : start + each - 2, :] = total[: each - 2, :]
        out[start + each - 2 : start + each - 1, :] = small


def finish_kernel(mine, other, weight, bias, decay, skip, gain):
    heads = weight.shape[0]
    count = mine.shape[0] // (heads + 1)
    tiles = gain.shape[1] // 128
    core = lax.axis_index("core")

    def place(source, half):
        for j in range(count):
            i = half * count + j
            start = j * (heads + 1)
            weight[:, 128 * i : 128 * i + 128] = source[start : start + heads, :]
            row = source[start + heads : start + heads + 1, :]
            if i < tiles:
                gain[:, 128 * i : 128 * i + 128] = row
            if i == tiles:
                bias[...] = row[:, :heads]
            if i == tiles + 1:
                decay[...] = row[:, :heads]
            if i == tiles + 2:
                skip[...] = row[:, :heads]

    for half in range(2):

        @pl.when(core == half)
        def _():
            place(mine, half)
            place(other, 1 - half)


def vmem(count):
    return [pl.BlockSpec(memory_space=pltpu.VMEM)] * count


def smem(count):
    return [pl.BlockSpec(memory_space=pltpu.SMEM)] * count


def shape(dims, kind=F32):
    return jax.ShapeDtypeStruct(dims, kind)


LARGE = pltpu.CompilerParams(vmem_limit_bytes=56 * 1024 * 1024)
SMALL = pltpu.CompilerParams(vmem_limit_bytes=16 * 1024 * 1024)


def body(
    hidden_in,
    teacher_queries,
    teacher_keys,
    teacher_values,
    doc_lengths,
    dt_weight,
    dt_bias,
    decay_log,
    skip_gain,
    norm_gain,
):
    rows = teacher_queries.shape[1]
    heads = dt_weight.shape[1]
    kv = teacher_keys.shape[2] // HDIM
    width = heads * HDIM
    features = width * lax.axis_size("grp")
    depth = hidden_in.shape[2]
    chips = lax.axis_size("z")
    blocks = 2 * chips
    row_total = lax.axis_size("dp") * rows * blocks
    hidden = hidden_in[0]
    gain = norm_gain[None, :]
    cargo = 2 * kv * HDIM + 3 * heads

    payload, slope, consts = pl.pallas_call(
        functools.partial(prep_kernel, kv),
        out_shape=[
            shape((cargo, 128), BF16),
            shape((heads, 128)),
            shape((const_rows(heads), 128)),
        ],
        in_specs=smem(4) + vmem(5),
        out_specs=vmem(3),
        compiler_params=LARGE,
        name="prep",
    )(
        doc_lengths, dt_bias, decay_log, skip_gain, gain, hidden, dt_weight.T,
        teacher_keys[0], teacher_values[0],
    )

    swap = [(0, 1), (1, 0)]
    hop = [(i, (i + 1) % chips) for i in range(chips)]
    run = functools.partial(forward, kv, heads, rows)

    def across(part):
        return lax.ppermute(part, "core", swap)

    hop1 = lax.ppermute(payload, "z", hop)
    sib0 = across(payload)
    local = pl.pallas_call(
        functools.partial(pack_kernel, kv),
        out_shape=shape((local_rows(heads, kv)[1], 128), BF16),
        in_specs=vmem(3),
        out_specs=pl.BlockSpec(memory_space=pltpu.VMEM),
        compiler_params=SMALL,
        name="pack",
    )(teacher_queries[0], payload, consts)
    hop1, local = lax.optimization_barrier((hop1, local))
    hop2 = lax.ppermute(hop1, "z", hop)
    sib1 = across(hop1)
    slope_other = across(slope)
    origin, keep = run(0, [local])
    hop2, origin = lax.optimization_barrier((hop2, origin))
    hop3 = lax.ppermute(hop2, "z", hop)
    sib2 = across(hop2)
    (carry1,) = run(1, [local, sib1, sib0, hop1, origin])
    hop3, carry1, slope_other = lax.optimization_barrier((hop3, carry1, slope_other))
    hop4 = lax.ppermute(hop3, "z", hop)
    sib3 = across(hop3)
    (carry2,) = run(2, [local, sib2, sib1, hop2, origin, carry1])
    hop4, carry2 = lax.optimization_barrier((hop4, carry2))
    sib4 = across(hop4)
    (carry3,) = run(3, [local, sib3, sib2, hop3, origin, carry1, carry2])
    real, half, stats = run(
        4, [local, sib4, sib3, hop4, origin, carry1, carry2, carry3, keep]
    )
    hidden_late, stats = lax.optimization_barrier((hidden, stats))
    far = across(hidden_late)
    groups = lax.axis_size("grp")
    all_stats = [stats] + [
        lax.ppermute(stats, "grp", [(i, (i + k) % groups) for i in range(groups)])
        for k in range(1, groups)
    ]

    student, grads, grad_gain, small = pl.pallas_call(
        functools.partial(backward_kernel, kv, heads, len(all_stats), features, row_total),
        out_shape=[
            shape((rows, width), BF16),
            shape((blocks, heads, 128)),
            shape((1, width)),
            shape((8, 128)),
        ],
        in_specs=vmem(5 + len(all_stats)),
        out_specs=vmem(4),
        scratch_shapes=[
            pltpu.VMEM((rows, 128), F32),
            pltpu.VMEM((rows, 128), F32),
            pltpu.VMEM((BACK, heads, 128), F32),
            pltpu.VMEM((heads, 128), F32),
            pltpu.VMEM((heads, 128), F32),
            pltpu.VMEM((heads, 128), F32),
            pltpu.VMEM((128, 128), F32),
        ],
        compiler_params=SMALL,
        name="backward",
    )(local, keep, carry2, real, half, *all_stats)

    grads = lax.all_to_all(grads.reshape(chips, 2 * heads, 128), "z", 0, 0, tiled=True)
    folded = pl.pallas_call(
        fold_kernel,
        out_shape=shape((3 * heads + 8, 128)),
        in_specs=vmem(3),
        out_specs=pl.BlockSpec(memory_space=pltpu.VMEM),
        compiler_params=SMALL,
        name="fold",
    )(grads, grad_gain, small)

    axes = ("z", "dp")
    count = chips * lax.axis_size("dp")
    half = pl.pallas_call(
        weight_kernel,
        out_shape=shape((count * (heads + 2), 128), BF16),
        in_specs=vmem(6),
        out_specs=pl.BlockSpec(memory_space=pltpu.VMEM),
        scratch_shapes=[pltpu.VMEM((count * (heads + 2), 128), F32)],
        compiler_params=SMALL,
        name="weights",
    )(folded, across(folded), slope, slope_other, hidden, far)
    half = half.reshape(count, (heads + 2) // 2, 2, 128)
    got = lax.all_to_all(half, axes, 0, 0, tiled=True)
    spread = pl.pallas_call(
        functools.partial(spread_kernel, count),
        out_shape=shape((count * (heads + 1), 128)),
        in_specs=vmem(1),
        out_specs=pl.BlockSpec(memory_space=pltpu.VMEM),
        scratch_shapes=[pltpu.VMEM((count * (heads + 2), 128), F32)],
        compiler_params=SMALL,
        name="spread",
    )(got.reshape(count * (heads + 2), 128))
    spread = spread.reshape(count, heads + 1, 1, 128)
    mine = lax.all_to_all(spread, axes, 0, 0, tiled=True)
    mine = mine.reshape(count * (heads + 1), 128)
    other = lax.ppermute(mine, "core", swap)
    grad_weight, bias, decay, skip, gained = pl.pallas_call(
        finish_kernel,
        out_shape=[shape((heads, depth))] + [shape((1, heads))] * 3 + [shape((1, width))],
        in_specs=vmem(2),
        out_specs=vmem(5),
        compiler_params=SMALL,
        name="finish",
    )(mine, other)
    return (student[None], grad_weight.T, bias[0], decay[0], skip[0], gained[0])


def solution(mesh):
    sizes = dict(mesh.shape)
    split = jax.sharding.Mesh(
        mesh.devices.reshape(sizes["ctx"] // 2, 2, sizes["grp"], sizes["dp"]),
        ("z", "core", "grp", "dp"),
    )
    ctx = ("z", "core")
    placed = (
        P("dp", ctx, None),
        P("dp", ctx, "grp"),
        P("dp", ctx, "grp"),
        P("dp", ctx, "grp"),
        P("dp", None),
        P(None, "grp"),
        P("grp"),
        P("grp"),
        P("grp"),
        P("grp"),
    )
    return jax.shard_map(
        body,
        mesh=split,
        in_specs=placed,
        out_specs=(P("dp", ctx, "grp"), P(None, "grp"), P("grp"), P("grp"), P("grp"), P("grp")),
        check_vma=False,
    )
```

```python
import functools
import math

import jax
import jax.numpy as jnp
from jax import lax
from jax.experimental import pallas as pl
from jax.experimental.pallas import tpu as pltpu
from jax.sharding import PartitionSpec as P

HDIM = 128
EPSILON = 1e-05
BACK = 8
NEG = -1e30
LOG2E = math.log2(math.e)
F32 = jnp.float32
BF16 = jnp.bfloat16


def mm(a, b):
    return jnp.dot(a, b, preferred_element_type=F32)


def two_parts(x):
    high = x.astype(BF16)
    return high, (x - high.astype(F32)).astype(BF16)


def mm_two(a, b):
    rows = a.shape[0]
    both = mm(jnp.concatenate(two_parts(a), axis=0), b)
    return both[:rows] + both[rows:]


def mm_apart(a, b):
    high, low = two_parts(a)
    return mm(high, b) + mm(low, b)


def mm_right(a, b):
    high, low = two_parts(b)
    return mm(a, high) + mm(a, low)


def iota(shape, dim):
    return lax.broadcasted_iota(jnp.int32, shape, dim)


def to_row(x):
    rows = x.shape[0]
    if rows < 128:
        x = jnp.concatenate([x, jnp.zeros((128 - rows, x.shape[1]), F32)], axis=0)
    return jnp.sum(x.T, axis=0, keepdims=True)


def column_of(values, rows):
    row = iota((rows, 128), 0)
    out = jnp.zeros((rows, 128), F32)
    for h in range(rows):
        out = jnp.where(row == h, values[h], out)
    return out


def place_of(consts, rows):
    core = lax.axis_index("core")
    place = lax.axis_index("z") * lax.axis_size("core") + core
    starts = [consts[i : i + 1, :].astype(jnp.int32) for i in range(3)]
    return (place * rows, *starts, core, place)


def segment_at(pos, info):
    return (
        (pos >= info[1]).astype(jnp.int32)
        + (pos >= info[2]).astype(jnp.int32)
        + (pos >= info[3]).astype(jnp.int32)
    )


def prep_kernel(
    kv,
    lengths,
    bias,
    decay,
    skip,
    gain,
    hidden,
    weight,
    keys,
    values,
    payload,
    slope,
    consts,
):
    heads = weight.shape[0]
    pre = (
        lax.dot_general(
            hidden[...], weight[...], (((1,), (1,)), ((), ())), preferred_element_type=F32
        ).T
        + column_of(bias, heads)
    )
    step = jnp.maximum(pre, 0.0) + jnp.log1p(jnp.exp(-jnp.abs(pre)))
    slope[...] = 1.0 / (1.0 + jnp.exp(-pre))
    for g in range(kv):
        cols = slice(g * HDIM, (g + 1) * HDIM)
        payload[g * HDIM : (g + 1) * HDIM, :] = keys[:, cols].astype(F32).T.astype(BF16)
        payload[(kv + g) * HDIM : (kv + g + 1) * HDIM, :] = values[:, cols]
    consts[0:heads, :] = jnp.exp(column_of(decay, heads))
    consts[heads : 2 * heads, :] = column_of(skip, heads)
    for h in range(heads):
        consts[2 * heads + h : 2 * heads + h + 1, :] = gain[:, h * HDIM : (h + 1) * HDIM]
    one = lengths[0, 0]
    two = one + lengths[0, 1]
    starts = (one, two, two + lengths[0, 2], 0, 0, 0, 0, 0)
    row = iota((8, 128), 0)
    marks = jnp.zeros((8, 128), jnp.int32)
    for i in range(3):
        marks = jnp.where(row == i, starts[i], marks)
    consts[3 * heads : 3 * heads + 8, :] = marks.astype(F32)
    consts[3 * heads + 8 :, :] = jnp.zeros((consts.shape[0] - 3 * heads - 8, 128), F32)
    first = 2 * kv * HDIM
    for part in range(3):
        piece = step.astype(BF16)
        payload[first + part * heads : first + (part + 1) * heads, :] = piece
        step = step - piece.astype(F32)


def pack_kernel(kv, queries, payload, consts, local):
    heads = queries.shape[1] // 128
    at = local_rows(heads, kv)[0]
    for h in range(heads):
        local[at[0] + 128 * h : at[0] + 128 * h + 128, :] = queries[:, 128 * h : 128 * h + 128]
    local[at[1] : at[1] + payload.shape[0], :] = payload[...]
    rest = consts[...]
    for part in range(3):
        piece = rest.astype(BF16)
        local[at[2 + part] : at[2 + part] + rest.shape[0], :] = piece
        rest = rest - piece.astype(F32)


def masks(info):
    first = info[0]
    before = jnp.where(
        first > 0, segment_at(jnp.maximum(first - 1, 0) + iota((1, 128), 1) * 0, info), -1
    )
    row_pos = first + iota((128, 128), 0)
    col_pos = first + iota((128, 128), 1)
    row_seg = segment_at(row_pos, info)
    allowed = (row_seg == segment_at(col_pos, info)) & (col_pos <= row_pos)
    carried = row_seg == before
    return first, before, allowed, carried


def match_row(info, first, before, d, rows):
    pos = first - 128 * d + iota((rows, 128), 1)
    return (segment_at(pos, info) == before) & (pos >= 0)


PARTS = ((0,), (1, 2), (3, 4), (5, 6), (7, 8))


def layout(*sizes):
    starts, total = [], 0
    for size in sizes:
        starts.append(total)
        total += -(-size // 128) * 128
    return starts, total


def carry_rows(heads, kv, part):
    count = len(PARTS[part])
    wide = heads * 128
    if part == 0:
        return layout(wide, wide, wide, 0, heads * 3, const_rows(heads), 0, 0)
    turned = kv * count * 128
    return layout(
        wide, wide, wide, wide, heads * (2 + 2 * count), 0, turned, turned, wide if part == 2 else 0
    )


def const_rows(heads):
    return -(-(3 * heads + 8) // 16) * 16


def local_rows(heads, kv):
    size = const_rows(heads)
    cargo = 2 * kv * HDIM + 3 * heads
    starts, total = [], 0
    for rows in (heads * 128, cargo, size, size, size):
        starts.append(total)
        total += rows
    return starts, total


def keep_rows(heads, kv):
    return layout(heads * 128, heads * 128, kv * 128, kv * 128, kv * 128)


def real_rows(heads, kv):
    count = BACK + 1
    wide = heads * 128
    return layout(
        wide, wide, 0, const_rows(heads), count * heads, BACK * heads, kv * count * 128
    )


def half_rows(heads, kv):
    return layout(heads * 128, kv * (BACK + 1) * 128)


def slab(start, h):
    return pl.ds(pl.multiple_of(start + h * 128, 128), 128)


def forward_kernel(kv, heads, part, *refs):
    refs = list(refs)

    def take(count):
        out = refs[:count]
        del refs[:count]
        return out

    first, last = part == 0, part == len(PARTS) - 1
    blocks = PARTS[part]
    local = take(1)[0]
    local_at = local_rows(heads, kv)[0]
    if first:
        sources = [[local]]
        carry, keep = take(2)
        cum_ref, value_ref, consts = refs[-3:]
        total = jnp.zeros(consts.shape, F32)
        for i in range(3):
            total += local[local_at[2 + i] : local_at[2 + i] + consts.shape[0], :].astype(F32)
        consts[...] = total
    else:
        sources = [take(1 if d % 2 == 0 else 2) for d in blocks]
        origin = take(1)[0]
        carries = [origin] + take(part - 1)
        before_carry = carries[-1]
        before_at = carry_rows(heads, kv, part - 1)[0]
    if last:
        keep, real, half, stats = take(4)
    elif not first:
        carry = take(1)[0]
    kt, vv, bias, step_ref = take(4)
    if not first:
        key32, fade_ref = take(2)
    origin_at = carry_rows(heads, kv, 0)[0]
    keep_at = keep_rows(heads, kv)[0]
    real_at = real_rows(heads, kv)[0]
    half_at = half_rows(heads, kv)[0]
    carry_at = carry_rows(heads, kv, part)[0]
    if first:
        constant, base = consts, 0
        carry[carry_at[5] : carry_at[5] + consts.shape[0], :] = consts[...]
    else:
        constant, base = origin, origin_at[5]
    cum_at = origin_at[4] + heads
    enter_at = carry_rows(heads, kv, 2)[0][8]
    group = heads // kv
    size = 3 * heads + 8
    info = place_of(constant[base + size - 8 : base + size, :], 128)
    even_core = info[4] == 0
    start, before, allowed, carried = masks(info)

    reach = (iota((128, 128), 0) <= iota((128, 128), 1)).astype(BF16)
    if first:
        after = jnp.zeros((heads, 128), F32)
    else:
        after = before_carry[before_at[4] : before_at[4] + heads, :]
    rate = constant[base : base + heads, :]
    for i, d in enumerate(blocks):
        at = slice(128 * i, 128 * i + 128)
        near = sources[i]

        def piece(low, high):
            if first:
                return near[0][local_at[1] + low : local_at[1] + high, :]
            if d % 2 == 0:
                return near[0][low:high, :]
            return jnp.where(even_core, near[0][low:high, :], near[1][low:high, :])

        for g in range(kv):
            block = piece(g * HDIM, (g + 1) * HDIM)
            value = piece((kv + g) * HDIM, (kv + g + 1) * HDIM)
            kt[g, :, at] = block
            vv[g, at, :] = value
            block, value = block.astype(F32), value.astype(F32)
            if last:
                row = (g * (BACK + 1) + d) * 128
                half[half_at[1] + row : half_at[1] + row + 128, :] = kt[g, :, at]
                real[real_at[6] + row : real_at[6] + row + 128, :] = value.T
            else:
                row = (g * len(blocks) + i) * 128
                out, where = (keep, keep_at[3:5]) if first else (carry, carry_at[6:8])
                out[where[0] + row : where[0] + row + 128, :] = block
                out[where[1] + row : where[1] + row + 128, :] = value.T
            if first:
                keep[keep_at[2] + 128 * g : keep_at[2] + 128 * g + 128, :] = value
                value_ref[g] = value
            else:
                key32[g, :, at] = block
        first_step = 2 * kv * HDIM
        parts = [piece(first_step + k * heads, first_step + (k + 1) * heads) for k in range(3)]
        step = parts[0].astype(F32) + parts[1].astype(F32) + parts[2].astype(F32)
        sums = mm(parts[0], reach) + mm(parts[1], reach) + mm(parts[2], reach)
        step_ref[i] = step
        if first:
            carry[cum_at : cum_at + heads, :] = sums
            cum_ref[...] = sums
            bias[:, at] = jnp.where(allowed, 0.0, NEG)
        else:
            total = jnp.broadcast_to(sums[:, 127:128], (heads, 128))
            left = jnp.maximum(total - sums, 0.0) + after
            found = match_row(info, start, before, d, heads)
            fade_ref[i] = jnp.where(found, jnp.exp(-rate * left), 0.0)
            after = after + total
            both = carried & match_row(info, start, before, d, 128)
            bias[:, at] = jnp.where(both, 0.0, NEG)
    if last:
        real[real_at[3] : real_at[3] + size, :] = origin[base : base + size, :]
        for p, source in enumerate(carries):
            where = carry_rows(heads, kv, p)[0]
            count = len(PARTS[p])
            low = where[4] + heads * 2
            rows = heads * count
            to = real_at[4] + heads * PARTS[p][0]
            real[to : to + rows, :] = source[low : low + rows, :]
            if p > 0:
                low = low + rows
                to = real_at[5] + heads * (PARTS[p][0] - 1)
                real[to : to + rows, :] = source[low : low + rows, :]
            turned, where = (keep, keep_at[3:5]) if p == 0 else (source, where[6:8])
            for g in range(kv):
                rows = 128 * count
                low = g * rows
                to = (g * (BACK + 1) + PARTS[p][0]) * 128
                half[half_at[1] + to : half_at[1] + to + rows, :] = turned[
                    where[0] + low : where[0] + low + rows, :
                ].astype(BF16)
                real[real_at[6] + to : real_at[6] + to + rows, :] = turned[
                    where[1] + low : where[1] + low + rows, :
                ]
        small, step_at = real, real_at[4] + heads * blocks[0]
        fade_at = real_at[5] + heads * (blocks[0] - 1)
    else:
        small, step_at = carry, carry_at[4] + heads * 2
        fade_at = step_at + heads * len(blocks)
        carry[carry_at[4] : carry_at[4] + heads, :] = after
    for i in range(len(blocks)):
        small[step_at + heads * i : step_at + heads * (i + 1), :] = step_ref[i]
        if not first:
            small[fade_at + heads * i : fade_at + heads * (i + 1), :] = fade_ref[i]

    def rate_of(h):
        return constant[pl.ds(base + h, 1), :]

    def one_head(h, sums):
        g = h // group
        query = local[slab(local_at[0], h), :]
        scores = mm(query, kt[g])
        scaled = scores * (LOG2E / math.sqrt(HDIM)) + bias[...]
        top = jnp.broadcast_to(jnp.max(scaled, axis=1, keepdims=True), (128, 128))
        if not first:
            old = before_carry[slab(before_at[0], h), :]
            top = jnp.maximum(old, top)
        weights = [
            jnp.exp2(scaled[:, 128 * i : 128 * i + 128] - top) for i in range(len(blocks))
        ]
        total = weights[0]
        for other in weights[1:]:
            total = total + other
        total = jnp.broadcast_to(jnp.sum(total, axis=1, keepdims=True), (128, 128))
        weights = jnp.concatenate([w.astype(BF16) for w in weights], axis=1)
        if not first:
            weight_row = jnp.concatenate(
                [
                    fade_ref[i, pl.ds(h, 1), :] * step_ref[i, pl.ds(h, 1), :]
                    for i in range(len(blocks))
                ],
                axis=1,
            )
            mixed = mm(weights, vv[g])
            state = mm_apart(key32[g] * weight_row, vv[g])
            scale = jnp.exp2(old - top)
            total = total + before_carry[slab(before_at[1], h), :] * scale
            mixed = mixed + before_carry[slab(before_at[2], h), :] * scale
            if part > 1:
                state = state + before_carry[slab(before_at[3], h), :]
        else:
            decay_row = rate_of(h)
            cum_row = jnp.broadcast_to(cum_ref[pl.ds(h, 1), :], (128, 128))
            cum_col = cum_row.T
            decay = jnp.where(
                allowed, jnp.exp(-decay_row * jnp.maximum(cum_col - cum_row, 0.0)), 0.0
            )
            decayed = scores[:, :128] * decay
            keep[slab(keep_at[1], h), :] = decayed
            skipped = constant[pl.ds(base + heads + h, 1), :] * value_ref[g]
            high, low = two_parts(decayed * step_ref[0, pl.ds(h, 1), :])
            joined = mm(jnp.concatenate([weights, high, low], axis=0), vv[g])
            mixed = joined[:128]
            keep[slab(keep_at[0], h), :] = joined[128:256] + joined[256:] + skipped
        if not last:
            carry[slab(carry_at[0], h), :] = top
            carry[slab(carry_at[1], h), :] = total
            carry[slab(carry_at[2], h), :] = mixed
            if not first:
                carry[slab(carry_at[3], h), :] = state
        if part == 2:
            cum_col = jnp.broadcast_to(origin[pl.ds(cum_at + h, 1), :], (128, 128)).T
            carry[slab(enter_at, h), :] = jnp.where(
                carried, jnp.exp(-rate_of(h) * cum_col), 0.0
            )
        if last:
            teach = (mixed / total).astype(BF16)
            half[slab(half_at[0], h), :] = teach
            off = mm_right(query, state) * carries[2][slab(enter_at, h), :]
            raw = keep[slab(keep_at[0], h), :] + off
            real[slab(real_at[0], h), :] = raw
            real[slab(real_at[1], h), :] = off
            gained = raw * constant[pl.ds(base + 2 * heads + h, 1), :]
            sums = (
                sums[0] + raw * raw,
                sums[1] + gained * gained,
                sums[2] + gained * teach.astype(F32),
            )
        return sums

    nothing = tuple(jnp.zeros((128, 128), F32) for _ in range(3 if last else 0))
    sums = lax.fori_loop(0, heads, one_head, nothing, unroll=(16, 8, 8, 16, 16)[part])
    if last:
        stats[...] = jnp.concatenate(
            [to_row(sums[0]), to_row(sums[1]), to_row(sums[2]), jnp.zeros((5, 128), F32)], axis=0
        )


def forward(kv, heads, rows, part, operands):
    blocks = PARTS[part]
    first, last = part == 0, part == len(PARTS) - 1
    wide = 128 * len(blocks)
    if last:
        outs = [
            shape((real_rows(heads, kv)[1], 128)),
            shape((half_rows(heads, kv)[1], 128), BF16),
            shape((8, 128)),
        ]
    else:
        outs = [shape((carry_rows(heads, kv, part)[1], 128))]
    if first:
        outs.append(shape((keep_rows(heads, kv)[1], 128)))
    scratch = [
        pltpu.VMEM((kv, HDIM, wide), BF16),
        pltpu.VMEM((kv, wide, HDIM), BF16),
        pltpu.VMEM((rows, wide), F32),
        pltpu.VMEM((len(blocks), heads, 128), F32),
    ]
    if first:
        scratch += [
            pltpu.VMEM((heads, 128), F32),
            pltpu.VMEM((kv, rows, HDIM), F32),
            pltpu.VMEM((const_rows(heads), 128), F32),
        ]
    else:
        scratch += [
            pltpu.VMEM((kv, HDIM, wide), F32),
            pltpu.VMEM((len(blocks), heads, 128), F32),
        ]
    return pl.pallas_call(
        functools.partial(forward_kernel, kv, heads, part),
        out_shape=outs,
        in_specs=vmem(len(operands)),
        out_specs=vmem(len(outs)),
        scratch_shapes=scratch,
        compiler_params=SMALL,
        cost_estimate=pl.CostEstimate(
            flops=len(blocks) * heads * rows * 128 * 128 * 12,
            bytes_accessed=len(blocks) * 3 * 1024 * 1024,
            transcendentals=2 * heads * rows * wide,
        ),
        name="forward_" + "abcde"[part],
    )(*operands)


def backward_kernel(kv, heads, groups, features, row_total, *refs):
    local, keep, enter, real, half, *refs = refs
    stats = refs[0][...]
    for other in refs[1:groups]:
        stats = stats + other[...]
    student_out, grads, gain_out, small_out, *refs = refs[groups:]
    inv_col, coef_col, late, skip_rows, direct_rows, minus_rows = refs
    keep_at = keep_rows(heads, kv)[0]
    real_at = real_rows(heads, kv)[0]
    half_at = half_rows(heads, kv)[0]
    group = heads // kv
    enter_at = carry_rows(heads, kv, 2)[0][8]
    size = 3 * heads + 8
    base = real_at[3]
    info = place_of(real[base + size - 8 : base + size, :], 128)
    place, count = info[5], grads.shape[0]
    grads[...] = jnp.zeros_like(grads)
    share = 2.0 / row_total
    squares, gained_squares, crossed = stats[0:1, :], stats[1:2, :], stats[2:3, :]
    inverse = lax.rsqrt(squares / features + EPSILON)
    inner = share * (inverse * gained_squares - crossed)
    coef = inverse * inverse * inverse * inner / features
    inv_col[...] = jnp.broadcast_to(inverse, (128, 128)).T
    coef_col[...] = jnp.broadcast_to(coef, (128, 128)).T
    row_i, col_i = iota((128, 128), 0), iota((128, 128), 1)
    later = (row_i >= col_i).astype(BF16)
    strict = (row_i < col_i).astype(BF16)

    def one_head(h, row_sums):
        g = h // group
        cols = slab(0, h)
        query = local[slab(0, h), :]
        raw, off = real[slab(real_at[0], h), :], real[slab(real_at[1], h), :]
        scale = real[pl.ds(base + 2 * heads + h, 1), :]
        inv = inv_col[...]
        normed = raw * inv * scale
        student_out[:, cols] = normed.astype(BF16)
        grad_normed = (normed - half[slab(half_at[0], h), :].astype(F32)) * share
        gain_out[:, cols] = jnp.sum(grad_normed * raw * inv, axis=0, keepdims=True)
        grad = inv * grad_normed * scale - raw * coef_col[...]
        value = keep[slab(keep_at[2], g), :]
        skip_rows[pl.ds(h, 1), :] = jnp.sum(grad * value, axis=0, keepdims=True)
        entering = enter[slab(enter_at, h), :]
        grad_state = mm_two((grad * entering).T, query)
        turned = [slab(g * ((BACK + 1) * 128), d) for d in range(BACK + 1)]
        keys = jnp.concatenate(
            [half[pl.ds(half_at[1] + turned[d].start, 128), :] for d in range(1, BACK + 1)],
            axis=1,
        )
        reached = mm_two(grad_state, keys)
        for d in range(1, BACK + 1):
            values = real[pl.ds(real_at[6] + turned[d].start, 128), :]
            late[d - 1, pl.ds(h, 1), :] = jnp.sum(
                reached[:, 128 * d - 128 : 128 * d] * values, axis=0, keepdims=True
            )
        own_values = real[pl.ds(real_at[6] + turned[0].start, 128), :].astype(BF16)
        pulled = mm_two(grad, own_values)
        pairs = keep[slab(keep_at[1], h), :] * pulled
        direct_rows[pl.ds(h, 1), :] = jnp.sum(pairs, axis=0, keepdims=True)
        pairs = jnp.where(
            row_i > col_i, pairs * real[pl.ds(real_at[4] + h, 1), :], 0.0
        )
        minus_rows[pl.ds(h, 1), :] = jnp.sum(pairs, axis=0, keepdims=True)
        sums = jnp.sum(pairs + grad * off, axis=1, keepdims=True)
        return jnp.where(col_i == h, jnp.broadcast_to(sums, (128, 128)), row_sums)

    row_sums = lax.fori_loop(0, heads, one_head, jnp.zeros((128, 128), F32), unroll=16)

    def summed(x, triangle):
        high, low = two_parts(x)
        rest = (x - high.astype(F32) - low.astype(F32)).astype(BF16)
        return mm(high, triangle) + mm(low, triangle) + mm(rest, triangle)

    rate = real[base : base + heads, :]
    spanned = summed(row_sums.T[:heads, :] - minus_rows[...], later)
    grads[place] = direct_rows[...] - rate * spanned
    rate_rows = spanned * real[real_at[4] : real_at[4] + heads, :]
    earlier = jnp.zeros((heads, 128), F32)
    for d in range(BACK, 0, -1):
        step = real[real_at[4] + heads * d : real_at[4] + heads * (d + 1), :]
        fade = real[real_at[5] + heads * (d - 1) : real_at[5] + heads * d, :]
        direct = late[d - 1] * fade
        whole = direct * step
        spanned = summed(whole, strict) + earlier
        grads[lax.rem(place - d + count, count)] = direct - rate * spanned
        rate_rows = rate_rows + spanned * step
        earlier = earlier + jnp.sum(whole, axis=1, keepdims=True)
    small_out[...] = jnp.concatenate(
        [to_row(skip_rows[...]), -to_row(rate_rows * rate), jnp.zeros((6, 128), F32)], axis=0
    )


def fold_kernel(grads, gain, small, out):
    total = jnp.sum(grads[...], axis=0)
    rows = total.shape[0]
    tiles = gain.shape[1] // 128
    out[0:rows, :] = total
    for i in range(tiles):
        out[rows + i : rows + i + 1, :] = gain[:, 128 * i : 128 * i + 128]
    out[rows + tiles : rows + tiles + 8, :] = small[...]


def weight_kernel(own, other, slope, slope_other, hidden, far, out, wide):
    heads = slope.shape[0]
    total = own[...] + other[...]
    core = lax.axis_index("core")
    low_core = core == 0
    near_slope, far_slope = slope[...], slope_other[...]
    top, bottom = total[0:heads], total[heads : 2 * heads]
    near_pre = jnp.where(low_core, top, bottom) * near_slope
    far_pre = jnp.where(low_core, bottom, top) * far_slope
    near_low, far_low = near_pre.astype(BF16), far_pre.astype(BF16)
    side = far.shape[1] // 2
    count = side // 128
    tiles = total.shape[0] - 2 * heads - 8
    lines = [total[2 * heads + i : 2 * heads + i + 1] for i in range(tiles)]
    lines.append(to_row(near_pre + far_pre))
    base = 2 * heads + tiles
    lines += [total[base + 1 : base + 2], total[base : base + 1]]
    for j in range(count):
        start = j * (heads + 2)
        cols = pl.ds(pl.multiple_of(core * side + 128 * j, 128), 128)
        wide[start : start + heads, :] = mm(near_low, hidden[:, cols]) + mm(
            far_low, far[:, cols]
        )
        line = jnp.zeros((1, 128), F32)
        if j < len(lines):
            line = jnp.where(low_core, lines[j], line)
        high = line.astype(BF16).astype(F32)
        wide[start + heads : start + heads + 1, :] = high
        wide[start + heads + 1 : start + heads + 2, :] = line - high
    out[...] = wide[...].astype(BF16)


def spread_kernel(count, got, out, wide):
    wide[...] = got[...].astype(F32)
    each = wide.shape[0] // count
    total = wide[0:each, :]
    for j in range(1, count):
        total = total + wide[each * j : each * (j + 1), :]
    small = total[each - 2 : each - 1, :] + total[each - 1 : each, :]
    for j in range(count):
        start = (each - 1) * j
        out[start : start + each - 2, :] = total[: each - 2, :]
        out[start + each - 2 : start + each - 1, :] = small


def finish_kernel(mine, other, weight, bias, decay, skip, gain):
    heads = weight.shape[0]
    count = mine.shape[0] // (heads + 1)
    tiles = gain.shape[1] // 128
    core = lax.axis_index("core")

    def place(source, half):
        for j in range(count):
            i = half * count + j
            start = j * (heads + 1)
            weight[:, 128 * i : 128 * i + 128] = source[start : start + heads, :]
            row = source[start + heads : start + heads + 1, :]
            if i < tiles:
                gain[:, 128 * i : 128 * i + 128] = row
            if i == tiles:
                bias[...] = row[:, :heads]
            if i == tiles + 1:
                decay[...] = row[:, :heads]
            if i == tiles + 2:
                skip[...] = row[:, :heads]

    for half in range(2):

        @pl.when(core == half)
        def _():
            place(mine, half)
            place(other, 1 - half)


def vmem(count):
    return [pl.BlockSpec(memory_space=pltpu.VMEM)] * count


def smem(count):
    return [pl.BlockSpec(memory_space=pltpu.SMEM)] * count


def shape(dims, kind=F32):
    return jax.ShapeDtypeStruct(dims, kind)


LARGE = pltpu.CompilerParams(vmem_limit_bytes=56 * 1024 * 1024)
SMALL = pltpu.CompilerParams(vmem_limit_bytes=16 * 1024 * 1024)


def body(
    hidden_in,
    teacher_queries,
    teacher_keys,
    teacher_values,
    doc_lengths,
    dt_weight,
    dt_bias,
    decay_log,
    skip_gain,
    norm_gain,
):
    rows = teacher_queries.shape[1]
    heads = dt_weight.shape[1]
    kv = teacher_keys.shape[2] // HDIM
    width = heads * HDIM
    features = width * lax.axis_size("grp")
    depth = hidden_in.shape[2]
    chips = lax.axis_size("z")
    blocks = 2 * chips
    row_total = lax.axis_size("dp") * rows * blocks
    hidden = hidden_in[0]
    gain = norm_gain[None, :]
    cargo = 2 * kv * HDIM + 3 * heads

    payload, slope, consts = pl.pallas_call(
        functools.partial(prep_kernel, kv),
        out_shape=[
            shape((cargo, 128), BF16),
            shape((heads, 128)),
            shape((const_rows(heads), 128)),
        ],
        in_specs=smem(4) + vmem(5),
        out_specs=vmem(3),
        compiler_params=LARGE,
        name="prep",
    )(
        doc_lengths, dt_bias, decay_log, skip_gain, gain, hidden, dt_weight.T,
        teacher_keys[0], teacher_values[0],
    )

    swap = [(0, 1), (1, 0)]
    hop = [(i, (i + 1) % chips) for i in range(chips)]
    run = functools.partial(forward, kv, heads, rows)

    def across(part):
        return lax.ppermute(part, "core", swap)

    hop1 = lax.ppermute(payload, "z", hop)
    sib0 = across(payload)
    local = pl.pallas_call(
        functools.partial(pack_kernel, kv),
        out_shape=shape((local_rows(heads, kv)[1], 128), BF16),
        in_specs=vmem(3),
        out_specs=pl.BlockSpec(memory_space=pltpu.VMEM),
        compiler_params=SMALL,
        name="pack",
    )(teacher_queries[0], payload, consts)
    hop1, local = lax.optimization_barrier((hop1, local))
    hop2 = lax.ppermute(hop1, "z", hop)
    sib1 = across(hop1)
    origin, keep = run(0, [local])
    hop2, origin = lax.optimization_barrier((hop2, origin))
    hop3 = lax.ppermute(hop2, "z", hop)
    sib2 = across(hop2)
    (carry1,) = run(1, [local, sib1, sib0, hop1, origin])
    hop3, carry1 = lax.optimization_barrier((hop3, carry1))
    hop4 = lax.ppermute(hop3, "z", hop)
    sib3 = across(hop3)
    (carry2,) = run(2, [local, sib2, sib1, hop2, origin, carry1])
    hop4, carry2 = lax.optimization_barrier((hop4, carry2))
    sib4 = across(hop4)
    (carry3,) = run(3, [local, sib3, sib2, hop3, origin, carry1, carry2])
    real, half, stats = run(
        4, [local, sib4, sib3, hop4, origin, carry1, carry2, carry3, keep]
    )
    hidden_late, slope_late, stats = lax.optimization_barrier((hidden, slope, stats))
    far, slope_other = across(hidden_late), across(slope_late)
    groups = lax.axis_size("grp")
    all_stats = [stats] + [
        lax.ppermute(stats, "grp", [(i, (i + k) % groups) for i in range(groups)])
        for k in range(1, groups)
    ]
    all_stats[1], slope_other = lax.optimization_barrier((all_stats[1], slope_other))

    student, grads, grad_gain, small = pl.pallas_call(
        functools.partial(backward_kernel, kv, heads, len(all_stats), features, row_total),
        out_shape=[
            shape((rows, width), BF16),
            shape((blocks, heads, 128)),
            shape((1, width)),
            shape((8, 128)),
        ],
        in_specs=vmem(5 + len(all_stats)),
        out_specs=vmem(4),
        scratch_shapes=[
            pltpu.VMEM((rows, 128), F32),
            pltpu.VMEM((rows, 128), F32),
            pltpu.VMEM((BACK, heads, 128), F32),
            pltpu.VMEM((heads, 128), F32),
            pltpu.VMEM((heads, 128), F32),
            pltpu.VMEM((heads, 128), F32),
        ],
        compiler_params=SMALL,
        name="backward",
    )(local, keep, carry2, real, half, *all_stats)

    grads = lax.all_to_all(grads.reshape(chips, 2 * heads, 128), "z", 0, 0, tiled=True)
    folded = pl.pallas_call(
        fold_kernel,
        out_shape=shape((3 * heads + 8, 128)),
        in_specs=vmem(3),
        out_specs=pl.BlockSpec(memory_space=pltpu.VMEM),
        compiler_params=SMALL,
        name="fold",
    )(grads, grad_gain, small)

    axes = ("z", "dp")
    count = chips * lax.axis_size("dp")
    half = pl.pallas_call(
        weight_kernel,
        out_shape=shape((count * (heads + 2), 128), BF16),
        in_specs=vmem(6),
        out_specs=pl.BlockSpec(memory_space=pltpu.VMEM),
        scratch_shapes=[pltpu.VMEM((count * (heads + 2), 128), F32)],
        compiler_params=SMALL,
        name="weights",
    )(folded, across(folded), slope, slope_other, hidden, far)
    half = half.reshape(count, (heads + 2) // 2, 2, 128)
    got = lax.all_to_all(half, axes, 0, 0, tiled=True)
    spread = pl.pallas_call(
        functools.partial(spread_kernel, count),
        out_shape=shape((count * (heads + 1), 128)),
        in_specs=vmem(1),
        out_specs=pl.BlockSpec(memory_space=pltpu.VMEM),
        scratch_shapes=[pltpu.VMEM((count * (heads + 2), 128), F32)],
        compiler_params=SMALL,
        name="spread",
    )(got.reshape(count * (heads + 2), 128))
    spread = spread.reshape(count, heads + 1, 1, 128)
    mine = lax.all_to_all(spread, axes, 0, 0, tiled=True)
    mine = mine.reshape(count * (heads + 1), 128)
    other = lax.ppermute(mine, "core", swap)
    grad_weight, bias, decay, skip, gained = pl.pallas_call(
        finish_kernel,
        out_shape=[shape((heads, depth))] + [shape((1, heads))] * 3 + [shape((1, width))],
        in_specs=vmem(2),
        out_specs=vmem(5),
        compiler_params=SMALL,
        name="finish",
    )(mine, other)
    return (student[None], grad_weight.T, bias[0], decay[0], skip[0], gained[0])


def solution(mesh):
    sizes = dict(mesh.shape)
    split = jax.sharding.Mesh(
        mesh.devices.reshape(sizes["ctx"] // 2, 2, sizes["grp"], sizes["dp"]),
        ("z", "core", "grp", "dp"),
    )
    ctx = ("z", "core")
    placed = (
        P("dp", ctx, None),
        P("dp", ctx, "grp"),
        P("dp", ctx, "grp"),
        P("dp", ctx, "grp"),
        P("dp", None),
        P(None, "grp"),
        P("grp"),
        P("grp"),
        P("grp"),
        P("grp"),
    )
    return jax.shard_map(
        body,
        mesh=split,
        in_specs=placed,
        out_specs=(P("dp", ctx, "grp"), P(None, "grp"), P("grp"), P("grp"), P("grp"), P("grp")),
        check_vma=False,
    )
```

```python
import functools
import math

import jax
import jax.numpy as jnp
from jax import lax
from jax.experimental import pallas as pl
from jax.experimental.pallas import tpu as pltpu
from jax.sharding import PartitionSpec as P

HDIM = 128
EPSILON = 1e-05
BACK = 8
NEG = -1e30
LOG2E = math.log2(math.e)
F32 = jnp.float32
BF16 = jnp.bfloat16


def mm(a, b):
    return jnp.dot(a, b, preferred_element_type=F32)


def two_parts(x):
    high = x.astype(BF16)
    return high, (x - high.astype(F32)).astype(BF16)


def mm_two(a, b):
    rows = a.shape[0]
    both = mm(jnp.concatenate(two_parts(a), axis=0), b)
    return both[:rows] + both[rows:]


def mm_right(a, b):
    high, low = two_parts(b)
    return mm(a, high) + mm(a, low)


def iota(shape, dim):
    return lax.broadcasted_iota(jnp.int32, shape, dim)


def to_row(x):
    rows = x.shape[0]
    if rows < 128:
        x = jnp.concatenate([x, jnp.zeros((128 - rows, x.shape[1]), F32)], axis=0)
    return jnp.sum(x.T, axis=0, keepdims=True)


def column_of(values, rows):
    row = iota((rows, 128), 0)
    out = jnp.zeros((rows, 128), F32)
    for h in range(rows):
        out = jnp.where(row == h, values[h], out)
    return out


def place_of(consts, rows):
    core = lax.axis_index("core")
    place = lax.axis_index("z") * lax.axis_size("core") + core
    starts = [consts[i : i + 1, :].astype(jnp.int32) for i in range(3)]
    return (place * rows, *starts, core, place)


def segment_at(pos, info):
    return (
        (pos >= info[1]).astype(jnp.int32)
        + (pos >= info[2]).astype(jnp.int32)
        + (pos >= info[3]).astype(jnp.int32)
    )


def prep_kernel(
    kv,
    lengths,
    bias,
    decay,
    skip,
    gain,
    hidden,
    weight,
    keys,
    values,
    payload,
    slope,
    consts,
):
    heads = weight.shape[0]
    pre = (
        lax.dot_general(
            hidden[...], weight[...], (((1,), (1,)), ((), ())), preferred_element_type=F32
        ).T
        + column_of(bias, heads)
    )
    step = jnp.maximum(pre, 0.0) + jnp.log1p(jnp.exp(-jnp.abs(pre)))
    slope[...] = 1.0 / (1.0 + jnp.exp(-pre))
    for g in range(kv):
        cols = slice(g * HDIM, (g + 1) * HDIM)
        payload[g * HDIM : (g + 1) * HDIM, :] = keys[:, cols].astype(F32).T.astype(BF16)
        payload[(kv + g) * HDIM : (kv + g + 1) * HDIM, :] = values[:, cols]
    consts[0:heads, :] = jnp.exp(column_of(decay, heads))
    consts[heads : 2 * heads, :] = column_of(skip, heads)
    for h in range(heads):
        consts[2 * heads + h : 2 * heads + h + 1, :] = gain[:, h * HDIM : (h + 1) * HDIM]
    one = lengths[0, 0]
    two = one + lengths[0, 1]
    starts = (one, two, two + lengths[0, 2], 0, 0, 0, 0, 0)
    row = iota((8, 128), 0)
    marks = jnp.zeros((8, 128), jnp.int32)
    for i in range(3):
        marks = jnp.where(row == i, starts[i], marks)
    consts[3 * heads : 3 * heads + 8, :] = marks.astype(F32)
    consts[3 * heads + 8 :, :] = jnp.zeros((consts.shape[0] - 3 * heads - 8, 128), F32)
    first = 2 * kv * HDIM
    for part in range(3):
        piece = step.astype(BF16)
        payload[first + part * heads : first + (part + 1) * heads, :] = piece
        step = step - piece.astype(F32)


def pack_kernel(kv, queries, payload, consts, local):
    heads = queries.shape[1] // 128
    at = local_rows(heads, kv)[0]
    for h in range(heads):
        local[at[0] + 128 * h : at[0] + 128 * h + 128, :] = queries[:, 128 * h : 128 * h + 128]
    local[at[1] : at[1] + payload.shape[0], :] = payload[...]
    rest = consts[...]
    for part in range(3):
        piece = rest.astype(BF16)
        local[at[2 + part] : at[2 + part] + rest.shape[0], :] = piece
        rest = rest - piece.astype(F32)


def masks(info):
    first = info[0]
    before = jnp.where(
        first > 0, segment_at(jnp.maximum(first - 1, 0) + iota((1, 128), 1) * 0, info), -1
    )
    row_pos = first + iota((128, 128), 0)
    col_pos = first + iota((128, 128), 1)
    row_seg = segment_at(row_pos, info)
    allowed = (row_seg == segment_at(col_pos, info)) & (col_pos <= row_pos)
    carried = row_seg == before
    return first, before, allowed, carried


def match_row(info, first, before, d, rows):
    pos = first - 128 * d + iota((rows, 128), 1)
    return (segment_at(pos, info) == before) & (pos >= 0)


PARTS = ((0,), (1, 2), (3, 4), (5, 6), (7, 8))


def layout(*sizes):
    starts, total = [], 0
    for size in sizes:
        starts.append(total)
        total += -(-size // 128) * 128
    return starts, total


def carry_rows(heads, kv, part):
    count = len(PARTS[part])
    wide = heads * 128
    if part == 0:
        return layout(wide, wide, wide, 0, heads * 3, const_rows(heads), 0, 0)
    turned = kv * count * 128
    return layout(
        wide, wide, wide, wide, heads * (2 + 2 * count), 0, turned, turned, wide if part == 2 else 0
    )


def const_rows(heads):
    return -(-(3 * heads + 8) // 16) * 16


def local_rows(heads, kv):
    size = const_rows(heads)
    cargo = 2 * kv * HDIM + 3 * heads
    starts, total = [], 0
    for rows in (heads * 128, cargo, size, size, size):
        starts.append(total)
        total += rows
    return starts, total


def keep_rows(heads, kv):
    return layout(heads * 128, heads * 128, kv * 128, kv * 128, kv * 128)


def real_rows(heads, kv):
    count = BACK + 1
    wide = heads * 128
    return layout(
        wide, wide, 0, const_rows(heads), count * heads, BACK * heads, kv * count * 128
    )


def half_rows(heads, kv):
    return layout(heads * 128, kv * (BACK + 1) * 128)


def slab(start, h):
    return pl.ds(pl.multiple_of(start + h * 128, 128), 128)


def forward_kernel(kv, heads, part, *refs):
    refs = list(refs)

    def take(count):
        out = refs[:count]
        del refs[:count]
        return out

    first, last = part == 0, part == len(PARTS) - 1
    blocks = PARTS[part]
    local = take(1)[0]
    local_at = local_rows(heads, kv)[0]
    if first:
        sources = [[local]]
        carry, keep = take(2)
        cum_ref, value_ref, consts = refs[-3:]
        total = jnp.zeros(consts.shape, F32)
        for i in range(3):
            total += local[local_at[2 + i] : local_at[2 + i] + consts.shape[0], :].astype(F32)
        consts[...] = total
    else:
        sources = [take(1 if d % 2 == 0 else 2) for d in blocks]
        origin = take(1)[0]
        carries = [origin] + take(part - 1)
        before_carry = carries[-1]
        before_at = carry_rows(heads, kv, part - 1)[0]
    if last:
        keep, real, half, stats = take(4)
    elif not first:
        carry = take(1)[0]
    kt, vv, bias, step_ref = take(4)
    if not first:
        key32, fade_ref = take(2)
    origin_at = carry_rows(heads, kv, 0)[0]
    keep_at = keep_rows(heads, kv)[0]
    real_at = real_rows(heads, kv)[0]
    half_at = half_rows(heads, kv)[0]
    carry_at = carry_rows(heads, kv, part)[0]
    if first:
        constant, base = consts, 0
        carry[carry_at[5] : carry_at[5] + consts.shape[0], :] = consts[...]
    else:
        constant, base = origin, origin_at[5]
    cum_at = origin_at[4] + heads
    enter_at = carry_rows(heads, kv, 2)[0][8]
    group = heads // kv
    size = 3 * heads + 8
    info = place_of(constant[base + size - 8 : base + size, :], 128)
    even_core = info[4] == 0
    start, before, allowed, carried = masks(info)

    reach = (iota((128, 128), 0) <= iota((128, 128), 1)).astype(BF16)
    if first:
        after = jnp.zeros((heads, 128), F32)
    else:
        after = before_carry[before_at[4] : before_at[4] + heads, :]
    rate = constant[base : base + heads, :]
    for i, d in enumerate(blocks):
        at = slice(128 * i, 128 * i + 128)
        near = sources[i]

        def piece(low, high):
            if first:
                return near[0][local_at[1] + low : local_at[1] + high, :]
            if d % 2 == 0:
                return near[0][low:high, :]
            return jnp.where(even_core, near[0][low:high, :], near[1][low:high, :])

        for g in range(kv):
            block = piece(g * HDIM, (g + 1) * HDIM)
            value = piece((kv + g) * HDIM, (kv + g + 1) * HDIM)
            kt[g, :, at] = block
            vv[g, at, :] = value
            block, value = block.astype(F32), value.astype(F32)
            if last:
                row = (g * (BACK + 1) + d) * 128
                half[half_at[1] + row : half_at[1] + row + 128, :] = kt[g, :, at]
                real[real_at[6] + row : real_at[6] + row + 128, :] = value.T
            else:
                row = (g * len(blocks) + i) * 128
                out, where = (keep, keep_at[3:5]) if first else (carry, carry_at[6:8])
                out[where[0] + row : where[0] + row + 128, :] = block
                out[where[1] + row : where[1] + row + 128, :] = value.T
            if first:
                keep[keep_at[2] + 128 * g : keep_at[2] + 128 * g + 128, :] = value
                value_ref[g] = value
            else:
                key32[g, :, at] = block
        first_step = 2 * kv * HDIM
        parts = [piece(first_step + k * heads, first_step + (k + 1) * heads) for k in range(3)]
        step = parts[0].astype(F32) + parts[1].astype(F32) + parts[2].astype(F32)
        sums = mm(parts[0], reach) + mm(parts[1], reach) + mm(parts[2], reach)
        step_ref[i] = step
        if first:
            carry[cum_at : cum_at + heads, :] = sums
            cum_ref[...] = sums
            bias[:, at] = jnp.where(allowed, 0.0, NEG)
        else:
            total = jnp.broadcast_to(sums[:, 127:128], (heads, 128))
            left = jnp.maximum(total - sums, 0.0) + after
            found = match_row(info, start, before, d, heads)
            fade_ref[i] = jnp.where(found, jnp.exp(-rate * left), 0.0)
            after = after + total
            both = carried & match_row(info, start, before, d, 128)
            bias[:, at] = jnp.where(both, 0.0, NEG)
    if last:
        real[real_at[3] : real_at[3] + size, :] = origin[base : base + size, :]
        for p, source in enumerate(carries):
            where = carry_rows(heads, kv, p)[0]
            count = len(PARTS[p])
            low = where[4] + heads * 2
            rows = heads * count
            to = real_at[4] + heads * PARTS[p][0]
            real[to : to + rows, :] = source[low : low + rows, :]
            if p > 0:
                low = low + rows
                to = real_at[5] + heads * (PARTS[p][0] - 1)
                real[to : to + rows, :] = source[low : low + rows, :]
            turned, where = (keep, keep_at[3:5]) if p == 0 else (source, where[6:8])
            for g in range(kv):
                rows = 128 * count
                low = g * rows
                to = (g * (BACK + 1) + PARTS[p][0]) * 128
                half[half_at[1] + to : half_at[1] + to + rows, :] = turned[
                    where[0] + low : where[0] + low + rows, :
                ].astype(BF16)
                real[real_at[6] + to : real_at[6] + to + rows, :] = turned[
                    where[1] + low : where[1] + low + rows, :
                ]
        small, step_at = real, real_at[4] + heads * blocks[0]
        fade_at = real_at[5] + heads * (blocks[0] - 1)
    else:
        small, step_at = carry, carry_at[4] + heads * 2
        fade_at = step_at + heads * len(blocks)
        carry[carry_at[4] : carry_at[4] + heads, :] = after
    for i in range(len(blocks)):
        small[step_at + heads * i : step_at + heads * (i + 1), :] = step_ref[i]
        if not first:
            small[fade_at + heads * i : fade_at + heads * (i + 1), :] = fade_ref[i]

    def rate_of(h):
        return constant[pl.ds(base + h, 1), :]

    def one_head(h, sums):
        g = h // group
        query = local[slab(local_at[0], h), :]
        scores = mm(query, kt[g])
        scaled = scores * (LOG2E / math.sqrt(HDIM)) + bias[...]
        top = jnp.broadcast_to(jnp.max(scaled, axis=1, keepdims=True), (128, 128))
        if not first:
            old = before_carry[slab(before_at[0], h), :]
            top = jnp.maximum(old, top)
        weights = [
            jnp.exp2(scaled[:, 128 * i : 128 * i + 128] - top) for i in range(len(blocks))
        ]
        total = weights[0]
        for other in weights[1:]:
            total = total + other
        total = jnp.broadcast_to(jnp.sum(total, axis=1, keepdims=True), (128, 128))
        weights = jnp.concatenate([w.astype(BF16) for w in weights], axis=1)
        if not first:
            weight_row = jnp.concatenate(
                [
                    fade_ref[i, pl.ds(h, 1), :] * step_ref[i, pl.ds(h, 1), :]
                    for i in range(len(blocks))
                ],
                axis=1,
            )
            mixed = mm(weights, vv[g])
            state = mm_two(key32[g] * weight_row, vv[g])
            scale = jnp.exp2(old - top)
            total = total + before_carry[slab(before_at[1], h), :] * scale
            mixed = mixed + before_carry[slab(before_at[2], h), :] * scale
            if part > 1:
                state = state + before_carry[slab(before_at[3], h), :]
        else:
            decay_row = rate_of(h)
            cum_row = jnp.broadcast_to(cum_ref[pl.ds(h, 1), :], (128, 128))
            cum_col = cum_row.T
            decay = jnp.where(
                allowed, jnp.exp(-decay_row * jnp.maximum(cum_col - cum_row, 0.0)), 0.0
            )
            decayed = scores[:, :128] * decay
            keep[slab(keep_at[1], h), :] = decayed
            skipped = constant[pl.ds(base + heads + h, 1), :] * value_ref[g]
            high, low = two_parts(decayed * step_ref[0, pl.ds(h, 1), :])
            joined = mm(jnp.concatenate([weights, high, low], axis=0), vv[g])
            mixed = joined[:128]
            keep[slab(keep_at[0], h), :] = joined[128:256] + joined[256:] + skipped
        if not last:
            carry[slab(carry_at[0], h), :] = top
            carry[slab(carry_at[1], h), :] = total
            carry[slab(carry_at[2], h), :] = mixed
            if not first:
                carry[slab(carry_at[3], h), :] = state
        if part == 2:
            cum_col = jnp.broadcast_to(origin[pl.ds(cum_at + h, 1), :], (128, 128)).T
            carry[slab(enter_at, h), :] = jnp.where(
                carried, jnp.exp(-rate_of(h) * cum_col), 0.0
            )
        if last:
            teach = (mixed / total).astype(BF16)
            half[slab(half_at[0], h), :] = teach
            off = mm_right(query, state) * carries[2][slab(enter_at, h), :]
            raw = keep[slab(keep_at[0], h), :] + off
            real[slab(real_at[0], h), :] = raw
            real[slab(real_at[1], h), :] = off
            gained = raw * constant[pl.ds(base + 2 * heads + h, 1), :]
            sums = (
                sums[0] + raw * raw,
                sums[1] + gained * gained,
                sums[2] + gained * teach.astype(F32),
            )
        return sums

    nothing = tuple(jnp.zeros((128, 128), F32) for _ in range(3 if last else 0))
    sums = lax.fori_loop(0, heads, one_head, nothing, unroll=16)
    if last:
        stats[...] = jnp.concatenate(
            [to_row(sums[0]), to_row(sums[1]), to_row(sums[2]), jnp.zeros((5, 128), F32)], axis=0
        )


def forward(kv, heads, rows, part, operands):
    blocks = PARTS[part]
    first, last = part == 0, part == len(PARTS) - 1
    wide = 128 * len(blocks)
    if last:
        outs = [
            shape((real_rows(heads, kv)[1], 128)),
            shape((half_rows(heads, kv)[1], 128), BF16),
            shape((8, 128)),
        ]
    else:
        outs = [shape((carry_rows(heads, kv, part)[1], 128))]
    if first:
        outs.append(shape((keep_rows(heads, kv)[1], 128)))
    scratch = [
        pltpu.VMEM((kv, HDIM, wide), BF16),
        pltpu.VMEM((kv, wide, HDIM), BF16),
        pltpu.VMEM((rows, wide), F32),
        pltpu.VMEM((len(blocks), heads, 128), F32),
    ]
    if first:
        scratch += [
            pltpu.VMEM((heads, 128), F32),
            pltpu.VMEM((kv, rows, HDIM), F32),
            pltpu.VMEM((const_rows(heads), 128), F32),
        ]
    else:
        scratch += [
            pltpu.VMEM((kv, HDIM, wide), F32),
            pltpu.VMEM((len(blocks), heads, 128), F32),
        ]
    return pl.pallas_call(
        functools.partial(forward_kernel, kv, heads, part),
        out_shape=outs,
        in_specs=vmem(len(operands)),
        out_specs=vmem(len(outs)),
        scratch_shapes=scratch,
        compiler_params=SMALL,
        cost_estimate=pl.CostEstimate(
            flops=len(blocks) * heads * rows * 128 * 128 * 12,
            bytes_accessed=len(blocks) * 3 * 1024 * 1024,
            transcendentals=2 * heads * rows * wide,
        ),
        name="forward_" + "abcde"[part],
    )(*operands)


def backward_kernel(kv, heads, groups, features, row_total, *refs):
    local, keep, enter, real, half, *refs = refs
    stats = refs[0][...]
    for other in refs[1:groups]:
        stats = stats + other[...]
    student_out, grads, gain_out, small_out, *refs = refs[groups:]
    inv_col, coef_col, late, skip_rows, direct_rows, minus_rows = refs
    keep_at = keep_rows(heads, kv)[0]
    real_at = real_rows(heads, kv)[0]
    half_at = half_rows(heads, kv)[0]
    group = heads // kv
    enter_at = carry_rows(heads, kv, 2)[0][8]
    size = 3 * heads + 8
    base = real_at[3]
    info = place_of(real[base + size - 8 : base + size, :], 128)
    place, count = info[5], grads.shape[0]
    grads[...] = jnp.zeros_like(grads)
    share = 2.0 / row_total
    squares, gained_squares, crossed = stats[0:1, :], stats[1:2, :], stats[2:3, :]
    inverse = lax.rsqrt(squares / features + EPSILON)
    inner = share * (inverse * gained_squares - crossed)
    coef = inverse * inverse * inverse * inner / features
    inv_col[...] = jnp.broadcast_to(inverse, (128, 128)).T
    coef_col[...] = jnp.broadcast_to(coef, (128, 128)).T
    row_i, col_i = iota((128, 128), 0), iota((128, 128), 1)
    later = (row_i >= col_i).astype(BF16)
    strict = (row_i < col_i).astype(BF16)

    def one_head(h, row_sums):
        g = h // group
        cols = slab(0, h)
        query = local[slab(0, h), :]
        raw, off = real[slab(real_at[0], h), :], real[slab(real_at[1], h), :]
        scale = real[pl.ds(base + 2 * heads + h, 1), :]
        inv = inv_col[...]
        normed = raw * inv * scale
        student_out[:, cols] = normed.astype(BF16)
        grad_normed = (normed - half[slab(half_at[0], h), :].astype(F32)) * share
        gain_out[:, cols] = jnp.sum(grad_normed * raw * inv, axis=0, keepdims=True)
        grad = inv * grad_normed * scale - raw * coef_col[...]
        value = keep[slab(keep_at[2], g), :]
        skip_rows[pl.ds(h, 1), :] = jnp.sum(grad * value, axis=0, keepdims=True)
        entering = enter[slab(enter_at, h), :]
        grad_state = mm_two((grad * entering).T, query)
        turned = [slab(g * ((BACK + 1) * 128), d) for d in range(BACK + 1)]
        keys = jnp.concatenate(
            [half[pl.ds(half_at[1] + turned[d].start, 128), :] for d in range(1, BACK + 1)],
            axis=1,
        )
        reached = mm_two(grad_state, keys)
        for d in range(1, BACK + 1):
            values = real[pl.ds(real_at[6] + turned[d].start, 128), :]
            late[d - 1, pl.ds(h, 1), :] = jnp.sum(
                reached[:, 128 * d - 128 : 128 * d] * values, axis=0, keepdims=True
            )
        own_values = real[pl.ds(real_at[6] + turned[0].start, 128), :].astype(BF16)
        pulled = mm_two(grad, own_values)
        pairs = keep[slab(keep_at[1], h), :] * pulled
        direct_rows[pl.ds(h, 1), :] = jnp.sum(pairs, axis=0, keepdims=True)
        pairs = jnp.where(
            row_i > col_i, pairs * real[pl.ds(real_at[4] + h, 1), :], 0.0
        )
        minus_rows[pl.ds(h, 1), :] = jnp.sum(pairs, axis=0, keepdims=True)
        sums = jnp.sum(pairs + grad * off, axis=1, keepdims=True)
        return jnp.where(col_i == h, jnp.broadcast_to(sums, (128, 128)), row_sums)

    row_sums = lax.fori_loop(0, heads, one_head, jnp.zeros((128, 128), F32), unroll=16)

    def summed(x, triangle):
        high, low = two_parts(x)
        rest = (x - high.astype(F32) - low.astype(F32)).astype(BF16)
        return mm(high, triangle) + mm(low, triangle) + mm(rest, triangle)

    rate = real[base : base + heads, :]
    spanned = summed(row_sums.T[:heads, :] - minus_rows[...], later)
    grads[place] = direct_rows[...] - rate * spanned
    rate_rows = spanned * real[real_at[4] : real_at[4] + heads, :]
    earlier = jnp.zeros((heads, 128), F32)
    for d in range(BACK, 0, -1):
        step = real[real_at[4] + heads * d : real_at[4] + heads * (d + 1), :]
        fade = real[real_at[5] + heads * (d - 1) : real_at[5] + heads * d, :]
        direct = late[d - 1] * fade
        whole = direct * step
        spanned = summed(whole, strict) + earlier
        grads[lax.rem(place - d + count, count)] = direct - rate * spanned
        rate_rows = rate_rows + spanned * step
        earlier = earlier + jnp.sum(whole, axis=1, keepdims=True)
    small_out[...] = jnp.concatenate(
        [to_row(skip_rows[...]), -to_row(rate_rows * rate), jnp.zeros((6, 128), F32)], axis=0
    )


def fold_kernel(grads, gain, small, out):
    total = jnp.sum(grads[...], axis=0)
    rows = total.shape[0]
    tiles = gain.shape[1] // 128
    out[0:rows, :] = total
    for i in range(tiles):
        out[rows + i : rows + i + 1, :] = gain[:, 128 * i : 128 * i + 128]
    out[rows + tiles : rows + tiles + 8, :] = small[...]


def weight_kernel(own, other, slope, slope_other, hidden, far, out, wide):
    heads = slope.shape[0]
    total = own[...] + other[...]
    core = lax.axis_index("core")
    low_core = core == 0
    near_slope, far_slope = slope[...], slope_other[...]
    top, bottom = total[0:heads], total[heads : 2 * heads]
    near_pre = jnp.where(low_core, top, bottom) * near_slope
    far_pre = jnp.where(low_core, bottom, top) * far_slope
    near_low, far_low = near_pre.astype(BF16), far_pre.astype(BF16)
    side = far.shape[1] // 2
    count = side // 128
    tiles = total.shape[0] - 2 * heads - 8
    lines = [total[2 * heads + i : 2 * heads + i + 1] for i in range(tiles)]
    lines.append(to_row(near_pre + far_pre))
    base = 2 * heads + tiles
    lines += [total[base + 1 : base + 2], total[base : base + 1]]
    for j in range(count):
        start = j * (heads + 2)
        cols = pl.ds(pl.multiple_of(core * side + 128 * j, 128), 128)
        wide[start : start + heads, :] = mm(near_low, hidden[:, cols]) + mm(
            far_low, far[:, cols]
        )
        line = jnp.zeros((1, 128), F32)
        if j < len(lines):
            line = jnp.where(low_core, lines[j], line)
        high = line.astype(BF16).astype(F32)
        wide[start + heads : start + heads + 1, :] = high
        wide[start + heads + 1 : start + heads + 2, :] = line - high
    out[...] = wide[...].astype(BF16)


def spread_kernel(count, got, out, wide):
    wide[...] = got[...].astype(F32)
    each = wide.shape[0] // count
    total = wide[0:each, :]
    for j in range(1, count):
        total = total + wide[each * j : each * (j + 1), :]
    small = total[each - 2 : each - 1, :] + total[each - 1 : each, :]
    for j in range(count):
        start = (each - 1) * j
        out[start : start + each - 2, :] = total[: each - 2, :]
        out[start + each - 2 : start + each - 1, :] = small


def finish_kernel(mine, other, weight, bias, decay, skip, gain):
    heads = weight.shape[0]
    count = mine.shape[0] // (heads + 1)
    tiles = gain.shape[1] // 128
    core = lax.axis_index("core")

    def place(source, half):
        for j in range(count):
            i = half * count + j
            start = j * (heads + 1)
            weight[:, 128 * i : 128 * i + 128] = source[start : start + heads, :]
            row = source[start + heads : start + heads + 1, :]
            if i < tiles:
                gain[:, 128 * i : 128 * i + 128] = row
            if i == tiles:
                bias[...] = row[:, :heads]
            if i == tiles + 1:
                decay[...] = row[:, :heads]
            if i == tiles + 2:
                skip[...] = row[:, :heads]

    for half in range(2):

        @pl.when(core == half)
        def _():
            place(mine, half)
            place(other, 1 - half)


def vmem(count):
    return [pl.BlockSpec(memory_space=pltpu.VMEM)] * count


def smem(count):
    return [pl.BlockSpec(memory_space=pltpu.SMEM)] * count


def shape(dims, kind=F32):
    return jax.ShapeDtypeStruct(dims, kind)


LARGE = pltpu.CompilerParams(vmem_limit_bytes=56 * 1024 * 1024)
SMALL = pltpu.CompilerParams(vmem_limit_bytes=16 * 1024 * 1024)


def body(
    hidden_in,
    teacher_queries,
    teacher_keys,
    teacher_values,
    doc_lengths,
    dt_weight,
    dt_bias,
    decay_log,
    skip_gain,
    norm_gain,
):
    rows = teacher_queries.shape[1]
    heads = dt_weight.shape[1]
    kv = teacher_keys.shape[2] // HDIM
    width = heads * HDIM
    features = width * lax.axis_size("grp")
    depth = hidden_in.shape[2]
    chips = lax.axis_size("z")
    blocks = 2 * chips
    row_total = lax.axis_size("dp") * rows * blocks
    hidden = hidden_in[0]
    gain = norm_gain[None, :]
    cargo = 2 * kv * HDIM + 3 * heads

    payload, slope, consts = pl.pallas_call(
        functools.partial(prep_kernel, kv),
        out_shape=[
            shape((cargo, 128), BF16),
            shape((heads, 128)),
            shape((const_rows(heads), 128)),
        ],
        in_specs=smem(4) + vmem(5),
        out_specs=vmem(3),
        compiler_params=LARGE,
        name="prep",
    )(
        doc_lengths, dt_bias, decay_log, skip_gain, gain, hidden, dt_weight.T,
        teacher_keys[0], teacher_values[0],
    )

    swap = [(0, 1), (1, 0)]
    hop = [(i, (i + 1) % chips) for i in range(chips)]
    run = functools.partial(forward, kv, heads, rows)

    def across(part):
        return lax.ppermute(part, "core", swap)

    hop1 = lax.ppermute(payload, "z", hop)
    sib0 = across(payload)
    local = pl.pallas_call(
        functools.partial(pack_kernel, kv),
        out_shape=shape((local_rows(heads, kv)[1], 128), BF16),
        in_specs=vmem(3),
        out_specs=pl.BlockSpec(memory_space=pltpu.VMEM),
        compiler_params=SMALL,
        name="pack",
    )(teacher_queries[0], payload, consts)
    hop1, local = lax.optimization_barrier((hop1, local))
    hop2 = lax.ppermute(hop1, "z", hop)
    sib1 = across(hop1)
    origin, keep = run(0, [local])
    hop2, origin = lax.optimization_barrier((hop2, origin))
    hop3 = lax.ppermute(hop2, "z", hop)
    sib2 = across(hop2)
    (carry1,) = run(1, [local, sib1, sib0, hop1, origin])
    hop3, carry1 = lax.optimization_barrier((hop3, carry1))
    hop4 = lax.ppermute(hop3, "z", hop)
    sib3 = across(hop3)
    (carry2,) = run(2, [local, sib2, sib1, hop2, origin, carry1])
    hop4, carry2 = lax.optimization_barrier((hop4, carry2))
    sib4 = across(hop4)
    (carry3,) = run(3, [local, sib3, sib2, hop3, origin, carry1, carry2])
    real, half, stats = run(
        4, [local, sib4, sib3, hop4, origin, carry1, carry2, carry3, keep]
    )
    hidden_late, slope_late, stats = lax.optimization_barrier((hidden, slope, stats))
    far, slope_other = across(hidden_late), across(slope_late)
    groups = lax.axis_size("grp")
    all_stats = [stats] + [
        lax.ppermute(stats, "grp", [(i, (i + k) % groups) for i in range(groups)])
        for k in range(1, groups)
    ]
    all_stats[1], slope_other = lax.optimization_barrier((all_stats[1], slope_other))

    student, grads, grad_gain, small = pl.pallas_call(
        functools.partial(backward_kernel, kv, heads, len(all_stats), features, row_total),
        out_shape=[
            shape((rows, width), BF16),
            shape((blocks, heads, 128)),
            shape((1, width)),
            shape((8, 128)),
        ],
        in_specs=vmem(5 + len(all_stats)),
        out_specs=vmem(4),
        scratch_shapes=[
            pltpu.VMEM((rows, 128), F32),
            pltpu.VMEM((rows, 128), F32),
            pltpu.VMEM((BACK, heads, 128), F32),
            pltpu.VMEM((heads, 128), F32),
            pltpu.VMEM((heads, 128), F32),
            pltpu.VMEM((heads, 128), F32),
        ],
        compiler_params=SMALL,
        name="backward",
    )(local, keep, carry2, real, half, *all_stats)

    grads = lax.all_to_all(grads.reshape(chips, 2 * heads, 128), "z", 0, 0, tiled=True)
    folded = pl.pallas_call(
        fold_kernel,
        out_shape=shape((3 * heads + 8, 128)),
        in_specs=vmem(3),
        out_specs=pl.BlockSpec(memory_space=pltpu.VMEM),
        compiler_params=SMALL,
        name="fold",
    )(grads, grad_gain, small)

    axes = ("z", "dp")
    count = chips * lax.axis_size("dp")
    half = pl.pallas_call(
        weight_kernel,
        out_shape=shape((count * (heads + 2), 128), BF16),
        in_specs=vmem(6),
        out_specs=pl.BlockSpec(memory_space=pltpu.VMEM),
        scratch_shapes=[pltpu.VMEM((count * (heads + 2), 128), F32)],
        compiler_params=SMALL,
        name="weights",
    )(folded, across(folded), slope, slope_other, hidden, far)
    half = half.reshape(count, (heads + 2) // 2, 2, 128)
    got = lax.all_to_all(half, axes, 0, 0, tiled=True)
    spread = pl.pallas_call(
        functools.partial(spread_kernel, count),
        out_shape=shape((count * (heads + 1), 128)),
        in_specs=vmem(1),
        out_specs=pl.BlockSpec(memory_space=pltpu.VMEM),
        scratch_shapes=[pltpu.VMEM((count * (heads + 2), 128), F32)],
        compiler_params=SMALL,
        name="spread",
    )(got.reshape(count * (heads + 2), 128))
    spread = spread.reshape(count, heads + 1, 1, 128)
    mine = lax.all_to_all(spread, axes, 0, 0, tiled=True)
    mine = mine.reshape(count * (heads + 1), 128)
    other = lax.ppermute(mine, "core", swap)
    grad_weight, bias, decay, skip, gained = pl.pallas_call(
        finish_kernel,
        out_shape=[shape((heads, depth))] + [shape((1, heads))] * 3 + [shape((1, width))],
        in_specs=vmem(2),
        out_specs=vmem(5),
        compiler_params=SMALL,
        name="finish",
    )(mine, other)
    return (student[None], grad_weight.T, bias[0], decay[0], skip[0], gained[0])


def solution(mesh):
    sizes = dict(mesh.shape)
    split = jax.sharding.Mesh(
        mesh.devices.reshape(sizes["ctx"] // 2, 2, sizes["grp"], sizes["dp"]),
        ("z", "core", "grp", "dp"),
    )
    ctx = ("z", "core")
    placed = (
        P("dp", ctx, None),
        P("dp", ctx, "grp"),
        P("dp", ctx, "grp"),
        P("dp", ctx, "grp"),
        P("dp", None),
        P(None, "grp"),
        P("grp"),
        P("grp"),
        P("grp"),
        P("grp"),
    )
    return jax.shard_map(
        body,
        mesh=split,
        in_specs=placed,
        out_specs=(P("dp", ctx, "grp"), P(None, "grp"), P("grp"), P("grp"), P("grp"), P("grp")),
        check_vma=False,
    )
```
